32 devices in a mesh: img: 8 (over z, y), rows: 4 (over x, core).
Axes of the slice: x: 2, y: 2, z: 4, core: 2. Of those that a mesh axis runs over, the one named last changes fastest.
Arguments:
- inputs: bfloat16 [4, 256, 16, 16, 1024], P(None, 'img', 'rows'), may hold values from -18 to 18
- masks: int32 [4, 256, 16, 16], P(None, 'img', 'rows'), may hold values from 0 to 1, as said below
- partner: int32 [4, 256], P(None, ('img', 'rows')), may hold values from 0 to 255, as said below
- live: int32 [4, 256], P(None, ('img', 'rows')), may hold values from 0 to 1, as said below
- params: float32 [20738048], P(('img', 'rows')), may hold values from -1.5 to 1.5, as said below
- first: float32 [20738048], P(('img', 'rows')), may hold values from -1 to 1
- second: float32 [20738048], P(('img', 'rows')), may hold values from 0 to 1
- running: float32 [2, 11776], replicated, may hold values from -1 to 2
Outputs:
- loss_sums: float32 [4], replicated
- pair_counts: int32 [4], replicated
- new_params: float32 [20738048], P(('img', 'rows'))
- new_first: float32 [20738048], P(('img', 'rows'))
- new_second: float32 [20738048], P(('img', 'rows'))
- new_copy: bfloat16 [20738048], P(('img', 'rows'))
- new_running: float32 [2, 11776], replicated
The draws below stay inside these ranges and needn't reach their ends.
Inputs may be any that keep to these rules, and one draw needn't show every extreme that they name: `masks`: each image is valid on all 16 x 16 pixels, on its first 12 rows, or on its first 12 columns. partner[m, i] lies in the same aligned block of 8 images as i, differs from i, and partner[m, partner[m, i]] = i. live is equal on both images of a pair. `params`: the entries past the first 20734976 are zero.
All inputs are finite; a program needn't handle non-finite values.
Results may differ from the reference program's by a relative error of at most 0.025.
Values may be sent and summed in bfloat16 or wider, within the bound.
No kernel may reach another device: no remote copies, remote signals or barrier semaphores. Data moves between devices by JAX's collectives and lax.ppermute only.
A program may use at most 960 MiB of HBM per device.

```python
import math
import jax
import jax.numpy as jnp
from jax import lax

D_IN = 1024
MID = 512
OUT = 2048
PRED = 512
HEIGHT = 16
WIDTH = 16
MB = 4
STEP = 5
IMG_DEV = 32
IMAGES = 256
BLOCK = 8
NORM = 11776
PARAMS = 20734976
FLAT = 20738048


def draw_inputs(key, part):
    key = jax.random.fold_in(key, 1)
    base = jax.random.normal(key, (MB, IMAGES, HEIGHT, WIDTH, D_IN), jnp.float32)
    groups = IMAGES // IMG_DEV
    splits = IMG_DEV // BLOCK
    image_pos = (jnp.arange(IMAGES) // IMG_DEV).astype(jnp.float32) / max(groups - 1, 1)
    row_pos = (jnp.arange(HEIGHT) // (HEIGHT // splits)).astype(jnp.float32) / max(splits - 1, 1)
    rising = image_pos[:, None] + row_pos[None, :]
    base = jnp.clip(base, -6.0, 6.0)
    scale = 1.0 + rising
    return (base * scale[None, :, :, None, None]).astype(jnp.bfloat16)


def draw_masks(key, part):
    key = jax.random.fold_in(key, 2)
    kinds = jax.random.randint(key, (MB, IMAGES), 0, 3)[..., None, None]
    row_ids = jnp.arange(HEIGHT)[:, None] + jnp.zeros((1, WIDTH), jnp.int32)
    col_ids = jnp.arange(WIDTH)[None, :] + jnp.zeros((HEIGHT, 1), jnp.int32)
    narrow = col_ids < 3 * WIDTH // 4
    short = row_ids < 3 * HEIGHT // 4
    valid = jnp.where(kinds == 0, narrow, jnp.where(kinds == 1, short, True))
    return valid.astype(jnp.int32)


def pairing(key):
    blocks = IMAGES // BLOCK
    keys = jax.random.split(jax.random.fold_in(key, 7), MB * blocks)
    order = jax.vmap(lambda single: jax.random.permutation(single, BLOCK))(keys).reshape(MB, blocks, BLOCK)
    swapped = order.reshape(MB, blocks, BLOCK // 2, 2)[..., ::-1].reshape(MB, blocks, BLOCK)
    inverse = jnp.argsort(order, axis=-1)
    partner_local = jnp.take_along_axis(swapped, inverse, axis=-1).astype(jnp.int32)
    return (partner_local, blocks)


def draw_partner(key, part):
    partner_local, blocks = pairing(key)
    offsets = (jnp.arange(blocks, dtype=jnp.int32) * BLOCK)[None, :, None]
    return (partner_local + offsets).reshape(MB, IMAGES)


def draw_live(key, part):
    partner_local, blocks = pairing(key)
    span = max(blocks - 1, 1)
    tickets = jax.random.randint(jax.random.fold_in(key, 11), (MB, blocks, BLOCK), 0, 3 * span)
    paired = jnp.maximum(tickets, jnp.take_along_axis(tickets, partner_local, axis=-1))
    limits = (span + 2 * jnp.arange(blocks, dtype=jnp.int32))[None, :, None]
    return (paired < limits).astype(jnp.int32).reshape(MB, IMAGES)


def grad_scales():
    head = 1.5 * math.sqrt(MB) / (OUT * math.sqrt(IMAGES))
    conv = head / 8.0
    conv_count = D_IN * MID + 9 * MID * MID + MID * OUT + D_IN * OUT
    head_count = 3 * OUT * OUT + 2 * OUT * PRED
    conv_norm = 2 * MID + 2 * OUT
    head_norm = NORM - conv_norm
    pieces = [(conv, conv_count), (head, head_count), (conv, conv_norm), (head, head_norm), (conv, conv_norm), (head, head_norm + OUT), (head, FLAT - PARAMS)]
    return jnp.concatenate([jnp.full((count,), value, jnp.float32) for value, count in pieces])


def draw_params(key, part):
    keys = jax.random.split(jax.random.fold_in(key, 3), 10)
    fans = [D_IN, 9 * MID, MID, D_IN, OUT, OUT, PRED]
    counts = [D_IN * MID, 9 * MID * MID, MID * OUT, D_IN * OUT, 3 * OUT * OUT, OUT * PRED, PRED * OUT]
    pieces = []
    for index in range(7):
        pieces.append(jnp.clip(jax.random.normal(keys[index], (counts[index],), jnp.float32), -5.0, 5.0) / math.sqrt(fans[index]))
    pieces.append(jax.random.uniform(keys[7], (NORM,), jnp.float32, 0.6, 1.4))
    pieces.append(0.3 * jnp.clip(jax.random.normal(keys[8], (NORM,), jnp.float32), -5.0, 5.0))
    pieces.append(0.3 * jnp.clip(jax.random.normal(keys[9], (OUT,), jnp.float32), -5.0, 5.0))
    pieces.append(jnp.zeros((FLAT - PARAMS,), jnp.float32))
    return jnp.concatenate(pieces)


def draw_first(key, part):
    key = jax.random.fold_in(key, 4)
    return grad_scales() * jax.random.uniform(key, (FLAT,), jnp.float32, -1.5, 1.5)


def draw_second(key, part):
    key = jax.random.fold_in(key, 5)
    scales = grad_scales()
    factor = jnp.exp(jax.random.uniform(key, (FLAT,), jnp.float32, math.log(0.5), math.log(2.0)))
    return 2.0 * scales * scales * factor


def draw_running(key, part):
    keys = jax.random.split(jax.random.fold_in(key, 6), 2)
    means = 0.2 * jnp.clip(jax.random.normal(keys[0], (NORM,), jnp.float32), -5.0, 5.0)
    variances = jnp.exp(jax.random.uniform(keys[1], (NORM,), jnp.float32, math.log(0.5), math.log(2.0)))
    return jnp.stack([means, variances])


def setup_inputs(seed: int = 0) -> dict:
    seeds = jax.random.split(jax.random.key(seed), 9)
    return {
        "inputs": draw_inputs(jax.random.fold_in(seeds[8], 71), 0),
        "masks": draw_masks(jax.random.fold_in(seeds[8], 71), 0),
        "partner": draw_partner(jax.random.fold_in(seeds[8], 71), 0),
        "live": draw_live(jax.random.fold_in(seeds[8], 71), 0),
        "params": draw_params(jax.random.fold_in(seeds[8], 71), 0),
        "first": draw_first(jax.random.fold_in(seeds[8], 71), 0),
        "second": draw_second(jax.random.fold_in(seeds[8], 71), 0),
        "running": draw_running(jax.random.fold_in(seeds[8], 71), 0),
    }


EPS_NORM = 1e-05
MOMENTUM = 0.1
RATE = 0.03
BETA_ONE = 0.5
BETA_TWO = 0.5
DECAY = 0.01
ADAM_EPS = 1e-08
COS_EPS = 1e-06

@jax.custom_vjp
def low(v):
    return lax.optimization_barrier(v.astype(jnp.bfloat16)).astype(jnp.float32)

@jax.custom_vjp
def low_back(v):
    return v

def low_keep(v):
    return (low(v), None)

def low_pass(kept, grad):
    return (grad,)

def back_keep(v):
    return (v, None)

def back_low(kept, grad):
    return (low(grad),)
low.defvjp(low_keep, low_pass)
low_back.defvjp(back_keep, back_low)

def layout():
    return [('conv_in', (D_IN, MID)), ('conv_mid', (9 * MID, MID)), ('conv_out', (MID, OUT)), ('conv_side', (D_IN, OUT)), ('project', (3, OUT, OUT)), ('predict_in', (OUT, PRED)), ('predict_out', (PRED, OUT)), ('gammas', (NORM,)), ('betas', (NORM,)), ('pred_bias', (OUT,))]

def split(flat):
    pieces = {}
    offset = 0
    for name, shape in layout():
        count = math.prod(shape)
        pieces[name] = flat[offset:offset + count].reshape(shape)
        offset += count
    return pieces

def norm_ranges():
    widths = [MID, MID, OUT, OUT, OUT, OUT, OUT, PRED]
    return [(sum(widths[:layer]), widths[layer]) for layer in range(8)]

def product(left, right):
    return jnp.einsum('...c,cd->...d', left, right, precision=lax.Precision.HIGHEST)

def taps(padded, rows_out, cols_out):
    found = []
    for row_tap in range(3):
        for col_tap in range(3):
            found.append(padded[:, row_tap:row_tap + 2 * rows_out - 1:2, col_tap:col_tap + 2 * cols_out - 1:2])
    return jnp.concatenate(found, axis=-1)

def batch_norm(hidden, weight, gamma, beta):
    axes = tuple(range(hidden.ndim - 1))
    total = jnp.sum(weight)
    average = lax.optimization_barrier(jnp.sum(weight * hidden, axis=axes)) / total
    variance = lax.optimization_barrier(jnp.sum(weight * hidden * hidden, axis=axes)) / total - average * average
    return (gamma * (hidden - average) * lax.rsqrt(variance + EPS_NORM) + beta, average, variance)

def forward_one(weights, images, weight_in, partner_row, live_row, target):
    ranges = norm_ranges()
    averages, variances = ([], [])

    def norm(hidden, weight, layer):
        start, width = ranges[layer]
        normed, average, variance = batch_norm(hidden, weight, weights['gammas'][start:start + width], weights['betas'][start:start + width])
        averages.append(average)
        variances.append(variance)
        return normed
    hidden_in = low_back(product(images, weights['conv_in']))
    act_in = low(jax.nn.silu(norm(hidden_in, weight_in, 0)) * weight_in)
    padded = jnp.pad(act_in, ((0, 0), (1, 0), (1, 0), (0, 0)))
    columns = taps(padded, HEIGHT // 2, WIDTH // 2)
    weight_out = weight_in[:, ::2, ::2]
    hidden_mid = low_back(product(columns, weights['conv_mid']))
    act_mid = low(jax.nn.silu(norm(hidden_mid, weight_out, 1)) * weight_out)
    hidden_out = low_back(product(act_mid, weights['conv_out']))
    hidden_side = low_back(product(images[:, ::2, ::2], weights['conv_side']))
    joined = norm(hidden_out, weight_out, 2) + norm(hidden_side, weight_out, 3)
    result = jax.nn.silu(joined) * weight_out
    pooled = lax.optimization_barrier(jnp.sum(result, axis=(1, 2))) / lax.optimization_barrier(jnp.sum(weight_out, axis=(1, 2)))
    ones = jnp.ones((pooled.shape[0], 1), jnp.float32)
    act = pooled
    for layer in range(3):
        hidden = low_back(product(low(act), weights['project'][layer]))
        act = norm(hidden, ones, 4 + layer)
        if layer < 2:
            act = jax.nn.silu(act)
    latent = act
    hidden_pred = low_back(product(low(latent), weights['predict_in']))
    act_pred = low(jax.nn.silu(norm(hidden_pred, ones, 7)))
    predicted = low_back(product(act_pred, weights['predict_out'])) + weights['pred_bias']
    goal = target[partner_row]
    cosine = lax.optimization_barrier(jnp.sum(predicted * goal, axis=-1)) * lax.rsqrt(lax.optimization_barrier(jnp.sum(predicted * predicted, axis=-1)) + COS_EPS) * lax.rsqrt(lax.optimization_barrier(jnp.sum(goal * goal, axis=-1)) + COS_EPS)
    flags = live_row.astype(jnp.float32)
    return (-jnp.sum(flags * cosine), jnp.sum(flags), latent, jnp.concatenate(averages), jnp.concatenate(variances))

def reference(inputs, masks, partner, live, params, first, second, running):

    def total_loss(flat, targets):
        weights = split(low(flat)[:PARAMS])
        objective = jnp.float32(0.0)
        extras = []
        for micro in range(MB):
            weight_in = masks[micro].astype(jnp.float32)[..., None]
            images = inputs[micro].astype(jnp.float32) * weight_in
            loss_sum, count, latent, average, variance = forward_one(weights, images, weight_in, partner[micro], live[micro], targets[micro])
            objective = objective + loss_sum / count
            extras.append((loss_sum, latent, average, variance))
        return (objective, extras)
    ignored, first_extras = total_loss(params, jnp.zeros((MB, IMAGES, OUT), jnp.float32))
    targets = jnp.stack([entry[1] for entry in first_extras])
    objective, pullback, extras = jax.vjp(lambda flat: total_loss(flat, targets), params, has_aux=True)
    grad, = pullback(jnp.float32(1.0))
    new_first = BETA_ONE * first + (1.0 - BETA_ONE) * grad
    new_second = BETA_TWO * second + (1.0 - BETA_TWO) * grad * grad
    corrected_first = new_first / (1.0 - BETA_ONE ** STEP)
    corrected_second = new_second / (1.0 - BETA_TWO ** STEP)
    new_params = params - RATE * (corrected_first / (jnp.sqrt(corrected_second) + ADAM_EPS) + DECAY * params)
    run_mean, run_var = (running[0], running[1])
    for micro in range(MB):
        run_mean = (1.0 - MOMENTUM) * run_mean + MOMENTUM * extras[micro][2]
        run_var = (1.0 - MOMENTUM) * run_var + MOMENTUM * extras[micro][3]
    loss_sums = jnp.stack([entry[0] for entry in extras])
    pair_counts = lax.optimization_barrier(jnp.sum(live, axis=1)).astype(jnp.int32)
    return (loss_sums, pair_counts, new_params, new_first, new_second, new_params.astype(jnp.bfloat16), jnp.stack([run_mean, run_var]))
```

```python
import jax
import jax.numpy as jnp
from jax import lax
from jax.experimental import pallas as pl
from jax.experimental.pallas import tpu as pltpu
from jax.sharding import Mesh, PartitionSpec as P

D_IN = 1024
MID = 512
OUT = 2048
PRED = 512
MB = 4
STEP = 5
NORM = 11776
PARAMS = 20734976

EPS_NORM = 1e-05
MOMENTUM = 0.1
RATE = 0.03
BETA_ONE = 0.5
BETA_TWO = 0.5
DECAY = 0.01
ADAM_EPS = 1e-08
COS_EPS = 1e-06

ROW_CIN, ROW_CMID, ROW_COUT, ROW_SIDE = 0, 256, 1408, 1920
ROW_PROJ, ROW_PIN, ROW_POUT, ROW_VEC = 2944, 9088, 9600, 10112
LANES = 8
ALL = ("g", "p", "x", "c")
PLANE = ("p", "x", "c")
F32, BF16 = jnp.float32, jnp.bfloat16


def params_of(mib=60, steps=1):
    return pltpu.CompilerParams(
        vmem_limit_bytes=mib << 20, dimension_semantics=("arbitrary",) * steps
    )


def whole_block(shape):
    zeros = (0,) * len(shape)
    return pl.BlockSpec(shape, lambda *_: zeros)


def sigmoid(v):
    return 1.0 / (1.0 + jnp.exp(-v))


def dot(a, b):
    return jnp.dot(a, b, preferred_element_type=F32)


def dot_nt(a, b):
    return lax.dot_general(a, b, (((1,), (1,)), ((), ())), preferred_element_type=F32)


def dot_tn(a, b):
    return lax.dot_general(a, b, (((0,), (0,)), ((), ())), preferred_element_type=F32)


def fold(v):
    return jnp.sum(v.reshape(-1, 8, v.shape[-1]), axis=0)


def unwide(wide_ref, scratch, out_ref):
    rows = wide_ref.shape[0]
    for part in range(4):
        for col in range(4):
            lanes = pl.ds(part * 512 + col * 128, 128)
            scratch[col, pl.ds(part, rows, stride=4), :] = wide_ref[:, lanes].astype(F32)
    for col in range(4):
        out_ref[:, col * 128 : (col + 1) * 128] = scratch[col].astype(BF16)


def window_kernel(off_ref, flat_ref, out_ref):
    off = off_ref[0]
    rows = out_ref.shape[0]
    for col in range(16):
        out_ref[:, col * 128 : (col + 1) * 128] = flat_ref[pl.ds(off + col, rows, stride=16), :].astype(BF16)


def flat_to_window(params, rows, shift, index, count):
    own = params.shape[0] // 128
    head = shift * count
    nxt = lax.ppermute(
        params[: head * 128].astype(BF16), ALL, [(i + 1, i) for i in range(count - 1)]
    )
    flat = jnp.concatenate([params, nxt.astype(F32), jnp.zeros((1024,), F32)]).reshape(-1, 128)
    return pl.pallas_call(
        window_kernel,
        out_shape=jax.ShapeDtypeStruct((rows, 2048), BF16),
        in_specs=[pl.BlockSpec(memory_space=pltpu.SMEM), whole_block((own + head + 8, 128))],
        out_specs=whole_block((rows, 2048)),
        compiler_params=pltpu.CompilerParams(vmem_limit_bytes=40 << 20),
    )((index * shift).astype(jnp.int32)[None], flat)


def adam(grad, params, first, second):
    new_first = BETA_ONE * first + (1.0 - BETA_ONE) * grad
    new_second = BETA_TWO * second + (1.0 - BETA_TWO) * grad * grad
    corrected_first = new_first / (1.0 - BETA_ONE**STEP)
    corrected_second = new_second / (1.0 - BETA_TWO**STEP)
    new_params = params - RATE * (
        corrected_first / (jnp.sqrt(corrected_second) + ADAM_EPS) + DECAY * params
    )
    return new_params, new_first, new_second


def adam_kernel(off_ref, tail_ref, win_ref, p_ref, m_ref, v_ref, po_ref, mo_ref, vo_ref, co_ref, flat):
    step = pl.program_id(0)

    @pl.when(step == 0)
    def _():
        tail = tail_ref.shape[0]
        rows = win_ref.shape[0]
        for col in range(16):
            lanes = pl.ds(col * 128, 128)
            flat[pl.ds(col, tail, stride=16), :] = tail_ref[:, lanes].astype(F32)
            flat[pl.ds(tail * 16 + col, rows, stride=16), :] = win_ref[:, lanes].astype(F32)

    size = p_ref.shape[0]
    grad = flat[pl.ds(off_ref[0] + step * size, size), :]
    po_ref[...], mo_ref[...], vo_ref[...] = adam(grad, p_ref[...], m_ref[...], v_ref[...])
    co_ref[...] = po_ref[...].astype(BF16)


def adam_from_window(window, shift, index, count, params, first, second):
    own = params.shape[0] // 128
    rows = window.shape[0]
    tail = -(-shift * (count - 1) // 256) * 16
    block = 512
    steps = -(-own // block)
    assert steps * block <= rows * 16
    prev = lax.ppermute(window[rows - tail :], ALL, [(i, i + 1) for i in range(count - 1)])
    off = (tail * 16 - index * shift).astype(jnp.int32)[None]
    spec = pl.BlockSpec((block, 128), lambda i: (i, 0))
    shaped = [v.reshape(own, 128) for v in (params, first, second)]
    outs = pl.pallas_call(
        adam_kernel,
        grid=(steps,),
        out_shape=[jax.ShapeDtypeStruct((own, 128), F32)] * 3 + [jax.ShapeDtypeStruct((own, 128), BF16)],
        in_specs=[pl.BlockSpec(memory_space=pltpu.SMEM), whole_block((tail, 2048)), whole_block((rows, 2048))] + [spec] * 3,
        out_specs=[spec] * 4,
        scratch_shapes=[pltpu.VMEM(((tail + rows) * 16, 128), F32)],
        compiler_params=params_of(40),
    )(off, prev, window, *shaped)
    return [v.reshape(-1) for v in outs]


def conv_in_kernel(x_ref, xh_ref, w_ref, w2_ref, wide_ref, h_ref, hh_ref, xe_ref, st_ref, wf, wb, hs, xs):
    micro, part = pl.program_id(0), pl.program_id(1)

    @pl.when((micro == 0) & (part == 0))
    def _():
        unwide(wide_ref, wf, wb)

    images = x_ref.shape[1] // 64
    h = dot(x_ref[0], wb[...])
    hh = dot(xh_ref[0], wb[...])
    for col in range(4):
        hs[col, 0 : images * 64, :] = h[:, col * 128 : (col + 1) * 128]
        hs[col, images * 64 :, :] = hh[:, col * 128 : (col + 1) * 128]

    def body(i, carry):
        at = pl.multiple_of(i * 64, 64)
        low = pl.multiple_of(i * 16, 16)
        w = jnp.broadcast_to(w_ref[0, pl.ds(at, 64), :], (64, 128))
        new = []
        for col in range(4):
            lanes = slice(col * 128, (col + 1) * 128)
            h = hs[col, pl.ds(at, 64), :] * w
            new.append((carry[col][0] + fold(h), carry[col][1] + fold(h * h)))
            hs[col, pl.ds(at, 64), :] = h
            for side in range(2):
                half = hs[col, pl.ds(at + side, 32, stride=2), :].reshape(2, 2, 8, 128)
                for row in range(2):
                    h_ref[0, 2 * row + side, pl.ds(low, 16), lanes] = half[:, row].reshape(16, 128)
                hat = pl.multiple_of(i * 8, 8)
                hh_ref[0, side, pl.ds(hat, 8), lanes] = hs[col, pl.ds(images * 64 + low + side, 8, stride=2), :]
        w = jnp.broadcast_to(w2_ref[0, pl.ds(low, 16), :], (16, 128))
        for col in range(8):
            lanes = slice(col * 128, (col + 1) * 128)
            for row in range(2):
                xs[col, row * 16 : row * 16 + 16, :] = x_ref[0, pl.ds(at + row * 32, 16), lanes].astype(F32)
            xe_ref[0, pl.ds(low, 16), lanes] = (xs[col, pl.ds(0, 16, stride=2), :] * w).astype(BF16)
        return tuple(new)

    zero = jnp.zeros((8, 128), F32)
    found = lax.fori_loop(0, images, body, ((zero, zero),) * 4)

    @pl.when(part == 0)
    def _():
        st_ref[...] = jnp.zeros_like(st_ref)

    for col in range(4):
        lanes = slice(col * 128, (col + 1) * 128)
        for k in range(2):
            st_ref[0, k : k + 1, lanes] += jnp.sum(found[col][k], axis=0, keepdims=True)


def conv_in(x, xh, w, w2, wide):
    micros, pixels, _ = x.shape
    images = pixels // 64
    parts = 2
    b = images // parts
    return pl.pallas_call(
        conv_in_kernel,
        grid=(micros, parts),
        out_shape=[
            jax.ShapeDtypeStruct((micros, 4, images * 16, MID), F32),
            jax.ShapeDtypeStruct((micros, 2, images * 8, MID), F32),
            jax.ShapeDtypeStruct((micros, images * 16, D_IN), BF16),
            jax.ShapeDtypeStruct((micros, 8, MID), F32),
        ],
        in_specs=[
            pl.BlockSpec((1, b * 64, D_IN), lambda m, k: (m, k, 0)),
            pl.BlockSpec((1, b * 16, D_IN), lambda m, k: (m, k, 0)),
            pl.BlockSpec((1, b * 64, 1), lambda m, k: (m, k, 0)),
            pl.BlockSpec((1, b * 16, 1), lambda m, k: (m, k, 0)),
            whole_block((256, 2048)),
        ],
        out_specs=[
            pl.BlockSpec((1, 4, b * 16, MID), lambda m, k: (m, 0, k, 0)),
            pl.BlockSpec((1, 2, b * 8, MID), lambda m, k: (m, 0, k, 0)),
            pl.BlockSpec((1, b * 16, D_IN), lambda m, k: (m, k, 0)),
            pl.BlockSpec((1, 8, MID), lambda m, k: (m, 0, 0)),
        ],
        scratch_shapes=[
            pltpu.VMEM((4, D_IN, 128), F32),
            pltpu.VMEM((D_IN, MID), BF16),
            pltpu.VMEM((4, b * 80, 128), F32),
            pltpu.VMEM((8, 32, 128), F32),
        ],
        compiler_params=params_of(56, 2),
        cost_estimate=pl.CostEstimate(
            flops=2 * micros * images * 80 * D_IN * MID, bytes_accessed=40 << 20, transcendentals=0
        ),
    )(x, xh, w, w2, wide)


def side_kernel(xe_ref, w_ref, hs_ref, st_ref):
    h = dot(xe_ref[0], w_ref[...])
    hs_ref[0] = h
    st_ref[...] = jnp.zeros_like(st_ref)
    st_ref[0, 0:1, :] = jnp.sum(h, axis=0, keepdims=True)
    st_ref[0, 1:2, :] = jnp.sum(h * h, axis=0, keepdims=True)


def conv_side(xe, weight):
    micros, rows, _ = xe.shape
    cols = 4
    n = OUT // cols
    return pl.pallas_call(
        side_kernel,
        grid=(micros, cols),
        out_shape=[
            jax.ShapeDtypeStruct((micros, rows, OUT), F32),
            jax.ShapeDtypeStruct((micros, 8, OUT), F32),
        ],
        in_specs=[
            pl.BlockSpec((1, rows, D_IN), lambda m, k: (m, 0, 0)),
            pl.BlockSpec((D_IN, n), lambda m, k: (0, k)),
        ],
        out_specs=[
            pl.BlockSpec((1, rows, n), lambda m, k: (m, 0, k)),
            pl.BlockSpec((1, 8, n), lambda m, k: (m, 0, k)),
        ],
        compiler_params=params_of(56, 2),
        cost_estimate=pl.CostEstimate(
            flops=2 * micros * rows * D_IN * OUT, bytes_accessed=16 << 20, transcendentals=0
        ),
    )(xe, weight)


def shift_right(v):
    moved = pltpu.roll(v, 1, 1)
    return jnp.where(lax.broadcasted_iota(jnp.int32, v.shape, 1) == 0, 0.0, moved)


def shift_left(v):
    moved = pltpu.roll(v, 7, 1)
    return jnp.where(lax.broadcasted_iota(jnp.int32, v.shape, 1) == 7, 0.0, moved)


def conv_mid_kernel(h_ref, hh_ref, cf_ref, w_ref, wh_ref, wide_ref, cols_ref, hm_ref, st_ref, wb, wf):
    micro = pl.program_id(0)

    @pl.when(micro == 0)
    def _():
        unwide(wide_ref, wf, wb)

    images = h_ref.shape[2] // 16
    scale, shift = cf_ref[0, 0:1, :], cf_ref[0, 1:2, :]

    def act(h, w):
        v = h * scale + shift
        return v * sigmoid(v) * w

    def body(i, carry):
        at = pl.ds(pl.multiple_of(i * 16, 16), 16)
        half = pl.ds(pl.multiple_of(i * 8, 8), 8)
        a = [act(h_ref[0, k, at, :], w_ref[0, k, at, :]).reshape(2, 8, MID) for k in range(4)]
        above = [act(hh_ref[0, k, half, :], wh_ref[0, k, half, :]).reshape(1, 8, MID) for k in range(2)]
        a1s, a3s = shift_right(a[1]), shift_right(a[3])
        up2 = jnp.concatenate([above[0], a[2][:1]], axis=0)
        up3 = jnp.concatenate([above[1], a[3][:1]], axis=0)
        up3s = jnp.concatenate([shift_right(above[1]), a3s[:1]], axis=0)
        for tap, value in enumerate([up3s, up2, up3, a1s, a[0], a[1], a3s, a[2], a[3]]):
            cols_ref[0, at, tap * MID : (tap + 1) * MID] = value.reshape(16, MID).astype(BF16)
        return carry

    lax.fori_loop(0, images, body, 0)
    h = dot(cols_ref[0], wb[...])
    hm_ref[0] = h
    hw = h * w_ref[0, 0]
    st_ref[...] = jnp.zeros_like(st_ref)
    st_ref[0, 0:1, :] = jnp.sum(hw, axis=0, keepdims=True)
    st_ref[0, 1:2, :] = jnp.sum(hw * hw, axis=0, keepdims=True)


def conv_mid(h, hh, coef, wph, whalo, wide):
    micros, _, rows, _ = h.shape
    return pl.pallas_call(
        conv_mid_kernel,
        grid=(micros,),
        out_shape=[
            jax.ShapeDtypeStruct((micros, rows, 9 * MID), BF16),
            jax.ShapeDtypeStruct((micros, rows, MID), F32),
            jax.ShapeDtypeStruct((micros, 8, MID), F32),
            jax.ShapeDtypeStruct((9 * MID, MID), BF16),
        ],
        in_specs=[
            pl.BlockSpec((1, 4, rows, MID), lambda m: (m, 0, 0, 0)),
            pl.BlockSpec((1, 2, rows // 2, MID), lambda m: (m, 0, 0, 0)),
            pl.BlockSpec((1, 8, MID), lambda m: (m, 0, 0)),
            pl.BlockSpec((1, 4, rows, 1), lambda m: (m, 0, 0, 0)),
            pl.BlockSpec((1, 2, rows // 2, 1), lambda m: (m, 0, 0, 0)),
            whole_block((1152, 2048)),
        ],
        out_specs=[
            pl.BlockSpec((1, rows, 9 * MID), lambda m: (m, 0, 0)),
            pl.BlockSpec((1, rows, MID), lambda m: (m, 0, 0)),
            pl.BlockSpec((1, 8, MID), lambda m: (m, 0, 0)),
            pl.BlockSpec((9 * MID, MID), lambda m: (0, 0), pipeline_mode=pl.Buffered(1)),
        ],
        scratch_shapes=[pltpu.VMEM((4, 9 * MID, 128), F32)],
        compiler_params=params_of(60),
        cost_estimate=pl.CostEstimate(
            flops=2 * micros * rows * 9 * MID * MID, bytes_accessed=50 << 20, transcendentals=0
        ),
    )(h, hh, coef, wph, whalo, wide)


def conv_out_kernel(hm_ref, cf_ref, w_ref, weight_ref, am_ref, ho_ref, st_ref):
    v = hm_ref[0] * cf_ref[0, 0:1, :] + cf_ref[0, 1:2, :]
    am = (v * sigmoid(v) * w_ref[0, 0]).astype(BF16)
    am_ref[0] = am
    st_ref[...] = jnp.zeros_like(st_ref)
    for k in range(4):
        lanes = slice(k * 512, (k + 1) * 512)
        h = dot(am, weight_ref[:, lanes])
        ho_ref[0, :, lanes] = h
        st_ref[0, 0:1, lanes] = jnp.sum(h, axis=0, keepdims=True)
        st_ref[0, 1:2, lanes] = jnp.sum(h * h, axis=0, keepdims=True)


def conv_out(hm, coef, wph, weight):
    micros, rows, _ = hm.shape
    return pl.pallas_call(
        conv_out_kernel,
        grid=(micros,),
        out_shape=[
            jax.ShapeDtypeStruct((micros, rows, MID), BF16),
            jax.ShapeDtypeStruct((micros, rows, OUT), F32),
            jax.ShapeDtypeStruct((micros, 8, OUT), F32),
        ],
        in_specs=[
            pl.BlockSpec((1, rows, MID), lambda m: (m, 0, 0)),
            pl.BlockSpec((1, 8, MID), lambda m: (m, 0, 0)),
            pl.BlockSpec((1, 1, rows, 1), lambda m: (m, 0, 0, 0)),
            whole_block((MID, OUT)),
        ],
        out_specs=[
            pl.BlockSpec((1, rows, MID), lambda m: (m, 0, 0)),
            pl.BlockSpec((1, rows, OUT), lambda m: (m, 0, 0)),
            pl.BlockSpec((1, 8, OUT), lambda m: (m, 0, 0)),
        ],
        compiler_params=params_of(56),
        cost_estimate=pl.CostEstimate(
            flops=2 * micros * rows * MID * OUT, bytes_accessed=18 << 20, transcendentals=0
        ),
    )(hm, coef, wph, weight)


def pool_kernel(ho_ref, hs_ref, cf_ref, w_ref, out_ref):
    images = out_ref.shape[1]
    so, ss, shift = cf_ref[0, 0:1, :], cf_ref[0, 1:2, :], cf_ref[0, 2:3, :]

    def body(i, carry):
        total = []
        for k in range(8):
            at = pl.ds(pl.multiple_of(i * 128 + k * 16, 16), 16)
            j = ho_ref[0, at, :] * so + hs_ref[0, at, :] * ss + shift
            r = j * sigmoid(j) * w_ref[0, 0, at, :]
            total.append(jnp.sum(r, axis=0, keepdims=True))
        out_ref[0, pl.ds(pl.multiple_of(i * 8, 8), 8), :] = jnp.concatenate(total, axis=0)
        return carry

    lax.fori_loop(0, images // 8, body, 0)


def pool(ho, hs, coef, wph):
    micros, rows, _ = ho.shape
    n = 512
    images = rows // 16
    return pl.pallas_call(
        pool_kernel,
        grid=(micros, OUT // n),
        out_shape=jax.ShapeDtypeStruct((micros, images, OUT), F32),
        in_specs=[
            pl.BlockSpec((1, rows, n), lambda m, k: (m, 0, k)),
            pl.BlockSpec((1, rows, n), lambda m, k: (m, 0, k)),
            pl.BlockSpec((1, 8, n), lambda m, k: (m, 0, k)),
            pl.BlockSpec((1, 1, rows, 1), lambda m, k: (m, 0, 0, 0)),
        ],
        out_specs=pl.BlockSpec((1, images, n), lambda m, k: (m, 0, k)),
        compiler_params=params_of(56, 2),
        cost_estimate=pl.CostEstimate(
            flops=20 * micros * rows * OUT, bytes_accessed=18 << 20, transcendentals=micros * rows * OUT
        ),
    )(ho, hs, coef, wph)


def slope_kernel(ho_ref, hs_ref, cf_ref, w_ref, out_ref):
    images = out_ref.shape[2]
    so, ss, shift = cf_ref[0, 0:1, :], cf_ref[0, 1:2, :], cf_ref[0, 2:3, :]

    def body(i, carry):
        plain, out, side = [], [], []
        for k in range(8):
            at = pl.ds(pl.multiple_of(i * 128 + k * 16, 16), 16)
            ho, hs = ho_ref[0, at, :], hs_ref[0, at, :]
            j = ho * so + hs * ss + shift
            s = sigmoid(j)
            d = s * (1.0 + j * (1.0 - s)) * w_ref[0, 0, at, :]
            plain.append(jnp.sum(d, axis=0, keepdims=True))
            out.append(jnp.sum(d * ho, axis=0, keepdims=True))
            side.append(jnp.sum(d * hs, axis=0, keepdims=True))
        at = pl.ds(pl.multiple_of(i * 8, 8), 8)
        for k, value in enumerate((plain, out, side)):
            out_ref[0, k, at, :] = jnp.concatenate(value, axis=0)
        return carry

    lax.fori_loop(0, images // 8, body, 0)


def slopes(ho, hs, coef, wph):
    micros, rows, _ = ho.shape
    n = 512
    images = rows // 16
    return pl.pallas_call(
        slope_kernel,
        grid=(micros, OUT // n),
        out_shape=jax.ShapeDtypeStruct((micros, 3, images, OUT), F32),
        in_specs=[
            pl.BlockSpec((1, rows, n), lambda m, k: (m, 0, k)),
            pl.BlockSpec((1, rows, n), lambda m, k: (m, 0, k)),
            pl.BlockSpec((1, 8, n), lambda m, k: (m, 0, k)),
            pl.BlockSpec((1, 1, rows, 1), lambda m, k: (m, 0, 0, 0)),
        ],
        out_specs=pl.BlockSpec((1, 3, images, n), lambda m, k: (m, 0, 0, k)),
        compiler_params=params_of(56, 2),
        cost_estimate=pl.CostEstimate(
            flops=30 * micros * rows * OUT, bytes_accessed=20 << 20, transcendentals=micros * rows * OUT
        ),
    )(ho, hs, coef, wph)


def back_out_kernel(
    ho_ref, hs_ref, gs_ref, cf_ref, w_ref, am_ref, xe_ref, wo_ref, hm_ref, cm_ref,
    d_ref, st_ref, gw_ref, amt, xet, da, dho, dhs, acc_out, acc_side,
):
    micro, part = pl.program_id(0), pl.program_id(1)
    parts = pl.num_programs(1)
    images = gs_ref.shape[1]

    @pl.when(part == 0)
    def _():
        amt[...] = am_ref[0].T
        xet[...] = xe_ref[0].T

    cf = [cf_ref[0, k : k + 1, :] for k in range(7)]

    def body(i, carry):
        gs = gs_ref[0, pl.ds(pl.multiple_of(i * 8, 8), 8), :]
        for k in range(8):
            at = pl.ds(pl.multiple_of(i * 128 + k * 16, 16), 16)
            ho, hs = ho_ref[0, at, :], hs_ref[0, at, :]
            w = w_ref[0, 0, at, :]
            j = ho * cf[0] + hs * cf[1] + cf[2]
            s = sigmoid(j)
            g = s * (1.0 + j * (1.0 - s)) * gs[k : k + 1, :]
            dho[at, :] = ((g * cf[0] + cf[3] + ho * cf[4]) * w).astype(BF16)
            dhs[at, :] = ((g * cf[1] + cf[5] + hs * cf[6]) * w).astype(BF16)
        return carry

    lax.fori_loop(0, images // 8, body, 0)
    g_out = dot(amt[...], dho[...])
    g_side = dot(xet[...], dhs[...])
    back = dot_nt(dho[...], wo_ref[...])

    @pl.when(micro == 0)
    def _():
        acc_out[part] = g_out
        acc_side[part] = g_side

    @pl.when(micro > 0)
    def _():
        acc_out[part] += g_out
        acc_side[part] += g_side

    @pl.when(part == 0)
    def _():
        da[...] = back

    @pl.when(part > 0)
    def _():
        da[...] += back

    @pl.when(part == parts - 1)
    def _():
        hm = hm_ref[0]
        v = hm * cm_ref[0, 0:1, :] + cm_ref[0, 1:2, :]
        s = sigmoid(v)
        d = s * (1.0 + v * (1.0 - s)) * da[...] * w_ref[0, 0]
        d_ref[0] = d
        st_ref[...] = jnp.zeros_like(st_ref)
        st_ref[0, 0:1, :] = jnp.sum(d, axis=0, keepdims=True)
        st_ref[0, 1:2, :] = jnp.sum(d * hm, axis=0, keepdims=True)

    @pl.when((micro == pl.num_programs(0) - 1) & (part == parts - 1))
    def _():
        for k in range(4):
            for half in range(2):
                lanes = slice(half * 256, half * 256 + 256)
                gw_ref[2 * k + half, 0:MID, :] = acc_out[k, :, lanes].astype(BF16)
                gw_ref[2 * k + half, MID:, :] = acc_side[k, :, lanes].astype(BF16)


def back_out(ho, hs, gs, coef, wph, am, xe, weight, hm, coef_mid):
    micros, rows, _ = ho.shape
    n = 512
    images = rows // 16
    return pl.pallas_call(
        back_out_kernel,
        grid=(micros, OUT // n),
        out_shape=[
            jax.ShapeDtypeStruct((micros, rows, MID), F32),
            jax.ShapeDtypeStruct((micros, 8, MID), F32),
            jax.ShapeDtypeStruct((LANES, MID + D_IN, 256), BF16),
        ],
        in_specs=[
            pl.BlockSpec((1, rows, n), lambda m, k: (m, 0, k)),
            pl.BlockSpec((1, rows, n), lambda m, k: (m, 0, k)),
            pl.BlockSpec((1, images, n), lambda m, k: (m, 0, k)),
            pl.BlockSpec((1, 8, n), lambda m, k: (m, 0, k)),
            pl.BlockSpec((1, 1, rows, 1), lambda m, k: (m, 0, 0, 0)),
            pl.BlockSpec((1, rows, MID), lambda m, k: (m, 0, 0)),
            pl.BlockSpec((1, rows, D_IN), lambda m, k: (m, 0, 0)),
            pl.BlockSpec((MID, n), lambda m, k: (0, k)),
            pl.BlockSpec((1, rows, MID), lambda m, k: (m, 0, 0)),
            pl.BlockSpec((1, 8, MID), lambda m, k: (m, 0, 0)),
        ],
        out_specs=[
            pl.BlockSpec((1, rows, MID), lambda m, k: (m, 0, 0)),
            pl.BlockSpec((1, 8, MID), lambda m, k: (m, 0, 0)),
            whole_block((LANES, MID + D_IN, 256)),
        ],
        scratch_shapes=[
            pltpu.VMEM((MID, rows), BF16),
            pltpu.VMEM((D_IN, rows), BF16),
            pltpu.VMEM((rows, MID), F32),
            pltpu.VMEM((rows, n), BF16),
            pltpu.VMEM((rows, n), BF16),
            pltpu.VMEM((OUT // n, MID, n), F32),
            pltpu.VMEM((OUT // n, D_IN, n), F32),
        ],
        compiler_params=params_of(60, 2),
        cost_estimate=pl.CostEstimate(
            flops=2 * micros * rows * OUT * (2 * MID + D_IN), bytes_accessed=40 << 20, transcendentals=micros * rows * OUT
        ),
    )(ho, hs, gs, coef, wph, am, xe, weight, hm, coef_mid)


def back_mid_kernel(
    hm_ref, d_ref, cm_ref, cols_ref, wb, h_ref, hh_ref, cf_ref, w_ref, wh_ref,
    din_ref, dh_ref, st_ref, gw_ref, dt, acc,
):
    micro = pl.program_id(0)
    images = h_ref.shape[2] // 16

    low = ((d_ref[0] * cm_ref[0, 0:1, :] + cm_ref[0, 1:2, :] + hm_ref[0] * cm_ref[0, 2:3, :]) * w_ref[0, 0]).astype(BF16)
    for tap in range(9):
        lanes = slice(tap * MID, (tap + 1) * MID)
        g = dot_tn(cols_ref[0, :, lanes], low)

        @pl.when(micro == 0)
        def _():
            for col in range(4):
                acc[col, lanes, :] = g[:, col * 128 : (col + 1) * 128]

        @pl.when(micro > 0)
        def _():
            for col in range(4):
                acc[col, lanes, :] += g[:, col * 128 : (col + 1) * 128]

    scale, shift = cf_ref[0, 0:1, :], cf_ref[0, 1:2, :]
    zero = jnp.zeros((8, MID), F32)

    def back(h, grad, w):
        v = h * scale + shift
        s = sigmoid(v)
        return s * (1.0 + v * (1.0 - s)) * grad * w

    def body(i, carry):
        total, product = carry
        at = pl.ds(pl.multiple_of(i * 16, 16), 16)
        half = pl.ds(pl.multiple_of(i * 8, 8), 8)
        near = pl.ds(pl.multiple_of((i % (images // 2)) * 16, 16), 16)
        t = [dt[k, near, :].reshape(2, 8, MID) for k in range(9)]
        below1 = t[1]
        below3 = t[2] + shift_left(t[0])
        last = jnp.zeros((1, 8, MID), F32)
        grads = [
            t[4],
            t[5] + shift_left(t[3]),
            t[7] + jnp.concatenate([below1[1:], last], axis=0),
            t[8] + shift_left(t[6]) + jnp.concatenate([below3[1:], last], axis=0),
        ]
        for k in range(4):
            h = h_ref[0, k, at, :]
            d = back(h, grads[k].reshape(16, MID), w_ref[0, k, at, :])
            din_ref[0, k, at, :] = d.astype(BF16)
            total = total + fold(d)
            product = product + fold(d * h)
        for k, grad in enumerate((below1, below3)):
            h = hh_ref[0, k, half, :]
            d = back(h, grad[0], wh_ref[0, k, half, :])
            dh_ref[0, k, half, :] = d
            total = total + d
            product = product + d * h
        return total, product

    found = (zero, zero)
    for part in range(2):
        start, stop = part * images // 2, (part + 1) * images // 2
        for tap in range(9):
            dt[tap] = dot_nt(low[start * 16 : stop * 16], wb[tap * MID : (tap + 1) * MID, :])
        found = lax.fori_loop(start, stop, body, found)
    total, product = found
    st_ref[...] = jnp.zeros_like(st_ref)
    st_ref[0, 0:1, :] = jnp.sum(total, axis=0, keepdims=True)
    st_ref[0, 1:2, :] = jnp.sum(product, axis=0, keepdims=True)

    @pl.when(micro == pl.num_programs(0) - 1)
    def _():
        for k in range(LANES):
            for half in range(2):
                found = acc[(k % 2) * 2 + half, pl.ds(k // 2, 9 * MID // 4, stride=4), :]
                gw_ref[k, :, half * 128 : half * 128 + 128] = found.astype(BF16)


def back_mid(hm, d, coef_mid, cols, weight, h, hh, coef, wph, whalo):
    micros, _, rows, _ = h.shape
    return pl.pallas_call(
        back_mid_kernel,
        grid=(micros,),
        out_shape=[
            jax.ShapeDtypeStruct((micros, 4, rows, MID), BF16),
            jax.ShapeDtypeStruct((micros, 2, rows // 2, MID), F32),
            jax.ShapeDtypeStruct((micros, 8, MID), F32),
            jax.ShapeDtypeStruct((LANES, 1152, 256), BF16),
        ],
        in_specs=[
            pl.BlockSpec((1, rows, MID), lambda m: (m, 0, 0)),
            pl.BlockSpec((1, rows, MID), lambda m: (m, 0, 0)),
            pl.BlockSpec((1, 8, MID), lambda m: (m, 0, 0)),
            pl.BlockSpec((1, rows, 9 * MID), lambda m: (m, 0, 0)),
            pl.BlockSpec((9 * MID, MID), lambda m: (0, 0), pipeline_mode=pl.Buffered(1)),
            pl.BlockSpec((1, 4, rows, MID), lambda m: (m, 0, 0, 0)),
            pl.BlockSpec((1, 2, rows // 2, MID), lambda m: (m, 0, 0, 0)),
            pl.BlockSpec((1, 8, MID), lambda m: (m, 0, 0)),
            pl.BlockSpec((1, 4, rows, 1), lambda m: (m, 0, 0, 0)),
            pl.BlockSpec((1, 2, rows // 2, 1), lambda m: (m, 0, 0, 0)),
        ],
        out_specs=[
            pl.BlockSpec((1, 4, rows, MID), lambda m: (m, 0, 0, 0)),
            pl.BlockSpec((1, 2, rows // 2, MID), lambda m: (m, 0, 0, 0)),
            pl.BlockSpec((1, 8, MID), lambda m: (m, 0, 0)),
            pl.BlockSpec((LANES, 1152, 256), lambda m: (0, 0, 0), pipeline_mode=pl.Buffered(1)),
        ],
        scratch_shapes=[
            pltpu.VMEM((9, rows // 2, MID), F32),
            pltpu.VMEM((4, 9 * MID, 128), F32),
        ],
        compiler_params=params_of(62),
        cost_estimate=pl.CostEstimate(
            flops=4 * micros * rows * 9 * MID * MID, bytes_accessed=60 << 20, transcendentals=micros * rows * 5 * MID
        ),
    )(hm, d, coef_mid, cols, weight, h, hh, coef, wph, whalo)


def back_in_kernel(h_ref, din_ref, dh_ref, cf_ref, w_ref, wh_ref, x_ref, xh_ref, gw_ref, ds, acc, turned):
    micro, part = pl.program_id(0), pl.program_id(1)
    images = h_ref.shape[2] // 16
    ca, cb, cc = cf_ref[0, 0:1, :], cf_ref[0, 1:2, :], cf_ref[0, 2:3, :]

    def body(i, carry):
        at = pl.ds(pl.multiple_of(i * 16, 16), 16)
        half = pl.ds(pl.multiple_of(i * 8, 8), 8)
        for k in range(4):
            h = h_ref[0, k, at, :]
            d = (din_ref[0, k, at, :].astype(F32) * ca + cb + h * cc) * w_ref[0, k, at, :]
            row, side = k // 2, k % 2
            for o in range(2):
                for col in range(4):
                    to = pl.ds(i * 64 + (2 * o + row) * 16 + side, 8, stride=2)
                    ds[col, to, :] = d[o * 8 : o * 8 + 8, col * 128 : (col + 1) * 128]
        for side in range(2):
            d = dh_ref[0, side, half, :] * ca
            for col in range(4):
                ds[col, pl.ds(images * 64 + i * 16 + side, 8, stride=2), :] = d[:, col * 128 : (col + 1) * 128]
        return carry

    lax.fori_loop(0, images, body, 0)
    low = jnp.concatenate([ds[col].astype(BF16) for col in range(4)], axis=1)
    g = dot_tn(low[: images * 64], x_ref[0]) + dot_tn(low[images * 64 :], xh_ref[0])

    @pl.when((micro == 0) & (part == 0))
    def _():
        acc[...] = g

    @pl.when((micro > 0) | (part > 0))
    def _():
        acc[...] += g

    @pl.when((micro == pl.num_programs(0) - 1) & (part == pl.num_programs(1) - 1))
    def _():
        for col in range(4):
            turned[col] = acc[col * 128 : (col + 1) * 128, :].T
        for k in range(LANES):
            for half in range(2):
                found = turned[(k % 2) * 2 + half, pl.ds(k // 2, D_IN // 4, stride=4), :]
                gw_ref[k, :, half * 128 : half * 128 + 128] = found.astype(BF16)


def back_in(h, din, dhalo, coef, wph, whalo, x, xh):
    micros, _, rows, _ = h.shape
    parts = 2
    r = rows // parts
    return pl.pallas_call(
        back_in_kernel,
        grid=(micros, parts),
        out_shape=jax.ShapeDtypeStruct((LANES, 256, 256), BF16),
        in_specs=[
            pl.BlockSpec((1, 4, r, MID), lambda m, k: (m, 0, k, 0)),
            pl.BlockSpec((1, 4, r, MID), lambda m, k: (m, 0, k, 0)),
            pl.BlockSpec((1, 2, r // 2, MID), lambda m, k: (m, 0, k, 0)),
            pl.BlockSpec((1, 8, MID), lambda m, k: (m, 0, 0)),
            pl.BlockSpec((1, 4, r, 1), lambda m, k: (m, 0, k, 0)),
            pl.BlockSpec((1, 2, r // 2, 1), lambda m, k: (m, 0, k, 0)),
            pl.BlockSpec((1, r * 4, D_IN), lambda m, k: (m, k, 0)),
            pl.BlockSpec((1, r, D_IN), lambda m, k: (m, k, 0)),
        ],
        out_specs=whole_block((LANES, 256, 256)),
        scratch_shapes=[
            pltpu.VMEM((4, r * 5, 128), F32),
            pltpu.VMEM((MID, D_IN), F32),
            pltpu.VMEM((4, D_IN, 128), F32),
        ],
        compiler_params=params_of(60, 2),
        cost_estimate=pl.CostEstimate(
            flops=2 * micros * rows * 5 * D_IN * MID, bytes_accessed=50 << 20, transcendentals=0
        ),
    )(h, din, dhalo, coef, wph, whalo, x, xh)


def swap(value, axis, bit):
    size = lax.axis_size(axis)
    return lax.ppermute(value, axis, [(i, i ^ bit) for i in range(size)])


def bits_of(axis):
    size, bit, found = lax.axis_size(axis), 1, []
    while bit < size:
        found.append(bit)
        bit *= 2
    return found


def add_all(value, axes=("c", "x", "p", "g")):
    for axis in axes:
        for bit in bits_of(axis):
            value = value + swap(value, axis, bit)
    return value


def exchange_planes(value):
    planes = lax.axis_size("g")
    here = lax.axis_index("g")
    own = lax.dynamic_index_in_dim(value, here, 0, keepdims=True)
    result = lax.dynamic_update_slice_in_dim(jnp.zeros_like(value), own, here, 0)
    for step in range(1, planes):
        block = lax.dynamic_index_in_dim(value, (here + step) % planes, 0, keepdims=True)
        got = lax.ppermute(block, "g", [(i, (i + step) % planes) for i in range(planes)])
        result = lax.dynamic_update_slice_in_dim(result, got, (here + planes - step) % planes, 0)
    return result


def gather_axis(value, axis):
    value = value[None]
    for bit in bits_of(axis):
        other = swap(value, axis, bit)
        mine = (lax.axis_index(axis) // bit) % 2
        value = jnp.where(mine == 0, jnp.concatenate([value, other]), jnp.concatenate([other, value]))
    return value


def to_heads(value):
    routed = exchange_planes(value)
    for axis in ("p", "x", "c"):
        routed = gather_axis(routed, axis)
    order = (3, 2, 1, 0, 4) + tuple(range(5, routed.ndim))
    routed = jnp.transpose(routed, order)
    return routed.reshape((-1,) + value.shape[2:])


def norm_ranges():
    widths = [MID, MID, OUT, OUT, OUT, OUT, OUT, PRED]
    return [(sum(widths[:layer]), widths[layer]) for layer in range(8)]


def silu_back(value, grad):
    gate = jax.nn.sigmoid(value)
    return grad * gate * (1.0 + value * (1.0 - gate))


def head_norm(hidden, gamma, beta):
    count = hidden.shape[0]
    average = jnp.sum(hidden, axis=0) / count
    variance = jnp.sum(hidden * hidden, axis=0) / count - average * average
    scale = lax.rsqrt(variance + EPS_NORM)
    normed = (hidden - average) * scale
    return gamma * normed + beta, (normed, scale), average, variance


def head_norm_back(grad, kept, gamma):
    normed, scale = kept
    count = grad.shape[0]
    beta_sum = jnp.sum(grad, axis=0)
    gamma_sum = jnp.sum(grad * normed, axis=0)
    back = gamma * scale * (grad - beta_sum / count - normed * gamma_sum / count)
    return back, gamma_sum, beta_sum


def heads(pooled_low, wall, gammas, betas, bias, partner, live):
    project = [wall[ROW_PROJ + 2048 * k : ROW_PROJ + 2048 * (k + 1)] for k in range(3)]
    predict_in = wall[ROW_PIN:ROW_POUT].reshape(OUT, PRED)
    predict_out = wall[ROW_POUT:ROW_VEC]
    means, variances, kept_all, normed_all, lows = [], [], [], [], []
    low = pooled_low
    for k in range(3):
        normed, kept, mean, variance = head_norm(dot(low, project[k]), gammas[4 + k], betas[4 + k])
        means.append(mean)
        variances.append(variance)
        kept_all.append(kept)
        normed_all.append(normed)
        lows.append(low)
        low = (jax.nn.silu(normed) if k < 2 else normed).astype(BF16)
    latent, latent_low = normed, low
    normed_q, kept_q, mean, variance = head_norm(dot(latent_low, predict_in), gammas[7], betas[7])
    means.append(mean)
    variances.append(variance)
    act = jax.nn.silu(normed_q).astype(BF16)
    predicted = dot(act, predict_out) + bias
    choose = (partner[:, None] == jnp.arange(latent.shape[0])[None, :]).astype(F32)
    target = jnp.dot(choose, latent, precision=lax.Precision.HIGHEST)
    inner = jnp.sum(predicted * target, axis=-1)
    inv_pred = lax.rsqrt(jnp.sum(predicted * predicted, axis=-1) + COS_EPS)
    inv_goal = lax.rsqrt(jnp.sum(target * target, axis=-1) + COS_EPS)
    flags = live.astype(F32)
    loss_sum = -jnp.sum(flags * inner * inv_pred * inv_goal)
    live_count = jnp.sum(flags)
    grad_cos = -flags / live_count
    grad_pred = grad_cos[:, None] * (
        target * (inv_pred * inv_goal)[:, None] - (inner * inv_pred**3 * inv_goal)[:, None] * predicted
    )
    grad_bias = jnp.sum(grad_pred, axis=0)
    low_p = grad_pred.astype(BF16)
    grad_act = dot_nt(low_p, predict_out)
    grad_q, gamma_q, beta_q = head_norm_back(silu_back(normed_q, grad_act), kept_q, gammas[7])
    low_q = grad_q.astype(BF16)
    grad_act = dot_nt(low_q, predict_in)
    low_f, gamma_sums, beta_sums = [None] * 3, [None] * 3, [None] * 3
    for k in (2, 1, 0):
        grad_normed = grad_act if k == 2 else silu_back(normed_all[k], grad_act)
        grad_hidden, gamma_sums[k], beta_sums[k] = head_norm_back(grad_normed, kept_all[k], gammas[4 + k])
        low_f[k] = grad_hidden.astype(BF16)
        grad_act = dot_nt(low_f[k], project[k])
    block = (lax.axis_index("p") % 2) * 4 + lax.axis_index("x") * 2 + lax.axis_index("c")

    def columns(v, start):
        return lax.dynamic_slice_in_dim(v, start, 256, 1)

    rows = [dot_tn(lows[k], columns(low_f[k], block * 256)).astype(BF16) for k in range(3)]
    g_in = dot_tn(latent_low, columns(low_q, (block % 2) * 256)).astype(BF16)
    rows.append(lax.dynamic_index_in_dim(g_in.reshape(PRED, 4, 256), block // 2, 1, keepdims=False))
    rows.append(dot_tn(act, columns(low_p, block * 256)).astype(BF16))
    vector = (gamma_sums + [gamma_q], beta_sums + [beta_q], grad_bias)
    return grad_act, jnp.concatenate(rows, axis=0), vector, block, loss_sum, live_count, means, variances


def norm_coefs(sums, total, gamma, beta):
    mean = sums[:, 0] / total[:, None]
    variance = sums[:, 1] / total[:, None] - mean * mean
    scale = lax.rsqrt(variance + EPS_NORM)
    a = gamma * scale
    return mean, variance, scale, a, beta - a * mean


def pack(rows):
    rows = list(rows) + [jnp.zeros_like(rows[0])] * (8 - len(rows))
    return jnp.stack(rows, axis=1)


def back_coefs(grad_sum, product_sum, mean, scale, a, total):
    gamma_sum = scale * (product_sum - mean * grad_sum)
    c = -a * scale * gamma_sum / total[:, None]
    b = -a * grad_sum / total[:, None] - c * mean
    return b, c, gamma_sum


def on_device(inputs, masks, partner, live, params, first, second, running):
    count = lax.axis_size(ALL)
    index = lax.axis_index(ALL)
    plane = lax.axis_index("g")
    own = params.shape[0] // 128
    micros, images, rows, width, _ = inputs.shape
    out_rows, out_cols = rows // 2, width // 2
    window_rows = -(-own // 256) * 16
    shift = window_rows * 16 - own
    near = shift * count <= own and window_rows * count % (16 * lax.axis_size("g")) == 0 and lax.axis_size(PLANE) == LANES

    around = [(i, i + 1) for i in range(lax.axis_size(("x", "c")) - 1)]
    x_halo = lax.ppermute(inputs[:, :, -1], ("x", "c"), around).reshape(micros, images * width, D_IN)
    mask = masks.astype(F32)
    mask_halo = lax.ppermute(masks[:, :, -1], ("x", "c"), around).astype(F32)
    x = inputs.reshape(micros, images * rows * width, D_IN)

    if near:
        wall = lax.all_gather(flat_to_window(params, window_rows, shift, index, count), ALL, axis=0, tiled=True)
    else:
        wall = lax.all_gather(params.astype(BF16), ALL, axis=0, tiled=True).reshape(-1, 2048)

    w_in = mask.reshape(micros, -1, 1)
    split = mask.reshape(micros, images, out_rows, 2, out_cols, 2)
    wph = jnp.transpose(split, (0, 3, 5, 1, 2, 4)).reshape(micros, 4, -1, 1)
    whalo = jnp.transpose(mask_halo.reshape(micros, images, out_cols, 2), (0, 3, 1, 2)).reshape(micros, 2, -1, 1)
    total_in = jnp.sum(mask, axis=(1, 2, 3))
    image_pixels = jnp.sum(split[:, :, :, 0, :, 0], axis=(2, 3))
    image_pixels = add_all(image_pixels, ("c", "x"))
    totals = add_all(
        jnp.stack([total_in, jnp.sum(image_pixels, axis=1) / lax.axis_size(("x", "c"))]), ("c", "x", "p", "g")
    )
    total_in, total_out = totals[0], totals[1]
    partner_all, live_all = to_heads(partner), to_heads(live)
    share_index = lax.axis_index(("x", "c"))

    vec = wall[ROW_VEC : ROW_VEC + 16].astype(F32).reshape(-1)
    ranges = norm_ranges()
    gammas = [vec[start : start + n] for start, n in ranges]
    betas = [vec[NORM + start : NORM + start + n] for start, n in ranges]
    bias = vec[2 * NORM : 2 * NORM + OUT]

    h, hh, xe, st = conv_in(x, x_halo, w_in, wph[:, 0], wall[ROW_CIN:ROW_CMID])
    sums = add_all(st)
    mean_in, var_in, scale_in, a_in, b_in = norm_coefs(sums, total_in, gammas[0], betas[0])
    coef_in = pack([a_in, b_in])
    hs, st_side = conv_side(xe, wall[ROW_SIDE:ROW_PROJ])
    cols, hm, st, w_mid = conv_mid(h, hh, coef_in, wph, whalo, wall[ROW_CMID:ROW_COUT])
    sums = add_all(jnp.concatenate([st[:, :2], st_side[:, :2]], axis=2))
    mean_mid, var_mid, scale_mid, a_mid, b_mid = norm_coefs(sums[..., :MID], total_out, gammas[1], betas[1])
    mean_side, var_side, scale_side, a_side, b_side = norm_coefs(sums[..., MID:], total_out, gammas[3], betas[3])
    am, ho, st = conv_out(hm, pack([a_mid, b_mid]), wph, wall[ROW_COUT:ROW_SIDE])
    sums = add_all(st[:, :2])
    mean_out, var_out, scale_out, a_out, b_out = norm_coefs(sums, total_out, gammas[2], betas[2])
    coef_join = pack([a_out, a_side, b_out + b_side])
    pooled = pool(ho, hs, coef_join, wph)
    for axis in ("x", "c"):
        half = pooled.shape[1] // 2
        here = lax.axis_index(axis)
        keep = lax.dynamic_slice_in_dim(pooled, here * half, half, 1)
        send = lax.dynamic_slice_in_dim(pooled, (1 - here) * half, half, 1)
        pooled = keep + swap(send, axis, 1)
    share = pooled.shape[1]
    share_pixels = lax.dynamic_slice_in_dim(image_pixels, share_index * share, share, 1)
    pooled_low = to_heads((pooled / share_pixels[..., None]).astype(BF16))
    slope = slopes(ho, hs, coef_join, wph)

    grad_pool, head_rows, head_vec, block, loss_sum, live_count, head_means, head_vars = heads(
        pooled_low, wall, gammas, betas, bias, partner_all, live_all
    )

    grad_pool = grad_pool.astype(BF16).reshape(lax.axis_size("g"), lax.axis_size("p"), images, OUT)
    grad_pool = lax.dynamic_index_in_dim(grad_pool, lax.axis_index("p"), 1, keepdims=False)
    gs = exchange_planes(grad_pool).astype(F32) / image_pixels[..., None]

    sums = add_all(jnp.sum(gs[:, None] * slope, axis=2))
    bo, co, gamma_out = back_coefs(sums[:, 0], sums[:, 1], mean_out, scale_out, a_out, total_out)
    bs, cs, gamma_side = back_coefs(sums[:, 0], sums[:, 2], mean_side, scale_side, a_side, total_out)
    beta_joined = sums[:, 0]
    coef_back = pack([a_out, a_side, b_out + b_side, bo, co, bs, cs])
    d_mid, st, g_out = back_out(
        ho, hs, gs, coef_back, wph, am, xe, wall[ROW_COUT:ROW_SIDE], hm, pack([a_mid, b_mid])
    )
    sums = add_all(st[:, :2])
    bm, cm, gamma_mid = back_coefs(sums[:, 0], sums[:, 1], mean_mid, scale_mid, a_mid, total_out)
    beta_mid = sums[:, 0]
    d_in, d_halo, st, g_mid = back_mid(
        hm, d_mid, pack([a_mid, bm, cm]), cols, w_mid, h, hh, coef_in, wph, whalo
    )
    sums = add_all(st[:, :2])
    bi, ci, gamma_in = back_coefs(sums[:, 0], sums[:, 1], mean_in, scale_in, a_in, total_in)
    beta_in = sums[:, 0]
    g_in = back_in(h, d_in, d_halo, pack([a_in, bi, ci]), wph, whalo, x, x_halo)

    first_plane = (plane == 0).astype(F32)
    trunk_gamma = [jnp.sum(v, axis=0) * first_plane for v in (gamma_in, gamma_mid, gamma_out, gamma_side)]
    trunk_beta = [jnp.sum(v, axis=0) * first_plane for v in (beta_in, beta_mid, beta_joined, beta_joined)]
    vector = jnp.concatenate(trunk_gamma + head_vec[0] + trunk_beta + head_vec[1] + [head_vec[2]])
    vector = jnp.pad(vector, (0, 16 * 2048 - vector.shape[0])).astype(BF16).reshape(16, 2048)
    vector = lax.dynamic_slice_in_dim(vector, block * 256, 256, 1)
    trunk = jnp.concatenate([g_in, g_mid, g_out], axis=1)

    if near:
        head_part = jnp.concatenate(
            [head_rows, vector, jnp.zeros((window_rows * count - ROW_VEC - 16, 256), BF16)], axis=0
        )
        trunk = lax.psum_scatter(trunk, PLANE, scatter_dimension=0, tiled=False)
        part = jnp.concatenate([trunk, head_part], axis=0)
        part = lax.psum_scatter(part, "g", scatter_dimension=0, tiled=True)
        window = lax.all_to_all(part, PLANE, 0, 1, tiled=True)
        new_params, new_first, new_second, new_copy = adam_from_window(
            window, shift, index, count, params, first, second
        )
    else:
        alone = (lax.axis_index("p") < 2).astype(BF16)
        head_part = jnp.concatenate([head_rows, vector], axis=0) * alone
        head_part = lax.dynamic_update_slice(
            jnp.zeros((head_part.shape[0], 2048), BF16), head_part, (jnp.int32(0), (block * 256).astype(jnp.int32))
        )
        trunk = jnp.transpose(trunk, (1, 0, 2)).reshape(-1, 2048)
        flat = jnp.concatenate([trunk, head_part], axis=0).reshape(-1)
        flat = flat[: params.shape[0] * count]
        grad = lax.psum_scatter(flat, ALL, scatter_dimension=0, tiled=True).astype(F32)
        new_params, new_first, new_second = adam(grad, params, first, second)
        new_copy = new_params.astype(BF16)

    head_stats = jnp.stack([jnp.concatenate(head_means), jnp.concatenate(head_vars)])
    scalars = jnp.stack([loss_sum, live_count])
    head_stats = exchange_planes(jnp.broadcast_to(head_stats[None], (micros,) + head_stats.shape))
    scalars = exchange_planes(jnp.broadcast_to(scalars[None], (micros, 2)))
    averages = jnp.concatenate([mean_in, mean_mid, mean_out, mean_side, head_stats[:, 0]], axis=1)
    spreads = jnp.concatenate([var_in, var_mid, var_out, var_side, head_stats[:, 1]], axis=1)
    stats = jnp.stack([averages, spreads], axis=1)
    new_running = running
    for micro in range(micros):
        new_running = (1.0 - MOMENTUM) * new_running + MOMENTUM * stats[micro]
    return (
        scalars[:, 0],
        scalars[:, 1].astype(jnp.int32),
        new_params,
        new_first,
        new_second,
        new_copy,
        new_running,
    )


def solution(mesh):
    img, rows = mesh.shape["img"], mesh.shape["rows"]
    fine = Mesh(mesh.devices.reshape(MB, img // MB, 2, rows // 2), ALL)
    split = P(ALL)
    placed = (
        P(None, ("g", "p"), ("x", "c"), None, None),
        P(None, ("g", "p"), ("x", "c"), None),
        P(None, ALL),
        P(None, ALL),
        split,
        split,
        split,
        P(),
    )
    return jax.shard_map(
        on_device,
        mesh=fine,
        in_specs=placed,
        out_specs=(P(), P(), split, split, split, split, P()),
        check_vma=False,
    )
```

```python
import jax
import jax.numpy as jnp
from jax import lax
from jax.experimental import pallas as pl
from jax.experimental.pallas import tpu as pltpu
from jax.sharding import Mesh, PartitionSpec as P

D_IN = 1024
MID = 512
OUT = 2048
PRED = 512
MB = 4
STEP = 5
NORM = 11776
PARAMS = 20734976

EPS_NORM = 1e-05
MOMENTUM = 0.1
RATE = 0.03
BETA_ONE = 0.5
BETA_TWO = 0.5
DECAY = 0.01
ADAM_EPS = 1e-08
COS_EPS = 1e-06

ROW_CIN, ROW_CMID, ROW_COUT, ROW_SIDE = 0, 256, 1408, 1920
ROW_PROJ, ROW_PIN, ROW_POUT, ROW_VEC = 2944, 9088, 9600, 10112
LANES = 8
GROUPS, GROUP = 4, 736
GRAD_OUT, GRAD_MID = 1536, 1152
ALL = ("g", "p", "x", "c")
PLANE = ("p", "x", "c")
F32, BF16 = jnp.float32, jnp.bfloat16
COST_SHARE = 8


def params_of(mib=60, steps=1):
    return pltpu.CompilerParams(
        vmem_limit_bytes=mib << 20, dimension_semantics=("arbitrary",) * steps
    )


def cost(flops, moved):
    return pl.CostEstimate(flops=flops // COST_SHARE, bytes_accessed=moved // COST_SHARE, transcendentals=0)


def whole_block(shape):
    zeros = (0,) * len(shape)
    return pl.BlockSpec(shape, lambda *_: zeros)


def sigmoid(v):
    return 1.0 / (1.0 + jnp.exp(-v))


def dot(a, b):
    return jnp.dot(a, b, preferred_element_type=F32)


def dot_nt(a, b):
    return lax.dot_general(a, b, (((1,), (1,)), ((), ())), preferred_element_type=F32)


def dot_tn(a, b):
    return lax.dot_general(a, b, (((0,), (0,)), ((), ())), preferred_element_type=F32)


def fold(v):
    return jnp.sum(v.reshape(-1, 8, v.shape[-1]), axis=0)


def unwide(wide_ref, scratch, out_ref):
    rows = wide_ref.shape[0]
    for part in range(4):
        for col in range(4):
            lanes = pl.ds(part * 512 + col * 128, 128)
            scratch[col, pl.ds(part, rows, stride=4), :] = wide_ref[:, lanes].astype(F32)
    for col in range(4):
        out_ref[:, col * 128 : (col + 1) * 128] = scratch[col].astype(BF16)


def trunk_pieces(start, stop):
    found = []
    for group in range(GROUPS):
        low, high = max(start, group * GROUP), min(stop, (group + 1) * GROUP)
        if low < high:
            found.append((group, low - group * GROUP, low - start, high - low))
    return found


def trunk_specs(start, stop):
    def spec(group):
        return pl.BlockSpec(
            (1, LANES, GROUP, 256), lambda *_: (group, 0, 0, 0), pipeline_mode=pl.Buffered(1)
        )

    return [spec(piece[0]) for piece in trunk_pieces(start, stop)]


def join_trunk(refs, start, stop, out_ref):
    for ref, (_, low, to, rows) in zip(refs, trunk_pieces(start, stop)):
        for block in range(LANES):
            out_ref[to : to + rows, block * 256 : block * 256 + 256] = ref[0, block, low : low + rows, :]


def unwide_trunk(refs, start, stop, scratch, out_ref):
    for ref, (_, low, to, rows) in zip(refs, trunk_pieces(start, stop)):
        for part in range(4):
            for col in range(4):
                block, lanes = 2 * part + col // 2, slice((col % 2) * 128, (col % 2) * 128 + 128)
                scratch[col, pl.ds(part + 4 * to, rows, stride=4), :] = ref[0, block, low : low + rows, lanes].astype(F32)
    for col in range(4):
        out_ref[:, col * 128 : (col + 1) * 128] = scratch[col].astype(BF16)


def window_kernel(off_ref, flat_ref, out_ref):
    off = off_ref[0]
    rows = out_ref.shape[0]
    for col in range(16):
        out_ref[:, col * 128 : (col + 1) * 128] = flat_ref[pl.ds(off + col, rows, stride=16), :].astype(BF16)


def flat_to_window(params, rows, shift, index, count):
    own = params.shape[0] // 128
    head = shift * count
    nxt = lax.ppermute(
        params[: head * 128].astype(BF16), ALL, [(i + 1, i) for i in range(count - 1)]
    )
    flat = jnp.concatenate([params, nxt.astype(F32), jnp.zeros((1024,), F32)]).reshape(-1, 128)
    return pl.pallas_call(
        window_kernel,
        out_shape=jax.ShapeDtypeStruct((rows, 2048), BF16),
        in_specs=[pl.BlockSpec(memory_space=pltpu.SMEM), whole_block((own + head + 8, 128))],
        out_specs=whole_block((rows, 2048)),
        compiler_params=pltpu.CompilerParams(vmem_limit_bytes=40 << 20),
    )((index * shift).astype(jnp.int32)[None], flat)


def adam(grad, params, first, second):
    new_first = BETA_ONE * first + (1.0 - BETA_ONE) * grad
    new_second = BETA_TWO * second + (1.0 - BETA_TWO) * grad * grad
    corrected_first = new_first / (1.0 - BETA_ONE**STEP)
    corrected_second = new_second / (1.0 - BETA_TWO**STEP)
    new_params = params - RATE * (
        corrected_first / (jnp.sqrt(corrected_second) + ADAM_EPS) + DECAY * params
    )
    return new_params, new_first, new_second


def adam_kernel(off_ref, tail_ref, win_ref, p_ref, m_ref, v_ref, po_ref, mo_ref, vo_ref, co_ref, flat):
    step = pl.program_id(0)

    @pl.when(step == 0)
    def _():
        tail = tail_ref.shape[0]
        rows = win_ref.shape[0]
        for col in range(16):
            lanes = pl.ds(col * 128, 128)
            flat[pl.ds(col, tail, stride=16), :] = tail_ref[:, lanes].astype(F32)
            flat[pl.ds(tail * 16 + col, rows, stride=16), :] = win_ref[:, lanes].astype(F32)

    size = p_ref.shape[0]
    grad = flat[pl.ds(off_ref[0] + step * size, size), :]
    po_ref[...], mo_ref[...], vo_ref[...] = adam(grad, p_ref[...], m_ref[...], v_ref[...])
    co_ref[...] = po_ref[...].astype(BF16)


def tail_rows(shift, count):
    return -(-shift * (count - 1) // 256) * 16


def adam_from_window(window, prev, shift, index, params, first, second):
    own = params.shape[0] // 128
    rows, tail = window.shape[0], prev.shape[0]
    block = 512
    steps = -(-own // block)
    assert steps * block <= rows * 16
    off = (tail * 16 - index * shift).astype(jnp.int32)[None]
    spec = pl.BlockSpec((block, 128), lambda i: (i, 0))
    shaped = [v.reshape(own, 128) for v in (params, first, second)]
    outs = pl.pallas_call(
        adam_kernel,
        grid=(steps,),
        out_shape=[jax.ShapeDtypeStruct((own, 128), F32)] * 3 + [jax.ShapeDtypeStruct((own, 128), BF16)],
        in_specs=[pl.BlockSpec(memory_space=pltpu.SMEM), whole_block((tail, 2048)), whole_block((rows, 2048))] + [spec] * 3,
        out_specs=[spec] * 4,
        scratch_shapes=[pltpu.VMEM(((tail + rows) * 16, 128), F32)],
        compiler_params=params_of(40),
    )(off, prev, window, *shaped)
    return [v.reshape(-1) for v in outs]


def conv_in_kernel(x_ref, w_ref, w2_ref, wide_ref, h_ref, xe_ref, st_ref, wb, wf, hs, xs):
    micro, part = pl.program_id(0), pl.program_id(1)

    @pl.when((micro == 0) & (part == 0))
    def _():
        unwide(wide_ref, wf, wb)

    images = x_ref.shape[1] // 64
    h = dot(x_ref[0], wb[...])
    for col in range(4):
        hs[col] = h[:, col * 128 : (col + 1) * 128]

    def body(i, carry):
        at = pl.multiple_of(i * 64, 64)
        low = pl.multiple_of(i * 16, 16)
        w = jnp.broadcast_to(w_ref[0, pl.ds(at, 64), :], (64, 128))
        new = []
        for col in range(4):
            lanes = slice(col * 128, (col + 1) * 128)
            h = hs[col, pl.ds(at, 64), :] * w
            new.append((carry[col][0] + fold(h), carry[col][1] + fold(h * h)))
            hs[col, pl.ds(at, 64), :] = h
            for side in range(2):
                half = hs[col, pl.ds(at + side, 32, stride=2), :].reshape(2, 2, 8, 128)
                for row in range(2):
                    h_ref[0, 2 * row + side, pl.ds(low, 16), lanes] = half[:, row].reshape(16, 128)
        w = jnp.broadcast_to(w2_ref[0, pl.ds(low, 16), :], (16, 128))
        for col in range(8):
            lanes = slice(col * 128, (col + 1) * 128)
            for row in range(2):
                xs[col, row * 16 : row * 16 + 16, :] = x_ref[0, pl.ds(at + row * 32, 16), lanes].astype(F32)
            xe_ref[0, pl.ds(low, 16), lanes] = (xs[col, pl.ds(0, 16, stride=2), :] * w).astype(BF16)
        return tuple(new)

    zero = jnp.zeros((8, 128), F32)
    found = lax.fori_loop(0, images, body, ((zero, zero),) * 4)

    @pl.when(part == 0)
    def _():
        st_ref[...] = jnp.zeros_like(st_ref)

    for col in range(4):
        lanes = slice(col * 128, (col + 1) * 128)
        for k in range(2):
            st_ref[0, k : k + 1, lanes] += jnp.sum(found[col][k], axis=0, keepdims=True)


def conv_in(x, w, w2, wide):
    micros, pixels, _ = x.shape
    images = pixels // 64
    parts = 2
    b = images // parts
    return pl.pallas_call(
        conv_in_kernel,
        grid=(micros, parts),
        out_shape=[
            jax.ShapeDtypeStruct((micros, 4, images * 16, MID), F32),
            jax.ShapeDtypeStruct((micros, images * 16, D_IN), BF16),
            jax.ShapeDtypeStruct((micros, 8, MID), F32),
            jax.ShapeDtypeStruct((D_IN, MID), BF16),
        ],
        in_specs=[
            pl.BlockSpec((1, b * 64, D_IN), lambda m, k: (m, k, 0)),
            pl.BlockSpec((1, b * 64, 1), lambda m, k: (m, k, 0)),
            pl.BlockSpec((1, b * 16, 1), lambda m, k: (m, k, 0)),
            whole_block((256, 2048)),
        ],
        out_specs=[
            pl.BlockSpec((1, 4, b * 16, MID), lambda m, k: (m, 0, k, 0)),
            pl.BlockSpec((1, b * 16, D_IN), lambda m, k: (m, k, 0)),
            pl.BlockSpec((1, 8, MID), lambda m, k: (m, 0, 0)),
            whole_block((D_IN, MID)),
        ],
        scratch_shapes=[
            pltpu.VMEM((4, D_IN, 128), F32),
            pltpu.VMEM((4, b * 64, 128), F32),
            pltpu.VMEM((8, 32, 128), F32),
        ],
        compiler_params=params_of(56, 2),
        cost_estimate=cost(2 * micros * images * 64 * D_IN * MID, 40 << 20),
    )(x, w, w2, wide)


def halo_kernel(xh_ref, wb_ref, hh_ref, hs):
    h = dot(xh_ref[0], wb_ref[...])
    rows = hh_ref.shape[2]
    for col in range(4):
        lanes = slice(col * 128, (col + 1) * 128)
        hs[col] = h[:, lanes]
        for side in range(2):
            hh_ref[0, side, :, lanes] = hs[col, pl.ds(side, rows, stride=2), :]


def conv_in_halo(xh, weight):
    micros, pixels, _ = xh.shape
    return pl.pallas_call(
        halo_kernel,
        grid=(micros,),
        out_shape=jax.ShapeDtypeStruct((micros, 2, pixels // 2, MID), F32),
        in_specs=[pl.BlockSpec((1, pixels, D_IN), lambda m: (m, 0, 0)), whole_block((D_IN, MID))],
        out_specs=pl.BlockSpec((1, 2, pixels // 2, MID), lambda m: (m, 0, 0, 0)),
        scratch_shapes=[pltpu.VMEM((4, pixels, 128), F32)],
        compiler_params=params_of(40),
        cost_estimate=cost(2 * micros * pixels * D_IN * MID, 9 << 20),
    )(xh, weight)


def side_kernel(xe_ref, *refs):
    pieces, (hs_ref, st_ref, weight) = refs[:-3], refs[-3:]

    @pl.when((pl.program_id(0) == 0) & (pl.program_id(1) == 0))
    def _():
        join_trunk(pieces, ROW_SIDE, ROW_PROJ, weight)

    n = hs_ref.shape[2]
    h = dot(xe_ref[0], weight[:, pl.ds(pl.multiple_of(pl.program_id(1) * n, n), n)])
    hs_ref[0] = h
    st_ref[...] = jnp.zeros_like(st_ref)
    st_ref[0, 0:1, :] = jnp.sum(h, axis=0, keepdims=True)
    st_ref[0, 1:2, :] = jnp.sum(h * h, axis=0, keepdims=True)


def conv_side(xe, trunk):
    micros, rows, _ = xe.shape
    cols = 4
    n = OUT // cols
    return pl.pallas_call(
        side_kernel,
        grid=(micros, cols),
        out_shape=[
            jax.ShapeDtypeStruct((micros, rows, OUT), F32),
            jax.ShapeDtypeStruct((micros, 8, OUT), F32),
        ],
        in_specs=[
            pl.BlockSpec((1, rows, D_IN), lambda m, k: (m, 0, 0)),
        ]
        + trunk_specs(ROW_SIDE, ROW_PROJ),
        out_specs=[
            pl.BlockSpec((1, rows, n), lambda m, k: (m, 0, k)),
            pl.BlockSpec((1, 8, n), lambda m, k: (m, 0, k)),
        ],
        scratch_shapes=[pltpu.VMEM((D_IN, OUT), BF16)],
        compiler_params=params_of(56, 2),
        cost_estimate=cost(2 * micros * rows * D_IN * OUT, 16 << 20),
    )(xe, *[trunk] * len(trunk_pieces(ROW_SIDE, ROW_PROJ)))


def shift_right(v):
    moved = pltpu.roll(v, 1, 1)
    return jnp.where(lax.broadcasted_iota(jnp.int32, v.shape, 1) == 0, 0.0, moved)


def shift_left(v):
    moved = pltpu.roll(v, 7, 1)
    return jnp.where(lax.broadcasted_iota(jnp.int32, v.shape, 1) == 7, 0.0, moved)


def conv_mid_kernel(h_ref, hh_ref, cf_ref, w_ref, wh_ref, *refs):
    pieces, (cols_ref, hm_ref, st_ref, wb, wf) = refs[:-5], refs[-5:]
    micro = pl.program_id(0)

    @pl.when(micro == 0)
    def _():
        unwide_trunk(pieces, ROW_CMID, ROW_COUT, wf, wb)

    images = h_ref.shape[2] // 16
    scale, shift = cf_ref[0, 0:1, :], cf_ref[0, 1:2, :]

    def act(h, w):
        v = h * scale + shift
        return v * sigmoid(v) * w

    def body(i, carry):
        at = pl.ds(pl.multiple_of(i * 16, 16), 16)
        half = pl.ds(pl.multiple_of(i * 8, 8), 8)
        a = [act(h_ref[0, k, at, :], w_ref[0, k, at, :]).reshape(2, 8, MID) for k in range(4)]
        above = [act(hh_ref[0, k, half, :], wh_ref[0, k, half, :]).reshape(1, 8, MID) for k in range(2)]
        a1s, a3s = shift_right(a[1]), shift_right(a[3])
        up2 = jnp.concatenate([above[0], a[2][:1]], axis=0)
        up3 = jnp.concatenate([above[1], a[3][:1]], axis=0)
        up3s = jnp.concatenate([shift_right(above[1]), a3s[:1]], axis=0)
        for tap, value in enumerate([up3s, up2, up3, a1s, a[0], a[1], a3s, a[2], a[3]]):
            cols_ref[0, at, tap * MID : (tap + 1) * MID] = value.reshape(16, MID).astype(BF16)
        return carry

    lax.fori_loop(0, images, body, 0)
    h = dot(cols_ref[0], wb[...])
    hm_ref[0] = h
    hw = h * w_ref[0, 0]
    st_ref[...] = jnp.zeros_like(st_ref)
    st_ref[0, 0:1, :] = jnp.sum(hw, axis=0, keepdims=True)
    st_ref[0, 1:2, :] = jnp.sum(hw * hw, axis=0, keepdims=True)


def conv_mid(h, hh, coef, wph, whalo, trunk):
    micros, _, rows, _ = h.shape
    return pl.pallas_call(
        conv_mid_kernel,
        grid=(micros,),
        out_shape=[
            jax.ShapeDtypeStruct((micros, rows, 9 * MID), BF16),
            jax.ShapeDtypeStruct((micros, rows, MID), F32),
            jax.ShapeDtypeStruct((micros, 8, MID), F32),
            jax.ShapeDtypeStruct((9 * MID, MID), BF16),
        ],
        in_specs=[
            pl.BlockSpec((1, 4, rows, MID), lambda m: (m, 0, 0, 0)),
            pl.BlockSpec((1, 2, rows // 2, MID), lambda m: (m, 0, 0, 0)),
            pl.BlockSpec((1, 8, MID), lambda m: (m, 0, 0)),
            pl.BlockSpec((1, 4, rows, 1), lambda m: (m, 0, 0, 0)),
            pl.BlockSpec((1, 2, rows // 2, 1), lambda m: (m, 0, 0, 0)),
        ]
        + trunk_specs(ROW_CMID, ROW_COUT),
        out_specs=[
            pl.BlockSpec((1, rows, 9 * MID), lambda m: (m, 0, 0)),
            pl.BlockSpec((1, rows, MID), lambda m: (m, 0, 0)),
            pl.BlockSpec((1, 8, MID), lambda m: (m, 0, 0)),
            pl.BlockSpec((9 * MID, MID), lambda m: (0, 0), pipeline_mode=pl.Buffered(1)),
        ],
        scratch_shapes=[pltpu.VMEM((4, 9 * MID, 128), F32)],
        compiler_params=params_of(60),
        cost_estimate=cost(2 * micros * rows * 9 * MID * MID, 50 << 20),
    )(h, hh, coef, wph, whalo, *[trunk] * len(trunk_pieces(ROW_CMID, ROW_COUT)))


def conv_out_kernel(hm_ref, cf_ref, w_ref, *refs):
    pieces, (am_ref, ho_ref, st_ref, weight_ref) = refs[:-4], refs[-4:]

    @pl.when(pl.program_id(0) == 0)
    def _():
        join_trunk(pieces, ROW_COUT, ROW_SIDE, weight_ref)

    v = hm_ref[0] * cf_ref[0, 0:1, :] + cf_ref[0, 1:2, :]
    am = (v * sigmoid(v) * w_ref[0, 0]).astype(BF16)
    am_ref[0] = am
    st_ref[...] = jnp.zeros_like(st_ref)
    for k in range(4):
        lanes = slice(k * 512, (k + 1) * 512)
        h = dot(am, weight_ref[:, lanes])
        ho_ref[0, :, lanes] = h
        st_ref[0, 0:1, lanes] = jnp.sum(h, axis=0, keepdims=True)
        st_ref[0, 1:2, lanes] = jnp.sum(h * h, axis=0, keepdims=True)


def conv_out(hm, coef, wph, trunk):
    micros, rows, _ = hm.shape
    return pl.pallas_call(
        conv_out_kernel,
        grid=(micros,),
        out_shape=[
            jax.ShapeDtypeStruct((micros, rows, MID), BF16),
            jax.ShapeDtypeStruct((micros, rows, OUT), F32),
            jax.ShapeDtypeStruct((micros, 8, OUT), F32),
            jax.ShapeDtypeStruct((MID, OUT), BF16),
        ],
        in_specs=[
            pl.BlockSpec((1, rows, MID), lambda m: (m, 0, 0)),
            pl.BlockSpec((1, 8, MID), lambda m: (m, 0, 0)),
            pl.BlockSpec((1, 1, rows, 1), lambda m: (m, 0, 0, 0)),
        ]
        + trunk_specs(ROW_COUT, ROW_SIDE),
        out_specs=[
            pl.BlockSpec((1, rows, MID), lambda m: (m, 0, 0)),
            pl.BlockSpec((1, rows, OUT), lambda m: (m, 0, 0)),
            pl.BlockSpec((1, 8, OUT), lambda m: (m, 0, 0)),
            pl.BlockSpec((MID, OUT), lambda m: (0, 0), pipeline_mode=pl.Buffered(1)),
        ],
        compiler_params=params_of(56),
        cost_estimate=cost(2 * micros * rows * MID * OUT, 18 << 20),
    )(hm, coef, wph, *[trunk] * len(trunk_pieces(ROW_COUT, ROW_SIDE)))


def pool_kernel(ho_ref, hs_ref, cf_ref, w_ref, out_ref):
    images = out_ref.shape[1]
    so, ss, shift = cf_ref[0, 0:1, :], cf_ref[0, 1:2, :], cf_ref[0, 2:3, :]

    def body(i, carry):
        total = []
        for k in range(8):
            at = pl.ds(pl.multiple_of(i * 128 + k * 16, 16), 16)
            j = ho_ref[0, at, :] * so + hs_ref[0, at, :] * ss + shift
            r = j * sigmoid(j) * w_ref[0, 0, at, :]
            total.append(jnp.sum(r, axis=0, keepdims=True))
        out_ref[0, pl.ds(pl.multiple_of(i * 8, 8), 8), :] = jnp.concatenate(total, axis=0)
        return carry

    lax.fori_loop(0, images // 8, body, 0)


def pool(ho, hs, coef, wph):
    micros, rows, _ = ho.shape
    n = 512
    images = rows // 16
    return pl.pallas_call(
        pool_kernel,
        grid=(micros, OUT // n),
        out_shape=jax.ShapeDtypeStruct((micros, images, OUT), F32),
        in_specs=[
            pl.BlockSpec((1, rows, n), lambda m, k: (m, 0, k)),
            pl.BlockSpec((1, rows, n), lambda m, k: (m, 0, k)),
            pl.BlockSpec((1, 8, n), lambda m, k: (m, 0, k)),
            pl.BlockSpec((1, 1, rows, 1), lambda m, k: (m, 0, 0, 0)),
        ],
        out_specs=pl.BlockSpec((1, images, n), lambda m, k: (m, 0, k)),
        compiler_params=params_of(56, 2),
        cost_estimate=cost(20 * micros * rows * OUT, 18 << 20),
    )(ho, hs, coef, wph)


def slope_kernel(ho_ref, hs_ref, cf_ref, w_ref, out_ref):
    images = out_ref.shape[2]
    so, ss, shift = cf_ref[0, 0:1, :], cf_ref[0, 1:2, :], cf_ref[0, 2:3, :]

    def body(i, carry):
        plain, out, side = [], [], []
        for k in range(8):
            at = pl.ds(pl.multiple_of(i * 128 + k * 16, 16), 16)
            ho, hs = ho_ref[0, at, :], hs_ref[0, at, :]
            j = ho * so + hs * ss + shift
            s = sigmoid(j)
            d = s * (1.0 + j * (1.0 - s)) * w_ref[0, 0, at, :]
            plain.append(jnp.sum(d, axis=0, keepdims=True))
            out.append(jnp.sum(d * ho, axis=0, keepdims=True))
            side.append(jnp.sum(d * hs, axis=0, keepdims=True))
        at = pl.ds(pl.multiple_of(i * 8, 8), 8)
        for k, value in enumerate((plain, out, side)):
            out_ref[0, k, at, :] = jnp.concatenate(value, axis=0)
        return carry

    lax.fori_loop(0, images // 8, body, 0)


def slopes(ho, hs, coef, wph):
    micros, rows, _ = ho.shape
    n = 512
    images = rows // 16
    return pl.pallas_call(
        slope_kernel,
        grid=(micros, OUT // n),
        out_shape=jax.ShapeDtypeStruct((micros, 3, images, OUT), F32),
        in_specs=[
            pl.BlockSpec((1, rows, n), lambda m, k: (m, 0, k)),
            pl.BlockSpec((1, rows, n), lambda m, k: (m, 0, k)),
            pl.BlockSpec((1, 8, n), lambda m, k: (m, 0, k)),
            pl.BlockSpec((1, 1, rows, 1), lambda m, k: (m, 0, 0, 0)),
        ],
        out_specs=pl.BlockSpec((1, 3, images, n), lambda m, k: (m, 0, 0, k)),
        compiler_params=params_of(56, 2),
        cost_estimate=cost(30 * micros * rows * OUT, 20 << 20),
    )(ho, hs, coef, wph)


def back_out_kernel(
    ho_ref, hs_ref, gs_ref, cf_ref, w_ref, am_ref, xe_ref, wo_ref, hm_ref, cm_ref,
    d_ref, st_ref, gw_ref, amt, xet, da, dho, dhs, acc_out, acc_side,
):
    micro, part = pl.program_id(0), pl.program_id(1)
    parts = pl.num_programs(1)
    images = gs_ref.shape[1]

    @pl.when(part == 0)
    def _():
        amt[...] = am_ref[0].T
        xet[...] = xe_ref[0].T

    cf = [cf_ref[0, k : k + 1, :] for k in range(7)]

    def body(i, carry):
        gs = gs_ref[0, pl.ds(pl.multiple_of(i * 8, 8), 8), :]
        for k in range(8):
            at = pl.ds(pl.multiple_of(i * 128 + k * 16, 16), 16)
            ho, hs = ho_ref[0, at, :], hs_ref[0, at, :]
            w = w_ref[0, 0, at, :]
            j = ho * cf[0] + hs * cf[1] + cf[2]
            s = sigmoid(j)
            g = s * (1.0 + j * (1.0 - s)) * gs[k : k + 1, :]
            dho[at, :] = ((g * cf[0] + cf[3] + ho * cf[4]) * w).astype(BF16)
            dhs[at, :] = ((g * cf[1] + cf[5] + hs * cf[6]) * w).astype(BF16)
        return carry

    lax.fori_loop(0, images // 8, body, 0)
    g_out = dot(amt[...], dho[...])
    g_side = dot(xet[...], dhs[...])
    back = dot_nt(dho[...], wo_ref[...])

    @pl.when(micro == 0)
    def _():
        acc_out[part] = g_out
        acc_side[part] = g_side

    @pl.when(micro > 0)
    def _():
        acc_out[part] += g_out
        acc_side[part] += g_side

    @pl.when(part == 0)
    def _():
        da[...] = back

    @pl.when(part > 0)
    def _():
        da[...] += back

    @pl.when(part == parts - 1)
    def _():
        hm = hm_ref[0]
        v = hm * cm_ref[0, 0:1, :] + cm_ref[0, 1:2, :]
        s = sigmoid(v)
        d = s * (1.0 + v * (1.0 - s)) * da[...] * w_ref[0, 0]
        d_ref[0] = d
        st_ref[...] = jnp.zeros_like(st_ref)
        st_ref[0, 0:1, :] = jnp.sum(d, axis=0, keepdims=True)
        st_ref[0, 1:2, :] = jnp.sum(d * hm, axis=0, keepdims=True)

    @pl.when((micro == pl.num_programs(0) - 1) & (part == parts - 1))
    def _():
        for k in range(4):
            for half in range(2):
                lanes = slice(half * 256, half * 256 + 256)
                gw_ref[2 * k + half, 0:MID, :] = acc_out[k, :, lanes].astype(BF16)
                gw_ref[2 * k + half, MID:, :] = acc_side[k, :, lanes].astype(BF16)


def back_out(ho, hs, gs, coef, wph, am, xe, weight, hm, coef_mid):
    micros, rows, _ = ho.shape
    n = 512
    images = rows // 16
    return pl.pallas_call(
        back_out_kernel,
        grid=(micros, OUT // n),
        out_shape=[
            jax.ShapeDtypeStruct((micros, rows, MID), F32),
            jax.ShapeDtypeStruct((micros, 8, MID), F32),
            jax.ShapeDtypeStruct((LANES, GRAD_OUT, 256), BF16),
        ],
        in_specs=[
            pl.BlockSpec((1, rows, n), lambda m, k: (m, 0, k)),
            pl.BlockSpec((1, rows, n), lambda m, k: (m, 0, k)),
            pl.BlockSpec((1, images, n), lambda m, k: (m, 0, k)),
            pl.BlockSpec((1, 8, n), lambda m, k: (m, 0, k)),
            pl.BlockSpec((1, 1, rows, 1), lambda m, k: (m, 0, 0, 0)),
            pl.BlockSpec((1, rows, MID), lambda m, k: (m, 0, 0)),
            pl.BlockSpec((1, rows, D_IN), lambda m, k: (m, 0, 0)),
            pl.BlockSpec((MID, n), lambda m, k: (0, k)),
            pl.BlockSpec((1, rows, MID), lambda m, k: (m, 0, 0)),
            pl.BlockSpec((1, 8, MID), lambda m, k: (m, 0, 0)),
        ],
        out_specs=[
            pl.BlockSpec((1, rows, MID), lambda m, k: (m, 0, 0)),
            pl.BlockSpec((1, 8, MID), lambda m, k: (m, 0, 0)),
            whole_block((LANES, GRAD_OUT, 256)),
        ],
        scratch_shapes=[
            pltpu.VMEM((MID, rows), BF16),
            pltpu.VMEM((D_IN, rows), BF16),
            pltpu.VMEM((rows, MID), F32),
            pltpu.VMEM((rows, n), BF16),
            pltpu.VMEM((rows, n), BF16),
            pltpu.VMEM((OUT // n, MID, n), F32),
            pltpu.VMEM((OUT // n, D_IN, n), F32),
        ],
        compiler_params=params_of(60, 2),
        cost_estimate=cost(2 * micros * rows * OUT * (2 * MID + D_IN), 40 << 20),
    )(ho, hs, gs, coef, wph, am, xe, weight, hm, coef_mid)


def back_mid_kernel(
    hm_ref, d_ref, cm_ref, cols_ref, wb, h_ref, hh_ref, cf_ref, w_ref, wh_ref,
    din_ref, dh_ref, st_ref, gw_ref, dt, acc,
):
    micro = pl.program_id(0)
    images = h_ref.shape[2] // 16

    low = ((d_ref[0] * cm_ref[0, 0:1, :] + cm_ref[0, 1:2, :] + hm_ref[0] * cm_ref[0, 2:3, :]) * w_ref[0, 0]).astype(BF16)
    for tap in range(9):
        lanes = slice(tap * MID, (tap + 1) * MID)
        g = dot_tn(cols_ref[0, :, lanes], low)

        @pl.when(micro == 0)
        def _():
            for col in range(4):
                acc[col, lanes, :] = g[:, col * 128 : (col + 1) * 128]

        @pl.when(micro > 0)
        def _():
            for col in range(4):
                acc[col, lanes, :] += g[:, col * 128 : (col + 1) * 128]

    scale, shift = cf_ref[0, 0:1, :], cf_ref[0, 1:2, :]
    zero = jnp.zeros((8, MID), F32)

    def back(h, grad, w):
        v = h * scale + shift
        s = sigmoid(v)
        return s * (1.0 + v * (1.0 - s)) * grad * w

    def body(i, carry):
        total, product = carry
        at = pl.ds(pl.multiple_of(i * 16, 16), 16)
        half = pl.ds(pl.multiple_of(i * 8, 8), 8)
        near = pl.ds(pl.multiple_of((i % (images // 2)) * 16, 16), 16)
        t = [dt[k, near, :].reshape(2, 8, MID) for k in range(9)]
        below1 = t[1]
        below3 = t[2] + shift_left(t[0])
        last = jnp.zeros((1, 8, MID), F32)
        grads = [
            t[4],
            t[5] + shift_left(t[3]),
            t[7] + jnp.concatenate([below1[1:], last], axis=0),
            t[8] + shift_left(t[6]) + jnp.concatenate([below3[1:], last], axis=0),
        ]
        for k in range(4):
            h = h_ref[0, k, at, :]
            d = back(h, grads[k].reshape(16, MID), w_ref[0, k, at, :])
            din_ref[0, k, at, :] = d.astype(BF16)
            total = total + fold(d)
            product = product + fold(d * h)
        for k, grad in enumerate((below1, below3)):
            h = hh_ref[0, k, half, :]
            d = back(h, grad[0], wh_ref[0, k, half, :])
            dh_ref[0, k, half, :] = d
            total = total + d
            product = product + d * h
        return total, product

    found = (zero, zero)
    for part in range(2):
        start, stop = part * images // 2, (part + 1) * images // 2
        for tap in range(9):
            dt[tap] = dot_nt(low[start * 16 : stop * 16], wb[tap * MID : (tap + 1) * MID, :])
        found = lax.fori_loop(start, stop, body, found)
    total, product = found
    st_ref[...] = jnp.zeros_like(st_ref)
    st_ref[0, 0:1, :] = jnp.sum(total, axis=0, keepdims=True)
    st_ref[0, 1:2, :] = jnp.sum(product, axis=0, keepdims=True)

    @pl.when(micro == pl.num_programs(0) - 1)
    def _():
        for k in range(LANES):
            for half in range(2):
                found = acc[(k % 2) * 2 + half, pl.ds(k // 2, GRAD_MID, stride=4), :]
                gw_ref[k, :, half * 128 : half * 128 + 128] = found.astype(BF16)


def back_mid(hm, d, coef_mid, cols, weight, h, hh, coef, wph, whalo):
    micros, _, rows, _ = h.shape
    return pl.pallas_call(
        back_mid_kernel,
        grid=(micros,),
        out_shape=[
            jax.ShapeDtypeStruct((micros, 4, rows, MID), BF16),
            jax.ShapeDtypeStruct((micros, 2, rows // 2, MID), F32),
            jax.ShapeDtypeStruct((micros, 8, MID), F32),
            jax.ShapeDtypeStruct((LANES, GRAD_MID, 256), BF16),
        ],
        in_specs=[
            pl.BlockSpec((1, rows, MID), lambda m: (m, 0, 0)),
            pl.BlockSpec((1, rows, MID), lambda m: (m, 0, 0)),
            pl.BlockSpec((1, 8, MID), lambda m: (m, 0, 0)),
            pl.BlockSpec((1, rows, 9 * MID), lambda m: (m, 0, 0)),
            pl.BlockSpec((9 * MID, MID), lambda m: (0, 0), pipeline_mode=pl.Buffered(1)),
            pl.BlockSpec((1, 4, rows, MID), lambda m: (m, 0, 0, 0)),
            pl.BlockSpec((1, 2, rows // 2, MID), lambda m: (m, 0, 0, 0)),
            pl.BlockSpec((1, 8, MID), lambda m: (m, 0, 0)),
            pl.BlockSpec((1, 4, rows, 1), lambda m: (m, 0, 0, 0)),
            pl.BlockSpec((1, 2, rows // 2, 1), lambda m: (m, 0, 0, 0)),
        ],
        out_specs=[
            pl.BlockSpec((1, 4, rows, MID), lambda m: (m, 0, 0, 0)),
            pl.BlockSpec((1, 2, rows // 2, MID), lambda m: (m, 0, 0, 0)),
            pl.BlockSpec((1, 8, MID), lambda m: (m, 0, 0)),
            pl.BlockSpec((LANES, GRAD_MID, 256), lambda m: (0, 0, 0), pipeline_mode=pl.Buffered(1)),
        ],
        scratch_shapes=[
            pltpu.VMEM((9, rows // 2, MID), F32),
            pltpu.VMEM((4, 9 * MID, 128), F32),
        ],
        compiler_params=params_of(62),
        cost_estimate=cost(4 * micros * rows * 9 * MID * MID, 60 << 20),
    )(hm, d, coef_mid, cols, weight, h, hh, coef, wph, whalo)


def back_in_kernel(h_ref, din_ref, dh_ref, cf_ref, w_ref, wh_ref, x_ref, xh_ref, gw_ref, ds, acc, turned):
    micro, part = pl.program_id(0), pl.program_id(1)
    images = h_ref.shape[2] // 16
    ca, cb, cc = cf_ref[0, 0:1, :], cf_ref[0, 1:2, :], cf_ref[0, 2:3, :]

    def body(i, carry):
        at = pl.ds(pl.multiple_of(i * 16, 16), 16)
        half = pl.ds(pl.multiple_of(i * 8, 8), 8)
        for k in range(4):
            h = h_ref[0, k, at, :]
            d = (din_ref[0, k, at, :].astype(F32) * ca + cb + h * cc) * w_ref[0, k, at, :]
            row, side = k // 2, k % 2
            for o in range(2):
                for col in range(4):
                    to = pl.ds(i * 64 + (2 * o + row) * 16 + side, 8, stride=2)
                    ds[col, to, :] = d[o * 8 : o * 8 + 8, col * 128 : (col + 1) * 128]
        for side in range(2):
            d = dh_ref[0, side, half, :] * ca
            for col in range(4):
                ds[col, pl.ds(images * 64 + i * 16 + side, 8, stride=2), :] = d[:, col * 128 : (col + 1) * 128]
        return carry

    lax.fori_loop(0, images, body, 0)
    low = jnp.concatenate([ds[col].astype(BF16) for col in range(4)], axis=1)
    g = dot_tn(low[: images * 64], x_ref[0]) + dot_tn(low[images * 64 :], xh_ref[0])

    @pl.when((micro == 0) & (part == 0))
    def _():
        acc[...] = g

    @pl.when((micro > 0) | (part > 0))
    def _():
        acc[...] += g

    @pl.when((micro == pl.num_programs(0) - 1) & (part == pl.num_programs(1) - 1))
    def _():
        for col in range(4):
            turned[col] = acc[col * 128 : (col + 1) * 128, :].T
        for k in range(LANES):
            for half in range(2):
                found = turned[(k % 2) * 2 + half, pl.ds(k // 2, D_IN // 4, stride=4), :]
                gw_ref[k, :, half * 128 : half * 128 + 128] = found.astype(BF16)


def back_in(h, din, dhalo, coef, wph, whalo, x, xh):
    micros, _, rows, _ = h.shape
    parts = 2
    r = rows // parts
    return pl.pallas_call(
        back_in_kernel,
        grid=(micros, parts),
        out_shape=jax.ShapeDtypeStruct((LANES, 256, 256), BF16),
        in_specs=[
            pl.BlockSpec((1, 4, r, MID), lambda m, k: (m, 0, k, 0)),
            pl.BlockSpec((1, 4, r, MID), lambda m, k: (m, 0, k, 0)),
            pl.BlockSpec((1, 2, r // 2, MID), lambda m, k: (m, 0, k, 0)),
            pl.BlockSpec((1, 8, MID), lambda m, k: (m, 0, 0)),
            pl.BlockSpec((1, 4, r, 1), lambda m, k: (m, 0, k, 0)),
            pl.BlockSpec((1, 2, r // 2, 1), lambda m, k: (m, 0, k, 0)),
            pl.BlockSpec((1, r * 4, D_IN), lambda m, k: (m, k, 0)),
            pl.BlockSpec((1, r, D_IN), lambda m, k: (m, k, 0)),
        ],
        out_specs=whole_block((LANES, 256, 256)),
        scratch_shapes=[
            pltpu.VMEM((4, r * 5, 128), F32),
            pltpu.VMEM((MID, D_IN), F32),
            pltpu.VMEM((4, D_IN, 128), F32),
        ],
        compiler_params=params_of(60, 2),
        cost_estimate=cost(2 * micros * rows * 5 * D_IN * MID, 50 << 20),
    )(h, din, dhalo, coef, wph, whalo, x, xh)


def swap(value, axis, bit):
    size = lax.axis_size(axis)
    return lax.ppermute(value, axis, [(i, i ^ bit) for i in range(size)])


def bits_of(axis):
    size, bit, found = lax.axis_size(axis), 1, []
    while bit < size:
        found.append(bit)
        bit *= 2
    return found


def add_all(value, axes=("c", "x", "p", "g")):
    for axis in axes:
        for bit in bits_of(axis):
            value = value + swap(value, axis, bit)
    return value


def exchange_planes(value):
    planes = lax.axis_size("g")
    here = lax.axis_index("g")
    own = lax.dynamic_index_in_dim(value, here, 0, keepdims=True)
    result = lax.dynamic_update_slice_in_dim(jnp.zeros_like(value), own, here, 0)
    for step in range(1, planes):
        block = lax.dynamic_index_in_dim(value, (here + step) % planes, 0, keepdims=True)
        got = lax.ppermute(block, "g", [(i, (i + step) % planes) for i in range(planes)])
        result = lax.dynamic_update_slice_in_dim(result, got, (here + planes - step) % planes, 0)
    return result


def gather_axis(value, axis):
    value = value[None]
    for bit in bits_of(axis):
        other = swap(value, axis, bit)
        mine = (lax.axis_index(axis) // bit) % 2
        value = jnp.where(mine == 0, jnp.concatenate([value, other]), jnp.concatenate([other, value]))
    return value


def to_heads(value):
    routed = exchange_planes(value)
    for axis in ("p", "x", "c"):
        routed = gather_axis(routed, axis)
    order = (3, 2, 1, 0, 4) + tuple(range(5, routed.ndim))
    routed = jnp.transpose(routed, order)
    return routed.reshape((-1,) + value.shape[2:])


def halve(value, axis, dim):
    own = lax.axis_index(axis)
    keep = lax.dynamic_index_in_dim(value, own, dim, keepdims=False)
    send = lax.dynamic_index_in_dim(value, 1 - own, dim, keepdims=False)
    return keep + swap(send, axis, 1)


def plane_reduce(value):
    half = value.shape[1] // 2
    value = halve(value.reshape((2, 2, 2) + value.shape[1:]), "c", 2)
    a = halve(halve(value[:, :, :half], "x", 1), "p", 0)
    b = halve(halve(value[:, :, half:], "p", 0), "x", 0)
    return jnp.concatenate([a, b], axis=0)


def to_first_plane(value):
    planes = lax.axis_size("g")
    step = 1
    while step < planes:
        value = value + lax.ppermute(value, "g", [(i + step, i) for i in range(0, planes - step, 2 * step)])
        step *= 2
    return value


def spread_trunk(block, plane, plane_rows):
    planes = lax.axis_size("g")
    result = None
    for target in range(planes):
        parts = []
        for source in range(planes):
            low = max(target * GROUP, source * plane_rows)
            high = min((target + 1) * GROUP, (source + 1) * plane_rows)
            if low < high:
                piece = block[low - source * plane_rows : high - source * plane_rows]
                parts.append(piece if source == target else lax.ppermute(piece, "g", [(source, target)]))
        whole = parts[0] if len(parts) == 1 else jnp.concatenate(parts, axis=0)
        result = whole if result is None else jnp.where(plane == target, whole, result)
    return result


def first_rows_everywhere(block, plane, plane_rows):
    last = lax.axis_size("g") - 1
    at = ROW_VEC - last * plane_rows
    send = jnp.concatenate([block[:ROW_CMID], block[at : at + 16]], axis=0)
    first, vec = send[:ROW_CMID], send[ROW_CMID:]
    for target in range(1, last + 1):
        pairs = [(0, target), (last, last - target)]
        got = lax.ppermute(send, "g", pairs)
        first = jnp.where(plane == target, got[:ROW_CMID], first)
        vec = jnp.where(plane == last - target, got[ROW_CMID:], vec)
    rows = jnp.concatenate([first, vec], axis=0)
    for axis in PLANE:
        rows = gather_axis(rows, axis)
    rows = jnp.transpose(rows, (3, 2, 1, 0, 4)).reshape(-1, 2048)
    return rows[:ROW_CMID], rows[ROW_CMID:]


def norm_ranges():
    widths = [MID, MID, OUT, OUT, OUT, OUT, OUT, PRED]
    return [(sum(widths[:layer]), widths[layer]) for layer in range(8)]


def silu_back(value, grad):
    gate = jax.nn.sigmoid(value)
    return grad * gate * (1.0 + value * (1.0 - gate))


def head_norm(hidden, gamma, beta):
    count = hidden.shape[0]
    average = jnp.sum(hidden, axis=0) / count
    variance = jnp.sum(hidden * hidden, axis=0) / count - average * average
    scale = lax.rsqrt(variance + EPS_NORM)
    normed = (hidden - average) * scale
    return gamma * normed + beta, (normed, scale), average, variance


def head_norm_back(grad, kept, gamma):
    normed, scale = kept
    count = grad.shape[0]
    beta_sum = jnp.sum(grad, axis=0)
    gamma_sum = jnp.sum(grad * normed, axis=0)
    back = gamma * scale * (grad - beta_sum / count - normed * gamma_sum / count)
    return back, gamma_sum, beta_sum


def heads(pooled_low, wall, gammas, betas, bias, partner, live):
    project = [wall[ROW_PROJ + 2048 * k : ROW_PROJ + 2048 * (k + 1)] for k in range(3)]
    predict_in = wall[ROW_PIN:ROW_POUT].reshape(OUT, PRED)
    predict_out = wall[ROW_POUT:ROW_VEC]
    means, variances, kept_all, normed_all, lows = [], [], [], [], []
    low = pooled_low
    for k in range(3):
        normed, kept, mean, variance = head_norm(dot(low, project[k]), gammas[4 + k], betas[4 + k])
        means.append(mean)
        variances.append(variance)
        kept_all.append(kept)
        normed_all.append(normed)
        lows.append(low)
        low = (jax.nn.silu(normed) if k < 2 else normed).astype(BF16)
    latent, latent_low = normed, low
    normed_q, kept_q, mean, variance = head_norm(dot(latent_low, predict_in), gammas[7], betas[7])
    means.append(mean)
    variances.append(variance)
    act = jax.nn.silu(normed_q).astype(BF16)
    predicted = dot(act, predict_out) + bias
    choose = (partner[:, None] == jnp.arange(latent.shape[0])[None, :]).astype(F32)
    target = jnp.dot(choose, latent, precision=lax.Precision.HIGHEST)
    inner = jnp.sum(predicted * target, axis=-1)
    inv_pred = lax.rsqrt(jnp.sum(predicted * predicted, axis=-1) + COS_EPS)
    inv_goal = lax.rsqrt(jnp.sum(target * target, axis=-1) + COS_EPS)
    flags = live.astype(F32)
    loss_sum = -jnp.sum(flags * inner * inv_pred * inv_goal)
    live_count = jnp.sum(flags)
    grad_cos = -flags / live_count
    grad_pred = grad_cos[:, None] * (
        target * (inv_pred * inv_goal)[:, None] - (inner * inv_pred**3 * inv_goal)[:, None] * predicted
    )
    grad_bias = jnp.sum(grad_pred, axis=0)
    low_p = grad_pred.astype(BF16)
    grad_act = dot_nt(low_p, predict_out)
    grad_q, gamma_q, beta_q = head_norm_back(silu_back(normed_q, grad_act), kept_q, gammas[7])
    low_q = grad_q.astype(BF16)
    grad_act = dot_nt(low_q, predict_in)
    low_f, gamma_sums, beta_sums = [None] * 3, [None] * 3, [None] * 3
    for k in (2, 1, 0):
        grad_normed = grad_act if k == 2 else silu_back(normed_all[k], grad_act)
        grad_hidden, gamma_sums[k], beta_sums[k] = head_norm_back(grad_normed, kept_all[k], gammas[4 + k])
        low_f[k] = grad_hidden.astype(BF16)
        grad_act = dot_nt(low_f[k], project[k])
    block = (lax.axis_index("p") % 2) * 4 + lax.axis_index("x") * 2 + lax.axis_index("c")

    def columns(v, start):
        return lax.dynamic_slice_in_dim(v, start, 256, 1)

    rows = [dot_tn(lows[k], columns(low_f[k], block * 256)).astype(BF16) for k in range(3)]
    g_in = dot_tn(latent_low, columns(low_q, (block % 2) * 256)).astype(BF16)
    rows.append(lax.dynamic_index_in_dim(g_in.reshape(PRED, 4, 256), block // 2, 1, keepdims=False))
    rows.append(dot_tn(act, columns(low_p, block * 256)).astype(BF16))
    vector = (gamma_sums + [gamma_q], beta_sums + [beta_q], grad_bias)
    return grad_act, jnp.concatenate(rows, axis=0), vector, block, loss_sum, live_count, means, variances


def norm_coefs(sums, total, gamma, beta):
    mean = sums[:, 0] / total[:, None]
    variance = sums[:, 1] / total[:, None] - mean * mean
    scale = lax.rsqrt(variance + EPS_NORM)
    a = gamma * scale
    return mean, variance, scale, a, beta - a * mean


def pack(rows):
    rows = list(rows) + [jnp.zeros_like(rows[0])] * (8 - len(rows))
    return jnp.stack(rows, axis=1)


def back_coefs(grad_sum, product_sum, mean, scale, a, total):
    gamma_sum = scale * (product_sum - mean * grad_sum)
    c = -a * scale * gamma_sum / total[:, None]
    b = -a * grad_sum / total[:, None] - c * mean
    return b, c, gamma_sum


def on_device(inputs, masks, partner, live, params, first, second, running):
    count = lax.axis_size(ALL)
    index = lax.axis_index(ALL)
    plane = lax.axis_index("g")
    own = params.shape[0] // 128
    micros, images, rows, width, _ = inputs.shape
    out_rows, out_cols = rows // 2, width // 2
    window_rows = -(-own // 256) * 16
    shift = window_rows * 16 - own
    plane_rows = window_rows * LANES
    near = (
        shift * count <= own
        and lax.axis_size(PLANE) == LANES
        and ROW_COUT < plane_rows < ROW_PROJ <= 2 * plane_rows
        and window_rows - tail_rows(shift, count) < ROW_CMID <= window_rows
        and ROW_VEC % window_rows + 16 <= window_rows
        and ROW_VEC >= (lax.axis_size("g") - 1) * plane_rows
    )

    x = inputs.reshape(micros, images * rows * width, D_IN)
    x_last, mask_last = inputs[:, :, -1], masks[:, :, -1]
    mask = masks.astype(F32)
    w_in = mask.reshape(micros, -1, 1)
    split = mask.reshape(micros, images, out_rows, 2, out_cols, 2)
    wph = jnp.transpose(split, (0, 3, 5, 1, 2, 4)).reshape(micros, 4, -1, 1)
    around = [(i, i + 1) for i in range(lax.axis_size(("x", "c")) - 1)]
    mask_halo = lax.ppermute(mask_last, ("x", "c"), around).astype(F32)
    total_in = jnp.sum(mask, axis=(1, 2, 3))
    image_pixels = jnp.sum(split[:, :, :, 0, :, 0], axis=(2, 3))
    total_out = jnp.sum(image_pixels, axis=1)
    image_pixels = add_all(image_pixels, ("c", "x"))
    chosen = to_heads(jnp.stack([partner.astype(F32), live.astype(F32)], axis=-1))
    if near:
        window = flat_to_window(params, window_rows, shift, index, count)
        column = lax.all_to_all(window, PLANE, 1, 0, tiled=True)
        wide_in, vec = first_rows_everywhere(column, plane, plane_rows)
        trunk = spread_trunk(column, plane, plane_rows)
        trunk, x_last, wide_in, image_pixels, chosen, mask_halo = lax.optimization_barrier(
            (trunk, x_last, wide_in, image_pixels, chosen, mask_halo)
        )
        h, xe, st, w_first = conv_in(x, w_in, wph[:, 0], wide_in)
        trunk = lax.all_gather(trunk, ALL, axis=0, tiled=False).reshape(GROUPS, LANES, GROUP, 256)
    else:
        wall = lax.all_gather(params.astype(BF16), ALL, axis=0, tiled=True).reshape(-1, 2048)
        wide_in, vec = wall[:ROW_CMID], wall[ROW_VEC : ROW_VEC + 16]
        trunk = jnp.transpose(wall[:ROW_PROJ].reshape(GROUPS, GROUP, LANES, 256), (0, 2, 1, 3))
        h, xe, st, w_first = conv_in(x, w_in, wph[:, 0], wide_in)

    x_halo = lax.ppermute(x_last, ("x", "c"), around).reshape(micros, images * width, D_IN)
    whalo = jnp.transpose(mask_halo.reshape(micros, images, out_cols, 2), (0, 3, 1, 2)).reshape(micros, 2, -1, 1)
    share_index = lax.axis_index(("x", "c"))

    pixels = jnp.broadcast_to(jnp.stack([total_in, total_out], axis=1)[..., None], (micros, 2, 128))
    sums = add_all(jnp.concatenate([st[:, :2], pixels], axis=2))
    total_in, total_out = sums[:, 0, MID], sums[:, 1, MID]
    sums = sums[..., :MID]
    hh = conv_in_halo(x_halo, w_first)
    if near:
        window, trunk, sums, hh, total_in, total_out = lax.optimization_barrier(
            (window, trunk, sums, hh, total_in, total_out)
        )
        wall = lax.all_gather(window, ALL, axis=0, tiled=True)

    vec = vec.astype(F32).reshape(-1)
    ranges = norm_ranges()
    gammas = [vec[start : start + n] for start, n in ranges]
    betas = [vec[NORM + start : NORM + start + n] for start, n in ranges]
    bias = vec[2 * NORM : 2 * NORM + OUT]

    mean_in, var_in, scale_in, a_in, b_in = norm_coefs(sums, total_in, gammas[0], betas[0])
    coef_in = pack([a_in, b_in])
    hs, st_side = conv_side(xe, trunk)
    cols, hm, st, w_mid = conv_mid(h, hh, coef_in, wph, whalo, trunk)
    sums = add_all(jnp.concatenate([st[:, :2], st_side[:, :2]], axis=2))
    mean_mid, var_mid, scale_mid, a_mid, b_mid = norm_coefs(sums[..., :MID], total_out, gammas[1], betas[1])
    mean_side, var_side, scale_side, a_side, b_side = norm_coefs(sums[..., MID:], total_out, gammas[3], betas[3])
    am, ho, st, w_out = conv_out(hm, pack([a_mid, b_mid]), wph, trunk)
    sums = add_all(st[:, :2])
    mean_out, var_out, scale_out, a_out, b_out = norm_coefs(sums, total_out, gammas[2], betas[2])
    coef_join = pack([a_out, a_side, b_out + b_side])
    pooled = pool(ho, hs, coef_join, wph)
    for axis in ("x", "c"):
        half = pooled.shape[1] // 2
        here = lax.axis_index(axis)
        keep = lax.dynamic_slice_in_dim(pooled, here * half, half, 1)
        send = lax.dynamic_slice_in_dim(pooled, (1 - here) * half, half, 1)
        pooled = keep + swap(send, axis, 1)
    share = pooled.shape[1]
    share_pixels = lax.dynamic_slice_in_dim(image_pixels, share_index * share, share, 1)
    pooled_low = to_heads((pooled / share_pixels[..., None]).astype(BF16))
    slope = slopes(ho, hs, coef_join, wph)
    pooled_low, slope = lax.optimization_barrier((pooled_low, slope))

    grad_pool, head_rows, head_vec, block, loss_sum, live_count, head_means, head_vars = heads(
        pooled_low, wall, gammas, betas, bias, chosen[:, 0].astype(jnp.int32), chosen[:, 1]
    )

    def vector_rows(gamma, beta, extra):
        flat, at = jnp.zeros((16 * 2048,), F32), 0
        for value in gamma + beta + [extra]:
            flat = flat + jnp.pad(value, (at, flat.shape[0] - at - value.shape[0]))
            at += value.shape[0]
        return flat.astype(BF16).reshape(16, 2048)

    none_head = [jnp.zeros((n,), F32) for _, n in ranges[4:]]
    none_trunk = [jnp.zeros((n,), F32) for _, n in ranges[:4]]
    head_vector = vector_rows(none_trunk + head_vec[0], none_trunk + head_vec[1], head_vec[2])
    head_vector = lax.dynamic_slice_in_dim(head_vector, block * 256, 256, 1)

    scalars = jnp.pad(jnp.stack([loss_sum, live_count]), (0, 126))
    head_stats = jnp.concatenate(head_means + head_vars + [scalars]).reshape(1, -1, 128)
    head_stats = exchange_planes(jnp.broadcast_to(head_stats, (micros,) + head_stats.shape[1:])).reshape(micros, -1)
    head_size = NORM - sum(n for _, n in ranges[:4])
    scalars = head_stats[:, 2 * head_size : 2 * head_size + 2]

    grad_pool = grad_pool.astype(BF16).reshape(lax.axis_size("g"), lax.axis_size("p"), images, OUT)
    grad_pool = lax.dynamic_index_in_dim(grad_pool, lax.axis_index("p"), 1, keepdims=False)
    gs = exchange_planes(grad_pool)
    if near:
        head_part = jnp.concatenate(
            [
                jnp.zeros((ROW_PROJ, 256), BF16),
                head_rows,
                head_vector,
                jnp.zeros((window_rows * count - ROW_VEC - 16, 256), BF16),
            ],
            axis=0,
        )
        head_part, gs, head_stats = lax.optimization_barrier((head_part, gs, head_stats))
        head_part = lax.psum_scatter(head_part, "g", scatter_dimension=0, tiled=True)
    gs = gs.astype(F32) / image_pixels[..., None]

    sums = add_all(jnp.sum(gs[:, None] * slope, axis=2))
    bo, co, gamma_out = back_coefs(sums[:, 0], sums[:, 1], mean_out, scale_out, a_out, total_out)
    bs, cs, gamma_side = back_coefs(sums[:, 0], sums[:, 2], mean_side, scale_side, a_side, total_out)
    beta_joined = sums[:, 0]
    coef_back = pack([a_out, a_side, b_out + b_side, bo, co, bs, cs])
    d_mid, st, g_out = back_out(
        ho, hs, gs, coef_back, wph, am, xe, w_out, hm, pack([a_mid, b_mid])
    )
    if near:
        head_part, g_out = lax.optimization_barrier((head_part, g_out))
        g_out = lax.psum_scatter(g_out, PLANE, scatter_dimension=0, tiled=False)
    sums = add_all(st[:, :2])
    bm, cm, gamma_mid = back_coefs(sums[:, 0], sums[:, 1], mean_mid, scale_mid, a_mid, total_out)
    beta_mid = sums[:, 0]
    d_in, d_halo, st, g_mid = back_mid(
        hm, d_mid, pack([a_mid, bm, cm]), cols, w_mid, h, hh, coef_in, wph, whalo
    )
    if near:
        g_mid, g_out = lax.optimization_barrier((g_mid, g_out))
        g_mid = lax.psum_scatter(g_mid, PLANE, scatter_dimension=0, tiled=False)
        out_first = to_first_plane(g_out[: plane_rows - ROW_COUT])
        out_second = add_all(g_out[plane_rows - ROW_COUT :], ("g",))
    sums = add_all(st[:, :2])
    bi, ci, gamma_in = back_coefs(sums[:, 0], sums[:, 1], mean_in, scale_in, a_in, total_in)
    beta_in = sums[:, 0]
    g_in = back_in(h, d_in, d_halo, pack([a_in, bi, ci]), wph, whalo, x, x_halo)

    if near:
        g_in, g_mid, out_first, out_second = lax.optimization_barrier(
            (plane_reduce(g_in), g_mid, out_first, out_second)
        )
    trunk_gamma = [jnp.sum(v, axis=0) for v in (gamma_in, gamma_mid, gamma_out, gamma_side)]
    trunk_beta = [jnp.sum(v, axis=0) for v in (beta_in, beta_mid, beta_joined, beta_joined)]
    trunk_vector = vector_rows(trunk_gamma + none_head, trunk_beta + none_head, jnp.zeros((OUT,), F32))

    if near:
        def blank(n):
            return jnp.zeros((n, 256), BF16)

        first_rows = jnp.concatenate([blank(ROW_CMID), to_first_plane(g_mid), out_first], axis=0)
        second_rows = jnp.concatenate([out_second, blank(plane_rows - out_second.shape[0])], axis=0)
        part = jnp.where(plane == 0, first_rows, jnp.where(plane == 1, head_part + second_rows, head_part))
        window = lax.all_to_all(part, PLANE, 0, 1, tiled=True)
        tail = tail_rows(shift, count)
        prev = lax.ppermute(window[window_rows - tail :], ALL, [(i, i + 1) for i in range(count - 1)])
        g_in = to_first_plane(g_in)
        for axis in PLANE:
            g_in = gather_axis(g_in, axis)
        g_in = jnp.transpose(g_in, (3, 2, 1, 0, 4)).reshape(ROW_CMID, 2048)
        window = window.at[:ROW_CMID].add(jnp.where(index == 0, g_in, 0))
        prev = prev.at[: ROW_CMID - window_rows + tail].add(jnp.where(index == 1, g_in[window_rows - tail :], 0))
        at = ROW_VEC % window_rows
        window = window.at[at : at + 16].add(jnp.where(index == ROW_VEC // window_rows, trunk_vector, 0))
        new_params, new_first, new_second, new_copy = adam_from_window(
            window, prev, shift, index, params, first, second
        )
    else:
        alone = (lax.axis_index("p") < 2).astype(BF16)
        head_part = jnp.concatenate([head_rows, head_vector], axis=0) * alone
        head_part = lax.dynamic_update_slice(
            jnp.zeros((head_part.shape[0], 2048), BF16), head_part, (jnp.int32(0), (block * 256).astype(jnp.int32))
        )
        lone = (index == 0).astype(BF16)
        head_part = head_part.at[ROW_VEC - ROW_PROJ :].add(trunk_vector * lone)
        trunk = jnp.concatenate([g_in, g_mid, g_out], axis=1)
        trunk = jnp.transpose(trunk, (1, 0, 2)).reshape(-1, 2048)
        flat = jnp.concatenate([trunk, head_part], axis=0).reshape(-1)
        flat = flat[: params.shape[0] * count]
        grad = lax.psum_scatter(flat, ALL, scatter_dimension=0, tiled=True).astype(F32)
        new_params, new_first, new_second = adam(grad, params, first, second)
        new_copy = new_params.astype(BF16)

    averages = jnp.concatenate([mean_in, mean_mid, mean_out, mean_side, head_stats[:, :head_size]], axis=1)
    spreads = jnp.concatenate([var_in, var_mid, var_out, var_side, head_stats[:, head_size : 2 * head_size]], axis=1)
    stats = jnp.stack([averages, spreads], axis=1)
    new_running = running
    for micro in range(micros):
        new_running = (1.0 - MOMENTUM) * new_running + MOMENTUM * stats[micro]
    return (
        scalars[:, 0],
        scalars[:, 1].astype(jnp.int32),
        new_params,
        new_first,
        new_second,
        new_copy,
        new_running,
    )


def solution(mesh):
    img, rows = mesh.shape["img"], mesh.shape["rows"]
    fine = Mesh(mesh.devices.reshape(MB, img // MB, 2, rows // 2), ALL)
    split = P(ALL)
    placed = (
        P(None, ("g", "p"), ("x", "c"), None, None),
        P(None, ("g", "p"), ("x", "c"), None),
        P(None, ALL),
        P(None, ALL),
        split,
        split,
        split,
        P(),
    )
    return jax.shard_map(
        on_device,
        mesh=fine,
        in_specs=placed,
        out_specs=(P(), P(), split, split, split, split, P()),
        check_vma=False,
    )
```

```python
import jax
import jax.numpy as jnp
from jax import lax
from jax.experimental import pallas as pl
from jax.experimental.pallas import tpu as pltpu
from jax.sharding import Mesh, PartitionSpec as P

D_IN = 1024
MID = 512
OUT = 2048
PRED = 512
MB = 4
STEP = 5
NORM = 11776
PARAMS = 20734976

EPS_NORM = 1e-05
MOMENTUM = 0.1
RATE = 0.03
BETA_ONE = 0.5
BETA_TWO = 0.5
DECAY = 0.01
ADAM_EPS = 1e-08
COS_EPS = 1e-06

ROW_CIN, ROW_CMID, ROW_COUT, ROW_SIDE = 0, 256, 1408, 1920
ROW_PROJ, ROW_PIN, ROW_POUT, ROW_VEC = 2944, 9088, 9600, 10112
LANES = 8
GROUPS, GROUP = 4, 736
GRAD_OUT, GRAD_MID = 1536, 1152
ALL = ("g", "p", "x", "c")
PLANE = ("p", "x", "c")
F32, BF16 = jnp.float32, jnp.bfloat16
COST_SHARE = 8


def params_of(mib=60, steps=1):
    return pltpu.CompilerParams(
        vmem_limit_bytes=mib << 20, dimension_semantics=("arbitrary",) * steps
    )


def cost(flops, moved):
    return pl.CostEstimate(flops=flops // COST_SHARE, bytes_accessed=moved // COST_SHARE, transcendentals=0)


def whole_block(shape):
    zeros = (0,) * len(shape)
    return pl.BlockSpec(shape, lambda *_: zeros)


def sigmoid(v):
    return 1.0 / (1.0 + jnp.exp(-v))


def dot(a, b):
    return jnp.dot(a, b, preferred_element_type=F32)


def dot_nt(a, b):
    return lax.dot_general(a, b, (((1,), (1,)), ((), ())), preferred_element_type=F32)


def dot_tn(a, b):
    return lax.dot_general(a, b, (((0,), (0,)), ((), ())), preferred_element_type=F32)


def fold(v):
    return jnp.sum(v.reshape(-1, 8, v.shape[-1]), axis=0)


def unwide(wide_ref, scratch, out_ref):
    rows = wide_ref.shape[0]
    for part in range(4):
        for col in range(4):
            lanes = pl.ds(part * 512 + col * 128, 128)
            scratch[col, pl.ds(part, rows, stride=4), :] = wide_ref[:, lanes].astype(F32)
    for col in range(4):
        out_ref[:, col * 128 : (col + 1) * 128] = scratch[col].astype(BF16)


def trunk_pieces(start, stop):
    found = []
    for group in range(GROUPS):
        low, high = max(start, group * GROUP), min(stop, (group + 1) * GROUP)
        if low < high:
            found.append((group, low - group * GROUP, low - start, high - low))
    return found


def trunk_specs(start, stop):
    def spec(group):
        return pl.BlockSpec(
            (1, LANES, GROUP, 256), lambda *_: (group, 0, 0, 0), pipeline_mode=pl.Buffered(1)
        )

    return [spec(piece[0]) for piece in trunk_pieces(start, stop)]


def join_trunk(refs, start, stop, out_ref):
    for ref, (_, low, to, rows) in zip(refs, trunk_pieces(start, stop)):
        for block in range(LANES):
            out_ref[to : to + rows, block * 256 : block * 256 + 256] = ref[0, block, low : low + rows, :]


def unwide_trunk(refs, start, stop, scratch, out_ref):
    for ref, (_, low, to, rows) in zip(refs, trunk_pieces(start, stop)):
        for part in range(4):
            for col in range(4):
                block, lanes = 2 * part + col // 2, slice((col % 2) * 128, (col % 2) * 128 + 128)
                scratch[col, pl.ds(part + 4 * to, rows, stride=4), :] = ref[0, block, low : low + rows, lanes].astype(F32)
    for col in range(4):
        out_ref[:, col * 128 : (col + 1) * 128] = scratch[col].astype(BF16)


def window_kernel(off_ref, flat_ref, out_ref):
    off = off_ref[0]
    rows = out_ref.shape[0]
    for col in range(16):
        out_ref[:, col * 128 : (col + 1) * 128] = flat_ref[pl.ds(off + col, rows, stride=16), :].astype(BF16)


def flat_to_window(params, rows, shift, index, count):
    own = params.shape[0] // 128
    head = shift * count
    nxt = lax.ppermute(
        params[: head * 128].astype(BF16), ALL, [(i + 1, i) for i in range(count - 1)]
    )
    flat = jnp.concatenate([params, nxt.astype(F32), jnp.zeros((1024,), F32)]).reshape(-1, 128)
    return pl.pallas_call(
        window_kernel,
        out_shape=jax.ShapeDtypeStruct((rows, 2048), BF16),
        in_specs=[pl.BlockSpec(memory_space=pltpu.SMEM), whole_block((own + head + 8, 128))],
        out_specs=whole_block((rows, 2048)),
        compiler_params=pltpu.CompilerParams(vmem_limit_bytes=40 << 20),
    )((index * shift).astype(jnp.int32)[None], flat)


def adam(grad, params, first, second):
    new_first = BETA_ONE * first + (1.0 - BETA_ONE) * grad
    new_second = BETA_TWO * second + (1.0 - BETA_TWO) * grad * grad
    corrected_first = new_first / (1.0 - BETA_ONE**STEP)
    corrected_second = new_second / (1.0 - BETA_TWO**STEP)
    new_params = params - RATE * (
        corrected_first / (jnp.sqrt(corrected_second) + ADAM_EPS) + DECAY * params
    )
    return new_params, new_first, new_second


def adam_kernel(off_ref, tail_ref, win_ref, p_ref, m_ref, v_ref, po_ref, mo_ref, vo_ref, co_ref, flat):
    step = pl.program_id(0)

    @pl.when(step == 0)
    def _():
        tail = tail_ref.shape[0]
        rows = win_ref.shape[0]
        for col in range(16):
            lanes = pl.ds(col * 128, 128)
            flat[pl.ds(col, tail, stride=16), :] = tail_ref[:, lanes].astype(F32)
            flat[pl.ds(tail * 16 + col, rows, stride=16), :] = win_ref[:, lanes].astype(F32)

    size = p_ref.shape[0]
    grad = flat[pl.ds(off_ref[0] + step * size, size), :]
    po_ref[...], mo_ref[...], vo_ref[...] = adam(grad, p_ref[...], m_ref[...], v_ref[...])
    co_ref[...] = po_ref[...].astype(BF16)


def tail_rows(shift, count):
    return -(-shift * (count - 1) // 256) * 16


def adam_from_window(window, prev, shift, index, params, first, second):
    own = params.shape[0] // 128
    rows, tail = window.shape[0], prev.shape[0]
    block = 512
    steps = -(-own // block)
    assert steps * block <= rows * 16
    off = (tail * 16 - index * shift).astype(jnp.int32)[None]
    spec = pl.BlockSpec((block, 128), lambda i: (i, 0))
    shaped = [v.reshape(own, 128) for v in (params, first, second)]
    outs = pl.pallas_call(
        adam_kernel,
        grid=(steps,),
        out_shape=[jax.ShapeDtypeStruct((own, 128), F32)] * 3 + [jax.ShapeDtypeStruct((own, 128), BF16)],
        in_specs=[pl.BlockSpec(memory_space=pltpu.SMEM), whole_block((tail, 2048)), whole_block((rows, 2048))] + [spec] * 3,
        out_specs=[spec] * 4,
        scratch_shapes=[pltpu.VMEM(((tail + rows) * 16, 128), F32)],
        compiler_params=params_of(40),
    )(off, prev, window, *shaped)
    return [v.reshape(-1) for v in outs]


def conv_in_kernel(x_ref, w_ref, wide_ref, h_ref, xe_ref, st_ref, wb, wf, hs, xs):
    micro, part = pl.program_id(0), pl.program_id(1)

    @pl.when((micro == 0) & (part == 0))
    def _():
        unwide(wide_ref, wf, wb)

    images = x_ref.shape[1] // 64
    h = dot(x_ref[0], wb[...])
    for col in range(4):
        hs[col] = h[:, col * 128 : (col + 1) * 128]

    def body(i, carry):
        at = pl.multiple_of(i * 64, 64)
        low = pl.multiple_of(i * 16, 16)
        w = [jnp.broadcast_to(w_ref[0, k, pl.ds(low, 16), :], (16, 128)) for k in range(4)]
        new = []
        for col in range(4):
            lanes = slice(col * 128, (col + 1) * 128)
            total, square = carry[col]
            for side in range(2):
                half = hs[col, pl.ds(at + side, 32, stride=2), :].reshape(2, 2, 8, 128)
                for row in range(2):
                    h = half[:, row].reshape(16, 128) * w[2 * row + side]
                    total, square = total + fold(h), square + fold(h * h)
                    h_ref[0, 2 * row + side, pl.ds(low, 16), lanes] = h
            new.append((total, square))
        w = w[0]
        for col in range(8):
            lanes = slice(col * 128, (col + 1) * 128)
            for row in range(2):
                xs[col, row * 16 : row * 16 + 16, :] = x_ref[0, pl.ds(at + row * 32, 16), lanes].astype(F32)
            xe_ref[0, pl.ds(low, 16), lanes] = (xs[col, pl.ds(0, 16, stride=2), :] * w).astype(BF16)
        return tuple(new)

    zero = jnp.zeros((8, 128), F32)
    found = lax.fori_loop(0, images, body, ((zero, zero),) * 4)

    @pl.when(part == 0)
    def _():
        st_ref[...] = jnp.zeros_like(st_ref)

    for col in range(4):
        lanes = slice(col * 128, (col + 1) * 128)
        for k in range(2):
            st_ref[0, k : k + 1, lanes] += jnp.sum(found[col][k], axis=0, keepdims=True)


def conv_in(x, wph, wide):
    micros, pixels, _ = x.shape
    images = pixels // 64
    parts = 2
    b = images // parts
    return pl.pallas_call(
        conv_in_kernel,
        grid=(micros, parts),
        out_shape=[
            jax.ShapeDtypeStruct((micros, 4, images * 16, MID), F32),
            jax.ShapeDtypeStruct((micros, images * 16, D_IN), BF16),
            jax.ShapeDtypeStruct((micros, 8, MID), F32),
            jax.ShapeDtypeStruct((D_IN, MID), BF16),
        ],
        in_specs=[
            pl.BlockSpec((1, b * 64, D_IN), lambda m, k: (m, k, 0)),
            pl.BlockSpec((1, 4, b * 16, 1), lambda m, k: (m, 0, k, 0)),
            whole_block((256, 2048)),
        ],
        out_specs=[
            pl.BlockSpec((1, 4, b * 16, MID), lambda m, k: (m, 0, k, 0)),
            pl.BlockSpec((1, b * 16, D_IN), lambda m, k: (m, k, 0)),
            pl.BlockSpec((1, 8, MID), lambda m, k: (m, 0, 0)),
            whole_block((D_IN, MID)),
        ],
        scratch_shapes=[
            pltpu.VMEM((4, D_IN, 128), F32),
            pltpu.VMEM((4, b * 64, 128), F32),
            pltpu.VMEM((8, 32, 128), F32),
        ],
        compiler_params=params_of(56, 2),
        cost_estimate=cost(2 * micros * images * 64 * D_IN * MID, 40 << 20),
    )(x, wph, wide)


def halo_kernel(xh_ref, wb_ref, hh_ref, hs):
    h = dot(xh_ref[0], wb_ref[...])
    rows = hh_ref.shape[2]
    for col in range(4):
        lanes = slice(col * 128, (col + 1) * 128)
        hs[col] = h[:, lanes]
        for side in range(2):
            hh_ref[0, side, :, lanes] = hs[col, pl.ds(side, rows, stride=2), :]


def conv_in_halo(xh, weight):
    micros, pixels, _ = xh.shape
    return pl.pallas_call(
        halo_kernel,
        grid=(micros,),
        out_shape=jax.ShapeDtypeStruct((micros, 2, pixels // 2, MID), F32),
        in_specs=[pl.BlockSpec((1, pixels, D_IN), lambda m: (m, 0, 0)), whole_block((D_IN, MID))],
        out_specs=pl.BlockSpec((1, 2, pixels // 2, MID), lambda m: (m, 0, 0, 0)),
        scratch_shapes=[pltpu.VMEM((4, pixels, 128), F32)],
        compiler_params=params_of(40),
        cost_estimate=cost(2 * micros * pixels * D_IN * MID, 9 << 20),
    )(xh, weight)


def side_kernel(xe_ref, *refs):
    pieces, (hs_ref, st_ref, weight) = refs[:-3], refs[-3:]

    @pl.when((pl.program_id(0) == 0) & (pl.program_id(1) == 0))
    def _():
        join_trunk(pieces, ROW_SIDE, ROW_PROJ, weight)

    n = hs_ref.shape[2]
    h = dot(xe_ref[0], weight[:, pl.ds(pl.multiple_of(pl.program_id(1) * n, n), n)])
    hs_ref[0] = h
    st_ref[...] = jnp.zeros_like(st_ref)
    st_ref[0, 0:1, :] = jnp.sum(h, axis=0, keepdims=True)
    st_ref[0, 1:2, :] = jnp.sum(h * h, axis=0, keepdims=True)


def conv_side(xe, trunk):
    micros, rows, _ = xe.shape
    cols = 4
    n = OUT // cols
    return pl.pallas_call(
        side_kernel,
        grid=(micros, cols),
        out_shape=[
            jax.ShapeDtypeStruct((micros, rows, OUT), F32),
            jax.ShapeDtypeStruct((micros, 8, OUT), F32),
        ],
        in_specs=[
            pl.BlockSpec((1, rows, D_IN), lambda m, k: (m, 0, 0)),
        ]
        + trunk_specs(ROW_SIDE, ROW_PROJ),
        out_specs=[
            pl.BlockSpec((1, rows, n), lambda m, k: (m, 0, k)),
            pl.BlockSpec((1, 8, n), lambda m, k: (m, 0, k)),
        ],
        scratch_shapes=[pltpu.VMEM((D_IN, OUT), BF16)],
        compiler_params=params_of(56, 2),
        cost_estimate=cost(2 * micros * rows * D_IN * OUT, 16 << 20),
    )(xe, *[trunk] * len(trunk_pieces(ROW_SIDE, ROW_PROJ)))


def shift_right(v):
    moved = pltpu.roll(v, 1, 1)
    return jnp.where(lax.broadcasted_iota(jnp.int32, v.shape, 1) == 0, 0.0, moved)


def shift_left(v):
    moved = pltpu.roll(v, 7, 1)
    return jnp.where(lax.broadcasted_iota(jnp.int32, v.shape, 1) == 7, 0.0, moved)


def conv_mid_kernel(h_ref, hh_ref, cf_ref, w_ref, wh_ref, *refs):
    pieces, (cols_ref, hm_ref, st_ref, wb, wf) = refs[:-5], refs[-5:]
    micro = pl.program_id(0)

    @pl.when(micro == 0)
    def _():
        unwide_trunk(pieces, ROW_CMID, ROW_COUT, wf, wb)

    images = h_ref.shape[2] // 16
    scale, shift = cf_ref[0, 0:1, :], cf_ref[0, 1:2, :]

    def act(h, w):
        v = h * scale + shift
        return v * sigmoid(v) * w

    def body(i, carry):
        at = pl.ds(pl.multiple_of(i * 16, 16), 16)
        half = pl.ds(pl.multiple_of(i * 8, 8), 8)
        a = [act(h_ref[0, k, at, :], w_ref[0, k, at, :]).reshape(2, 8, MID) for k in range(4)]
        above = [act(hh_ref[0, k, half, :], wh_ref[0, k, half, :]).reshape(1, 8, MID) for k in range(2)]
        a1s, a3s = shift_right(a[1]), shift_right(a[3])
        up2 = jnp.concatenate([above[0], a[2][:1]], axis=0)
        up3 = jnp.concatenate([above[1], a[3][:1]], axis=0)
        up3s = jnp.concatenate([shift_right(above[1]), a3s[:1]], axis=0)
        for tap, value in enumerate([up3s, up2, up3, a1s, a[0], a[1], a3s, a[2], a[3]]):
            cols_ref[0, at, tap * MID : (tap + 1) * MID] = value.reshape(16, MID).astype(BF16)
        return carry

    lax.fori_loop(0, images, body, 0)
    h = dot(cols_ref[0], wb[...])
    hm_ref[0] = h
    hw = h * w_ref[0, 0]
    st_ref[...] = jnp.zeros_like(st_ref)
    st_ref[0, 0:1, :] = jnp.sum(hw, axis=0, keepdims=True)
    st_ref[0, 1:2, :] = jnp.sum(hw * hw, axis=0, keepdims=True)


def conv_mid(h, hh, coef, wph, whalo, trunk):
    micros, _, rows, _ = h.shape
    return pl.pallas_call(
        conv_mid_kernel,
        grid=(micros,),
        out_shape=[
            jax.ShapeDtypeStruct((micros, rows, 9 * MID), BF16),
            jax.ShapeDtypeStruct((micros, rows, MID), F32),
            jax.ShapeDtypeStruct((micros, 8, MID), F32),
            jax.ShapeDtypeStruct((9 * MID, MID), BF16),
        ],
        in_specs=[
            pl.BlockSpec((1, 4, rows, MID), lambda m: (m, 0, 0, 0)),
            pl.BlockSpec((1, 2, rows // 2, MID), lambda m: (m, 0, 0, 0)),
            pl.BlockSpec((1, 8, MID), lambda m: (m, 0, 0)),
            pl.BlockSpec((1, 4, rows, 1), lambda m: (m, 0, 0, 0)),
            pl.BlockSpec((1, 2, rows // 2, 1), lambda m: (m, 0, 0, 0)),
        ]
        + trunk_specs(ROW_CMID, ROW_COUT),
        out_specs=[
            pl.BlockSpec((1, rows, 9 * MID), lambda m: (m, 0, 0)),
            pl.BlockSpec((1, rows, MID), lambda m: (m, 0, 0)),
            pl.BlockSpec((1, 8, MID), lambda m: (m, 0, 0)),
            pl.BlockSpec((9 * MID, MID), lambda m: (0, 0), pipeline_mode=pl.Buffered(1)),
        ],
        scratch_shapes=[pltpu.VMEM((4, 9 * MID, 128), F32)],
        compiler_params=params_of(60),
        cost_estimate=cost(2 * micros * rows * 9 * MID * MID, 50 << 20),
    )(h, hh, coef, wph, whalo, *[trunk] * len(trunk_pieces(ROW_CMID, ROW_COUT)))


def conv_out_kernel(hm_ref, cf_ref, w_ref, *refs):
    pieces, (am_ref, ho_ref, st_ref, weight_ref) = refs[:-4], refs[-4:]

    @pl.when(pl.program_id(0) == 0)
    def _():
        join_trunk(pieces, ROW_COUT, ROW_SIDE, weight_ref)

    v = hm_ref[0] * cf_ref[0, 0:1, :] + cf_ref[0, 1:2, :]
    am = (v * sigmoid(v) * w_ref[0, 0]).astype(BF16)
    am_ref[0] = am
    st_ref[...] = jnp.zeros_like(st_ref)
    for k in range(4):
        lanes = slice(k * 512, (k + 1) * 512)
        h = dot(am, weight_ref[:, lanes])
        ho_ref[0, :, lanes] = h
        st_ref[0, 0:1, lanes] = jnp.sum(h, axis=0, keepdims=True)
        st_ref[0, 1:2, lanes] = jnp.sum(h * h, axis=0, keepdims=True)


def conv_out(hm, coef, wph, trunk):
    micros, rows, _ = hm.shape
    return pl.pallas_call(
        conv_out_kernel,
        grid=(micros,),
        out_shape=[
            jax.ShapeDtypeStruct((micros, rows, MID), BF16),
            jax.ShapeDtypeStruct((micros, rows, OUT), F32),
            jax.ShapeDtypeStruct((micros, 8, OUT), F32),
            jax.ShapeDtypeStruct((MID, OUT), BF16),
        ],
        in_specs=[
            pl.BlockSpec((1, rows, MID), lambda m: (m, 0, 0)),
            pl.BlockSpec((1, 8, MID), lambda m: (m, 0, 0)),
            pl.BlockSpec((1, 1, rows, 1), lambda m: (m, 0, 0, 0)),
        ]
        + trunk_specs(ROW_COUT, ROW_SIDE),
        out_specs=[
            pl.BlockSpec((1, rows, MID), lambda m: (m, 0, 0)),
            pl.BlockSpec((1, rows, OUT), lambda m: (m, 0, 0)),
            pl.BlockSpec((1, 8, OUT), lambda m: (m, 0, 0)),
            pl.BlockSpec((MID, OUT), lambda m: (0, 0), pipeline_mode=pl.Buffered(1)),
        ],
        compiler_params=params_of(56),
        cost_estimate=cost(2 * micros * rows * MID * OUT, 18 << 20),
    )(hm, coef, wph, *[trunk] * len(trunk_pieces(ROW_COUT, ROW_SIDE)))


def pool_kernel(ho_ref, hs_ref, cf_ref, w_ref, out_ref):
    images = out_ref.shape[1]
    so, ss, shift = cf_ref[0, 0:1, :], cf_ref[0, 1:2, :], cf_ref[0, 2:3, :]

    def body(i, carry):
        total = []
        for k in range(8):
            at = pl.ds(pl.multiple_of(i * 128 + k * 16, 16), 16)
            j = ho_ref[0, at, :] * so + hs_ref[0, at, :] * ss + shift
            r = j * sigmoid(j) * w_ref[0, 0, at, :]
            total.append(jnp.sum(r, axis=0, keepdims=True))
        out_ref[0, pl.ds(pl.multiple_of(i * 8, 8), 8), :] = jnp.concatenate(total, axis=0)
        return carry

    lax.fori_loop(0, images // 8, body, 0)


def pool(ho, hs, coef, wph):
    micros, rows, _ = ho.shape
    n = 512
    images = rows // 16
    return pl.pallas_call(
        pool_kernel,
        grid=(micros, OUT // n),
        out_shape=jax.ShapeDtypeStruct((micros, images, OUT), F32),
        in_specs=[
            pl.BlockSpec((1, rows, n), lambda m, k: (m, 0, k)),
            pl.BlockSpec((1, rows, n), lambda m, k: (m, 0, k)),
            pl.BlockSpec((1, 8, n), lambda m, k: (m, 0, k)),
            pl.BlockSpec((1, 1, rows, 1), lambda m, k: (m, 0, 0, 0)),
        ],
        out_specs=pl.BlockSpec((1, images, n), lambda m, k: (m, 0, k)),
        compiler_params=params_of(56, 2),
        cost_estimate=cost(20 * micros * rows * OUT, 18 << 20),
    )(ho, hs, coef, wph)


def slope_kernel(ho_ref, hs_ref, cf_ref, w_ref, out_ref):
    images = out_ref.shape[2]
    so, ss, shift = cf_ref[0, 0:1, :], cf_ref[0, 1:2, :], cf_ref[0, 2:3, :]

    def body(i, carry):
        plain, out, side = [], [], []
        for k in range(8):
            at = pl.ds(pl.multiple_of(i * 128 + k * 16, 16), 16)
            ho, hs = ho_ref[0, at, :], hs_ref[0, at, :]
            j = ho * so + hs * ss + shift
            s = sigmoid(j)
            d = s * (1.0 + j * (1.0 - s)) * w_ref[0, 0, at, :]
            plain.append(jnp.sum(d, axis=0, keepdims=True))
            out.append(jnp.sum(d * ho, axis=0, keepdims=True))
            side.append(jnp.sum(d * hs, axis=0, keepdims=True))
        at = pl.ds(pl.multiple_of(i * 8, 8), 8)
        for k, value in enumerate((plain, out, side)):
            out_ref[0, k, at, :] = jnp.concatenate(value, axis=0)
        return carry

    lax.fori_loop(0, images // 8, body, 0)


def slopes(ho, hs, coef, wph):
    micros, rows, _ = ho.shape
    n = 512
    images = rows // 16
    return pl.pallas_call(
        slope_kernel,
        grid=(micros, OUT // n),
        out_shape=jax.ShapeDtypeStruct((micros, 3, images, OUT), F32),
        in_specs=[
            pl.BlockSpec((1, rows, n), lambda m, k: (m, 0, k)),
            pl.BlockSpec((1, rows, n), lambda m, k: (m, 0, k)),
            pl.BlockSpec((1, 8, n), lambda m, k: (m, 0, k)),
            pl.BlockSpec((1, 1, rows, 1), lambda m, k: (m, 0, 0, 0)),
        ],
        out_specs=pl.BlockSpec((1, 3, images, n), lambda m, k: (m, 0, 0, k)),
        compiler_params=params_of(56, 2),
        cost_estimate=cost(30 * micros * rows * OUT, 20 << 20),
    )(ho, hs, coef, wph)


def back_out_kernel(
    ho_ref, hs_ref, gs_ref, cf_ref, w_ref, am_ref, xe_ref, wo_ref, hm_ref, cm_ref,
    d_ref, st_ref, gw_ref, amt, xet, da, dho, dhs, acc_out, acc_side,
):
    micro, part = pl.program_id(0), pl.program_id(1)
    parts = pl.num_programs(1)
    images = gs_ref.shape[1]

    @pl.when(part == 0)
    def _():
        amt[...] = am_ref[0].T
        xet[...] = xe_ref[0].T

    cf = [cf_ref[0, k : k + 1, :] for k in range(7)]

    def body(i, carry):
        gs = gs_ref[0, pl.ds(pl.multiple_of(i * 8, 8), 8), :]
        for k in range(8):
            at = pl.ds(pl.multiple_of(i * 128 + k * 16, 16), 16)
            ho, hs = ho_ref[0, at, :], hs_ref[0, at, :]
            w = w_ref[0, 0, at, :]
            j = ho * cf[0] + hs * cf[1] + cf[2]
            s = sigmoid(j)
            g = s * (1.0 + j * (1.0 - s)) * gs[k : k + 1, :]
            dho[at, :] = ((g * cf[0] + cf[3] + ho * cf[4]) * w).astype(BF16)
            dhs[at, :] = ((g * cf[1] + cf[5] + hs * cf[6]) * w).astype(BF16)
        return carry

    lax.fori_loop(0, images // 8, body, 0)
    g_out = dot(amt[...], dho[...])
    g_side = dot(xet[...], dhs[...])
    back = dot_nt(dho[...], wo_ref[...])

    @pl.when(micro == 0)
    def _():
        acc_out[part] = g_out
        acc_side[part] = g_side

    @pl.when(micro > 0)
    def _():
        acc_out[part] += g_out
        acc_side[part] += g_side

    @pl.when(part == 0)
    def _():
        da[...] = back

    @pl.when(part > 0)
    def _():
        da[...] += back

    @pl.when(part == parts - 1)
    def _():
        hm = hm_ref[0]
        v = hm * cm_ref[0, 0:1, :] + cm_ref[0, 1:2, :]
        s = sigmoid(v)
        d = s * (1.0 + v * (1.0 - s)) * da[...] * w_ref[0, 0]
        d_ref[0] = d
        st_ref[...] = jnp.zeros_like(st_ref)
        st_ref[0, 0:1, :] = jnp.sum(d, axis=0, keepdims=True)
        st_ref[0, 1:2, :] = jnp.sum(d * hm, axis=0, keepdims=True)

    @pl.when((micro == pl.num_programs(0) - 1) & (part == parts - 1))
    def _():
        for k in range(4):
            for half in range(2):
                lanes = slice(half * 256, half * 256 + 256)
                gw_ref[2 * k + half, 0:MID, :] = acc_out[k, :, lanes].astype(BF16)
                gw_ref[2 * k + half, MID:, :] = acc_side[k, :, lanes].astype(BF16)


def back_out(ho, hs, gs, coef, wph, am, xe, weight, hm, coef_mid):
    micros, rows, _ = ho.shape
    n = 512
    images = rows // 16
    return pl.pallas_call(
        back_out_kernel,
        grid=(micros, OUT // n),
        out_shape=[
            jax.ShapeDtypeStruct((micros, rows, MID), F32),
            jax.ShapeDtypeStruct((micros, 8, MID), F32),
            jax.ShapeDtypeStruct((LANES, GRAD_OUT, 256), BF16),
        ],
        in_specs=[
            pl.BlockSpec((1, rows, n), lambda m, k: (m, 0, k)),
            pl.BlockSpec((1, rows, n), lambda m, k: (m, 0, k)),
            pl.BlockSpec((1, images, n), lambda m, k: (m, 0, k)),
            pl.BlockSpec((1, 8, n), lambda m, k: (m, 0, k)),
            pl.BlockSpec((1, 1, rows, 1), lambda m, k: (m, 0, 0, 0)),
            pl.BlockSpec((1, rows, MID), lambda m, k: (m, 0, 0)),
            pl.BlockSpec((1, rows, D_IN), lambda m, k: (m, 0, 0)),
            pl.BlockSpec((MID, n), lambda m, k: (0, k)),
            pl.BlockSpec((1, rows, MID), lambda m, k: (m, 0, 0)),
            pl.BlockSpec((1, 8, MID), lambda m, k: (m, 0, 0)),
        ],
        out_specs=[
            pl.BlockSpec((1, rows, MID), lambda m, k: (m, 0, 0)),
            pl.BlockSpec((1, 8, MID), lambda m, k: (m, 0, 0)),
            whole_block((LANES, GRAD_OUT, 256)),
        ],
        scratch_shapes=[
            pltpu.VMEM((MID, rows), BF16),
            pltpu.VMEM((D_IN, rows), BF16),
            pltpu.VMEM((rows, MID), F32),
            pltpu.VMEM((rows, n), BF16),
            pltpu.VMEM((rows, n), BF16),
            pltpu.VMEM((OUT // n, MID, n), F32),
            pltpu.VMEM((OUT // n, D_IN, n), F32),
        ],
        compiler_params=params_of(60, 2),
        cost_estimate=cost(2 * micros * rows * OUT * (2 * MID + D_IN), 40 << 20),
    )(ho, hs, gs, coef, wph, am, xe, weight, hm, coef_mid)


def back_mid_kernel(
    hm_ref, d_ref, cm_ref, cols_ref, wb, h_ref, hh_ref, cf_ref, w_ref, wh_ref,
    din_ref, dh_ref, st_ref, gw_ref, dt, acc,
):
    micro = pl.program_id(0)
    images = h_ref.shape[2] // 16

    low = ((d_ref[0] * cm_ref[0, 0:1, :] + cm_ref[0, 1:2, :] + hm_ref[0] * cm_ref[0, 2:3, :]) * w_ref[0, 0]).astype(BF16)
    for tap in range(9):
        lanes = slice(tap * MID, (tap + 1) * MID)
        g = dot_tn(cols_ref[0, :, lanes], low)

        @pl.when(micro == 0)
        def _():
            for col in range(4):
                acc[col, lanes, :] = g[:, col * 128 : (col + 1) * 128]

        @pl.when(micro > 0)
        def _():
            for col in range(4):
                acc[col, lanes, :] += g[:, col * 128 : (col + 1) * 128]

    scale, shift = cf_ref[0, 0:1, :], cf_ref[0, 1:2, :]
    zero = jnp.zeros((8, MID), F32)

    def back(h, grad, w):
        v = h * scale + shift
        s = sigmoid(v)
        return s * (1.0 + v * (1.0 - s)) * grad * w

    def body(i, carry):
        total, product = carry
        at = pl.ds(pl.multiple_of(i * 16, 16), 16)
        half = pl.ds(pl.multiple_of(i * 8, 8), 8)
        near = pl.ds(pl.multiple_of((i % (images // 2)) * 16, 16), 16)
        t = [dt[k, near, :].reshape(2, 8, MID) for k in range(9)]
        below1 = t[1]
        below3 = t[2] + shift_left(t[0])
        last = jnp.zeros((1, 8, MID), F32)
        grads = [
            t[4],
            t[5] + shift_left(t[3]),
            t[7] + jnp.concatenate([below1[1:], last], axis=0),
            t[8] + shift_left(t[6]) + jnp.concatenate([below3[1:], last], axis=0),
        ]
        for k in range(4):
            h = h_ref[0, k, at, :]
            d = back(h, grads[k].reshape(16, MID), w_ref[0, k, at, :])
            din_ref[0, k, at, :] = d.astype(BF16)
            total = total + fold(d)
            product = product + fold(d * h)
        for k, grad in enumerate((below1, below3)):
            h = hh_ref[0, k, half, :]
            d = back(h, grad[0], wh_ref[0, k, half, :])
            dh_ref[0, k, half, :] = d
            total = total + d
            product = product + d * h
        return total, product

    found = (zero, zero)
    for part in range(2):
        start, stop = part * images // 2, (part + 1) * images // 2
        for tap in range(9):
            dt[tap] = dot_nt(low[start * 16 : stop * 16], wb[tap * MID : (tap + 1) * MID, :])
        found = lax.fori_loop(start, stop, body, found)
    total, product = found
    st_ref[...] = jnp.zeros_like(st_ref)
    st_ref[0, 0:1, :] = jnp.sum(total, axis=0, keepdims=True)
    st_ref[0, 1:2, :] = jnp.sum(product, axis=0, keepdims=True)

    @pl.when(micro == pl.num_programs(0) - 1)
    def _():
        for k in range(LANES):
            for half in range(2):
                found = acc[(k % 2) * 2 + half, pl.ds(k // 2, GRAD_MID, stride=4), :]
                gw_ref[k, :, half * 128 : half * 128 + 128] = found.astype(BF16)


def back_mid(hm, d, coef_mid, cols, weight, h, hh, coef, wph, whalo):
    micros, _, rows, _ = h.shape
    return pl.pallas_call(
        back_mid_kernel,
        grid=(micros,),
        out_shape=[
            jax.ShapeDtypeStruct((micros, 4, rows, MID), BF16),
            jax.ShapeDtypeStruct((micros, 2, rows // 2, MID), F32),
            jax.ShapeDtypeStruct((micros, 8, MID), F32),
            jax.ShapeDtypeStruct((LANES, GRAD_MID, 256), BF16),
        ],
        in_specs=[
            pl.BlockSpec((1, rows, MID), lambda m: (m, 0, 0)),
            pl.BlockSpec((1, rows, MID), lambda m: (m, 0, 0)),
            pl.BlockSpec((1, 8, MID), lambda m: (m, 0, 0)),
            pl.BlockSpec((1, rows, 9 * MID), lambda m: (m, 0, 0)),
            pl.BlockSpec((9 * MID, MID), lambda m: (0, 0), pipeline_mode=pl.Buffered(1)),
            pl.BlockSpec((1, 4, rows, MID), lambda m: (m, 0, 0, 0)),
            pl.BlockSpec((1, 2, rows // 2, MID), lambda m: (m, 0, 0, 0)),
            pl.BlockSpec((1, 8, MID), lambda m: (m, 0, 0)),
            pl.BlockSpec((1, 4, rows, 1), lambda m: (m, 0, 0, 0)),
            pl.BlockSpec((1, 2, rows // 2, 1), lambda m: (m, 0, 0, 0)),
        ],
        out_specs=[
            pl.BlockSpec((1, 4, rows, MID), lambda m: (m, 0, 0, 0)),
            pl.BlockSpec((1, 2, rows // 2, MID), lambda m: (m, 0, 0, 0)),
            pl.BlockSpec((1, 8, MID), lambda m: (m, 0, 0)),
            pl.BlockSpec((LANES, GRAD_MID, 256), lambda m: (0, 0, 0), pipeline_mode=pl.Buffered(1)),
        ],
        scratch_shapes=[
            pltpu.VMEM((9, rows // 2, MID), F32),
            pltpu.VMEM((4, 9 * MID, 128), F32),
        ],
        compiler_params=params_of(62),
        cost_estimate=cost(4 * micros * rows * 9 * MID * MID, 60 << 20),
    )(hm, d, coef_mid, cols, weight, h, hh, coef, wph, whalo)


def back_in_kernel(h_ref, din_ref, dh_ref, cf_ref, w_ref, wh_ref, x_ref, xh_ref, gw_ref, ds, acc, turned):
    micro, part = pl.program_id(0), pl.program_id(1)
    images = h_ref.shape[2] // 16
    ca, cb, cc = cf_ref[0, 0:1, :], cf_ref[0, 1:2, :], cf_ref[0, 2:3, :]

    def body(i, carry):
        at = pl.ds(pl.multiple_of(i * 16, 16), 16)
        half = pl.ds(pl.multiple_of(i * 8, 8), 8)
        for k in range(4):
            h = h_ref[0, k, at, :]
            d = (din_ref[0, k, at, :].astype(F32) * ca + cb + h * cc) * w_ref[0, k, at, :]
            row, side = k // 2, k % 2
            for o in range(2):
                for col in range(4):
                    to = pl.ds(i * 64 + (2 * o + row) * 16 + side, 8, stride=2)
                    ds[col, to, :] = d[o * 8 : o * 8 + 8, col * 128 : (col + 1) * 128]
        for side in range(2):
            d = dh_ref[0, side, half, :] * ca
            for col in range(4):
                ds[col, pl.ds(images * 64 + i * 16 + side, 8, stride=2), :] = d[:, col * 128 : (col + 1) * 128]
        return carry

    lax.fori_loop(0, images, body, 0)
    low = jnp.concatenate([ds[col].astype(BF16) for col in range(4)], axis=1)
    g = dot_tn(low[: images * 64], x_ref[0]) + dot_tn(low[images * 64 :], xh_ref[0])

    @pl.when((micro == 0) & (part == 0))
    def _():
        acc[...] = g

    @pl.when((micro > 0) | (part > 0))
    def _():
        acc[...] += g

    @pl.when((micro == pl.num_programs(0) - 1) & (part == pl.num_programs(1) - 1))
    def _():
        for col in range(4):
            turned[col] = acc[col * 128 : (col + 1) * 128, :].T
        for k in range(LANES):
            for half in range(2):
                found = turned[(k % 2) * 2 + half, pl.ds(k // 2, D_IN // 4, stride=4), :]
                gw_ref[k, :, half * 128 : half * 128 + 128] = found.astype(BF16)


def back_in(h, din, dhalo, coef, wph, whalo, x, xh):
    micros, _, rows, _ = h.shape
    parts = 2
    r = rows // parts
    return pl.pallas_call(
        back_in_kernel,
        grid=(micros, parts),
        out_shape=jax.ShapeDtypeStruct((LANES, 256, 256), BF16),
        in_specs=[
            pl.BlockSpec((1, 4, r, MID), lambda m, k: (m, 0, k, 0)),
            pl.BlockSpec((1, 4, r, MID), lambda m, k: (m, 0, k, 0)),
            pl.BlockSpec((1, 2, r // 2, MID), lambda m, k: (m, 0, k, 0)),
            pl.BlockSpec((1, 8, MID), lambda m, k: (m, 0, 0)),
            pl.BlockSpec((1, 4, r, 1), lambda m, k: (m, 0, k, 0)),
            pl.BlockSpec((1, 2, r // 2, 1), lambda m, k: (m, 0, k, 0)),
            pl.BlockSpec((1, r * 4, D_IN), lambda m, k: (m, k, 0)),
            pl.BlockSpec((1, r, D_IN), lambda m, k: (m, k, 0)),
        ],
        out_specs=whole_block((LANES, 256, 256)),
        scratch_shapes=[
            pltpu.VMEM((4, r * 5, 128), F32),
            pltpu.VMEM((MID, D_IN), F32),
            pltpu.VMEM((4, D_IN, 128), F32),
        ],
        compiler_params=params_of(60, 2),
        cost_estimate=cost(2 * micros * rows * 5 * D_IN * MID, 50 << 20),
    )(h, din, dhalo, coef, wph, whalo, x, xh)


def swap(value, axis, bit):
    size = lax.axis_size(axis)
    return lax.ppermute(value, axis, [(i, i ^ bit) for i in range(size)])


def bits_of(axis):
    size, bit, found = lax.axis_size(axis), 1, []
    while bit < size:
        found.append(bit)
        bit *= 2
    return found


def add_all(value, axes=("c", "x", "p", "g")):
    for axis in axes:
        for bit in bits_of(axis):
            value = value + swap(value, axis, bit)
    return value


def exchange_planes(value):
    planes = lax.axis_size("g")
    here = lax.axis_index("g")
    own = lax.dynamic_index_in_dim(value, here, 0, keepdims=True)
    result = lax.dynamic_update_slice_in_dim(jnp.zeros_like(value), own, here, 0)
    for step in range(1, planes):
        block = lax.dynamic_index_in_dim(value, (here + step) % planes, 0, keepdims=True)
        got = lax.ppermute(block, "g", [(i, (i + step) % planes) for i in range(planes)])
        result = lax.dynamic_update_slice_in_dim(result, got, (here + planes - step) % planes, 0)
    return result


def gather_axis(value, axis):
    value = value[None]
    for bit in bits_of(axis):
        other = swap(value, axis, bit)
        mine = (lax.axis_index(axis) // bit) % 2
        value = jnp.where(mine == 0, jnp.concatenate([value, other]), jnp.concatenate([other, value]))
    return value


def to_heads(value):
    routed = exchange_planes(value)
    for axis in ("p", "x", "c"):
        routed = gather_axis(routed, axis)
    order = (3, 2, 1, 0, 4) + tuple(range(5, routed.ndim))
    routed = jnp.transpose(routed, order)
    return routed.reshape((-1,) + value.shape[2:])


def halve(value, axis, dim):
    own = lax.axis_index(axis)
    keep = lax.dynamic_index_in_dim(value, own, dim, keepdims=False)
    send = lax.dynamic_index_in_dim(value, 1 - own, dim, keepdims=False)
    return keep + swap(send, axis, 1)


def plane_reduce(value):
    half = value.shape[1] // 2
    value = halve(value.reshape((2, 2, 2) + value.shape[1:]), "c", 2)
    a = halve(halve(value[:, :, :half], "x", 1), "p", 0)
    b = halve(halve(value[:, :, half:], "p", 0), "x", 0)
    return jnp.concatenate([a, b], axis=0)


def to_plane(value, first, steps=(1, 2)):
    for step in steps:
        pairs = [(i ^ step, i) for i in range(GROUPS) if step == 1 and i % 2 == first or i == first]
        value = value + lax.ppermute(value, "g", pairs)
    return value


def spread_trunk(block, plane, plane_rows):
    planes = lax.axis_size("g")
    result = None
    for target in range(planes):
        parts = []
        for source in range(planes):
            low = max(target * GROUP, source * plane_rows)
            high = min((target + 1) * GROUP, (source + 1) * plane_rows)
            if low < high:
                piece = block[low - source * plane_rows : high - source * plane_rows]
                parts.append(piece if source == target else lax.ppermute(piece, "g", [(source, target)]))
        whole = parts[0] if len(parts) == 1 else jnp.concatenate(parts, axis=0)
        result = whole if result is None else jnp.where(plane == target, whole, result)
    return result


def first_rows_everywhere(block, plane, plane_rows):
    last = lax.axis_size("g") - 1
    at = ROW_VEC - last * plane_rows
    send = jnp.concatenate([block[:ROW_CMID], block[at : at + 16]], axis=0)
    first, vec = send[:ROW_CMID], send[ROW_CMID:]
    for target in range(1, last + 1):
        pairs = [(0, target), (last, last - target)]
        got = lax.ppermute(send, "g", pairs)
        first = jnp.where(plane == target, got[:ROW_CMID], first)
        vec = jnp.where(plane == last - target, got[ROW_CMID:], vec)
    rows = jnp.concatenate([first, vec], axis=0)
    for axis in PLANE:
        rows = gather_axis(rows, axis)
    rows = jnp.transpose(rows, (3, 2, 1, 0, 4)).reshape(-1, 2048)
    return rows[:ROW_CMID], rows[ROW_CMID:]


def norm_ranges():
    widths = [MID, MID, OUT, OUT, OUT, OUT, OUT, PRED]
    return [(sum(widths[:layer]), widths[layer]) for layer in range(8)]


def silu_back(value, grad):
    gate = jax.nn.sigmoid(value)
    return grad * gate * (1.0 + value * (1.0 - gate))


def head_norm(hidden, gamma, beta):
    count = hidden.shape[0]
    average = jnp.sum(hidden, axis=0) / count
    variance = jnp.sum(hidden * hidden, axis=0) / count - average * average
    scale = lax.rsqrt(variance + EPS_NORM)
    normed = (hidden - average) * scale
    return gamma * normed + beta, (normed, scale), average, variance


def head_norm_back(grad, kept, gamma):
    normed, scale = kept
    count = grad.shape[0]
    beta_sum = jnp.sum(grad, axis=0)
    gamma_sum = jnp.sum(grad * normed, axis=0)
    back = gamma * scale * (grad - beta_sum / count - normed * gamma_sum / count)
    return back, gamma_sum, beta_sum


def heads(pooled_low, wall, gammas, betas, bias, partner, live):
    project = [wall[ROW_PROJ + 2048 * k : ROW_PROJ + 2048 * (k + 1)] for k in range(3)]
    predict_in = wall[ROW_PIN:ROW_POUT].reshape(OUT, PRED)
    predict_out = wall[ROW_POUT:ROW_VEC]
    means, variances, kept_all, normed_all, lows = [], [], [], [], []
    low = pooled_low
    for k in range(3):
        normed, kept, mean, variance = head_norm(dot(low, project[k]), gammas[4 + k], betas[4 + k])
        means.append(mean)
        variances.append(variance)
        kept_all.append(kept)
        normed_all.append(normed)
        lows.append(low)
        low = (jax.nn.silu(normed) if k < 2 else normed).astype(BF16)
    latent, latent_low = normed, low
    normed_q, kept_q, mean, variance = head_norm(dot(latent_low, predict_in), gammas[7], betas[7])
    means.append(mean)
    variances.append(variance)
    act = jax.nn.silu(normed_q).astype(BF16)
    predicted = dot(act, predict_out) + bias
    choose = (partner[:, None] == jnp.arange(latent.shape[0])[None, :]).astype(F32)
    target = jnp.dot(choose, latent, precision=lax.Precision.HIGHEST)
    inner = jnp.sum(predicted * target, axis=-1)
    inv_pred = lax.rsqrt(jnp.sum(predicted * predicted, axis=-1) + COS_EPS)
    inv_goal = lax.rsqrt(jnp.sum(target * target, axis=-1) + COS_EPS)
    flags = live.astype(F32)
    loss_sum = -jnp.sum(flags * inner * inv_pred * inv_goal)
    live_count = jnp.sum(flags)
    grad_cos = -flags / live_count
    grad_pred = grad_cos[:, None] * (
        target * (inv_pred * inv_goal)[:, None] - (inner * inv_pred**3 * inv_goal)[:, None] * predicted
    )
    grad_bias = jnp.sum(grad_pred, axis=0)
    low_p = grad_pred.astype(BF16)
    grad_act = dot_nt(low_p, predict_out)
    grad_q, gamma_q, beta_q = head_norm_back(silu_back(normed_q, grad_act), kept_q, gammas[7])
    low_q = grad_q.astype(BF16)
    grad_act = dot_nt(low_q, predict_in)
    low_f, gamma_sums, beta_sums = [None] * 3, [None] * 3, [None] * 3
    for k in (2, 1, 0):
        grad_normed = grad_act if k == 2 else silu_back(normed_all[k], grad_act)
        grad_hidden, gamma_sums[k], beta_sums[k] = head_norm_back(grad_normed, kept_all[k], gammas[4 + k])
        low_f[k] = grad_hidden.astype(BF16)
        grad_act = dot_nt(low_f[k], project[k])
    block = (lax.axis_index("p") % 2) * 4 + lax.axis_index("x") * 2 + lax.axis_index("c")

    def columns(v, start):
        return lax.dynamic_slice_in_dim(v, start, 256, 1)

    rows = [dot_tn(lows[k], columns(low_f[k], block * 256)).astype(BF16) for k in range(3)]
    g_in = dot_tn(latent_low, columns(low_q, (block % 2) * 256)).astype(BF16)
    rows.append(lax.dynamic_index_in_dim(g_in.reshape(PRED, 4, 256), block // 2, 1, keepdims=False))
    rows.append(dot_tn(act, columns(low_p, block * 256)).astype(BF16))
    vector = (gamma_sums + [gamma_q], beta_sums + [beta_q], grad_bias)
    return grad_act, jnp.concatenate(rows, axis=0), vector, block, loss_sum, live_count, means, variances


def place(values, size):
    flat, at = jnp.zeros((size,), F32), 0
    for value in values:
        flat = flat + jnp.pad(value, (at, size - at - value.shape[0]))
        at += value.shape[0]
    return flat


def norm_coefs(sums, total, gamma, beta):
    mean = sums[:, 0] / total[:, None]
    variance = sums[:, 1] / total[:, None] - mean * mean
    scale = lax.rsqrt(variance + EPS_NORM)
    a = gamma * scale
    return mean, variance, scale, a, beta - a * mean


def pack(rows):
    rows = list(rows) + [jnp.zeros_like(rows[0])] * (8 - len(rows))
    return jnp.stack(rows, axis=1)


def back_coefs(grad_sum, product_sum, mean, scale, a, total):
    gamma_sum = scale * (product_sum - mean * grad_sum)
    c = -a * scale * gamma_sum / total[:, None]
    b = -a * grad_sum / total[:, None] - c * mean
    return b, c, gamma_sum


def on_device(inputs, masks, partner, live, params, first, second, running):
    count = lax.axis_size(ALL)
    index = lax.axis_index(ALL)
    plane = lax.axis_index("g")
    own = params.shape[0] // 128
    micros, images, rows, width, _ = inputs.shape
    out_rows, out_cols = rows // 2, width // 2
    window_rows = -(-own // 256) * 16
    shift = window_rows * 16 - own
    plane_rows = window_rows * LANES
    near = (
        shift * count <= own
        and lax.axis_size("g") == GROUPS
        and lax.axis_size(PLANE) == LANES
        and ROW_COUT < plane_rows < ROW_PROJ <= 2 * plane_rows
        and window_rows - tail_rows(shift, count) < ROW_CMID <= window_rows
        and ROW_VEC % window_rows + 16 <= window_rows
        and ROW_VEC >= (lax.axis_size("g") - 1) * plane_rows
    )

    x = inputs.reshape(micros, images * rows * width, D_IN)
    x_last, mask_last = inputs[:, :, -1], masks[:, :, -1]
    mask = masks.astype(F32)
    split = mask.reshape(micros, images, out_rows, 2, out_cols, 2)
    wph = jnp.transpose(split, (0, 3, 5, 1, 2, 4)).reshape(micros, 4, -1, 1)
    around = [(i, i + 1) for i in range(lax.axis_size(("x", "c")) - 1)]
    total_in = jnp.sum(mask, axis=(1, 2, 3))
    image_pixels = jnp.sum(split[:, :, :, 0, :, 0], axis=(2, 3))
    total_out = jnp.sum(image_pixels, axis=1)
    chosen = jnp.stack([partner.astype(F32), live.astype(F32)], axis=-1)
    if near:
        window = flat_to_window(params, window_rows, shift, index, count)
        column = lax.all_to_all(window, PLANE, 1, 0, tiled=True)
        wide_in, vec = first_rows_everywhere(column, plane, plane_rows)
        trunk = spread_trunk(column, plane, plane_rows)
        trunk, x_last, wide_in = lax.optimization_barrier((trunk, x_last, wide_in))
        h, xe, st, w_first = conv_in(x, wph, wide_in)
        trunk = lax.all_gather(trunk, ALL, axis=0, tiled=False).reshape(GROUPS, LANES, GROUP, 256)
        st, image_pixels, chosen, mask_last = lax.optimization_barrier((st, image_pixels, chosen, mask_last))
    else:
        wall = lax.all_gather(params.astype(BF16), ALL, axis=0, tiled=True).reshape(-1, 2048)
        wide_in, vec = wall[:ROW_CMID], wall[ROW_VEC : ROW_VEC + 16]
        trunk = jnp.transpose(wall[:ROW_PROJ].reshape(GROUPS, GROUP, LANES, 256), (0, 2, 1, 3))
        h, xe, st, w_first = conv_in(x, wph, wide_in)

    x_halo = lax.ppermute(x_last, ("x", "c"), around).reshape(micros, images * width, D_IN)
    mask_halo = lax.ppermute(mask_last, ("x", "c"), around).astype(F32)
    image_pixels = add_all(image_pixels, ("c", "x"))
    chosen = to_heads(chosen)
    whalo = jnp.transpose(mask_halo.reshape(micros, images, out_cols, 2), (0, 3, 1, 2)).reshape(micros, 2, -1, 1)
    share_index = lax.axis_index(("x", "c"))

    pixels = jnp.broadcast_to(jnp.stack([total_in, total_out], axis=1)[..., None], (micros, 2, 128))
    sums = add_all(jnp.concatenate([st[:, :2], pixels], axis=2))
    total_in, total_out = sums[:, 0, MID], sums[:, 1, MID]
    sums = sums[..., :MID]
    hh = conv_in_halo(x_halo, w_first)
    if near:
        window, trunk, sums, hh, total_in, total_out, whalo, image_pixels, chosen = lax.optimization_barrier(
            (window, trunk, sums, hh, total_in, total_out, whalo, image_pixels, chosen)
        )
        wall = lax.all_gather(window, ALL, axis=0, tiled=True)

    vec = vec.astype(F32).reshape(-1)
    ranges = norm_ranges()
    gammas = [vec[start : start + n] for start, n in ranges]
    betas = [vec[NORM + start : NORM + start + n] for start, n in ranges]
    bias = vec[2 * NORM : 2 * NORM + OUT]

    mean_in, var_in, scale_in, a_in, b_in = norm_coefs(sums, total_in, gammas[0], betas[0])
    coef_in = pack([a_in, b_in])
    hs, st_side = conv_side(xe, trunk)
    cols, hm, st, w_mid = conv_mid(h, hh, coef_in, wph, whalo, trunk)
    sums = add_all(jnp.concatenate([st[:, :2], st_side[:, :2]], axis=2))
    mean_mid, var_mid, scale_mid, a_mid, b_mid = norm_coefs(sums[..., :MID], total_out, gammas[1], betas[1])
    mean_side, var_side, scale_side, a_side, b_side = norm_coefs(sums[..., MID:], total_out, gammas[3], betas[3])
    am, ho, st, w_out = conv_out(hm, pack([a_mid, b_mid]), wph, trunk)
    sums = add_all(st[:, :2])
    mean_out, var_out, scale_out, a_out, b_out = norm_coefs(sums, total_out, gammas[2], betas[2])
    coef_join = pack([a_out, a_side, b_out + b_side])
    pooled = pool(ho, hs, coef_join, wph)
    for axis in ("x", "c"):
        half = pooled.shape[1] // 2
        here = lax.axis_index(axis)
        keep = lax.dynamic_slice_in_dim(pooled, here * half, half, 1)
        send = lax.dynamic_slice_in_dim(pooled, (1 - here) * half, half, 1)
        pooled = keep + swap(send, axis, 1)
    share = pooled.shape[1]
    share_pixels = lax.dynamic_slice_in_dim(image_pixels, share_index * share, share, 1)
    pooled_low = to_heads((pooled / share_pixels[..., None]).astype(BF16))
    slope = slopes(ho, hs, coef_join, wph)
    pooled_low, slope = lax.optimization_barrier((pooled_low, slope))

    grad_pool, head_rows, head_vec, block, loss_sum, live_count, head_means, head_vars = heads(
        pooled_low, wall, gammas, betas, bias, chosen[:, 0].astype(jnp.int32), chosen[:, 1]
    )

    def vector_rows(gamma, beta, extra):
        return place(gamma + beta + [extra], 16 * 2048).astype(BF16).reshape(16, 2048)

    none_head = [jnp.zeros((n,), F32) for _, n in ranges[4:]]
    none_trunk = [jnp.zeros((n,), F32) for _, n in ranges[:4]]
    head_vector = vector_rows(none_trunk + head_vec[0], none_trunk + head_vec[1], head_vec[2])
    head_vector = lax.dynamic_slice_in_dim(head_vector, block * 256, 256, 1)

    head_stats = place(head_means + head_vars + [loss_sum[None], live_count[None]], 106 * 128).reshape(1, -1, 128)
    head_stats = exchange_planes(jnp.broadcast_to(head_stats, (micros,) + head_stats.shape[1:])).reshape(micros, -1)
    head_size = NORM - sum(n for _, n in ranges[:4])
    scalars = head_stats[:, 2 * head_size : 2 * head_size + 2]

    grad_pool = grad_pool.astype(BF16).reshape(lax.axis_size("g"), lax.axis_size("p"), images, OUT)
    grad_pool = lax.dynamic_index_in_dim(grad_pool, lax.axis_index("p"), 1, keepdims=False)
    gs = exchange_planes(grad_pool)
    if near:
        head_part = jnp.concatenate(
            [
                jnp.zeros((ROW_PROJ, 256), BF16),
                head_rows,
                head_vector,
                jnp.zeros((window_rows * count - ROW_VEC - 16, 256), BF16),
            ],
            axis=0,
        )
        head_part, gs, head_stats = lax.optimization_barrier((head_part, gs, head_stats))
        head_part = lax.psum_scatter(head_part, "g", scatter_dimension=0, tiled=True)
    gs = gs.astype(F32) / image_pixels[..., None]

    sums = add_all(jnp.sum(gs[:, None] * slope, axis=2))
    bo, co, gamma_out = back_coefs(sums[:, 0], sums[:, 1], mean_out, scale_out, a_out, total_out)
    bs, cs, gamma_side = back_coefs(sums[:, 0], sums[:, 2], mean_side, scale_side, a_side, total_out)
    beta_joined = sums[:, 0]
    coef_back = pack([a_out, a_side, b_out + b_side, bo, co, bs, cs])
    d_mid, st, g_out = back_out(
        ho, hs, gs, coef_back, wph, am, xe, w_out, hm, pack([a_mid, b_mid])
    )
    if near:
        head_part, g_out = lax.optimization_barrier((head_part, g_out))
        g_out = lax.psum_scatter(g_out, PLANE, scatter_dimension=0, tiled=False)
    sums = add_all(st[:, :2])
    bm, cm, gamma_mid = back_coefs(sums[:, 0], sums[:, 1], mean_mid, scale_mid, a_mid, total_out)
    beta_mid = sums[:, 0]
    d_in, d_halo, st, g_mid = back_mid(
        hm, d_mid, pack([a_mid, bm, cm]), cols, w_mid, h, hh, coef_in, wph, whalo
    )
    if near:
        g_mid, g_out = lax.optimization_barrier((g_mid, g_out))
        g_mid = lax.psum_scatter(g_mid, PLANE, scatter_dimension=0, tiled=False)
        out_first = to_plane(g_out[: plane_rows - ROW_COUT], 0, (1,))
        out_second = to_plane(g_out[plane_rows - ROW_COUT :], 1, (1,))
    sums = add_all(st[:, :2])
    bi, ci, gamma_in = back_coefs(sums[:, 0], sums[:, 1], mean_in, scale_in, a_in, total_in)
    beta_in = sums[:, 0]
    if near:
        bi, ci, out_first, out_second = lax.optimization_barrier((bi, ci, out_first, out_second))
        out_first, out_second = to_plane(out_first, 0, (2,)), to_plane(out_second, 1, (2,))
    g_in = back_in(h, d_in, d_halo, pack([a_in, bi, ci]), wph, whalo, x, x_halo)

    if near:
        g_in, g_mid, out_first, out_second = lax.optimization_barrier(
            (plane_reduce(g_in), g_mid, out_first, out_second)
        )
    trunk_gamma = [jnp.sum(v, axis=0) for v in (gamma_in, gamma_mid, gamma_out, gamma_side)]
    trunk_beta = [jnp.sum(v, axis=0) for v in (beta_in, beta_mid, beta_joined, beta_joined)]
    trunk_vector = vector_rows(trunk_gamma + none_head, trunk_beta + none_head, jnp.zeros((OUT,), F32))

    if near:
        def blank(n):
            return jnp.zeros((n, 256), BF16)

        first_rows = jnp.concatenate([blank(ROW_CMID), to_plane(g_mid, 0), out_first], axis=0)
        second_rows = jnp.concatenate([out_second, blank(plane_rows - out_second.shape[0])], axis=0)
        part = jnp.where(plane == 0, first_rows, jnp.where(plane == 1, head_part + second_rows, head_part))
        window = lax.all_to_all(part, PLANE, 0, 1, tiled=True)
        tail = tail_rows(shift, count)
        prev = lax.ppermute(window[window_rows - tail :], ALL, [(i, i + 1) for i in range(count - 1)])
        g_in = to_plane(g_in, 0)
        for axis in PLANE:
            g_in = gather_axis(g_in, axis)
        g_in = jnp.transpose(g_in, (3, 2, 1, 0, 4)).reshape(ROW_CMID, 2048)
        window = window.at[:ROW_CMID].add(jnp.where(index == 0, g_in, 0))
        prev = prev.at[: ROW_CMID - window_rows + tail].add(jnp.where(index == 1, g_in[window_rows - tail :], 0))
        at = ROW_VEC % window_rows
        window = window.at[at : at + 16].add(jnp.where(index == ROW_VEC // window_rows, trunk_vector, 0))
        new_params, new_first, new_second, new_copy = adam_from_window(
            window, prev, shift, index, params, first, second
        )
    else:
        alone = (lax.axis_index("p") < 2).astype(BF16)
        head_part = jnp.concatenate([head_rows, head_vector], axis=0) * alone
        head_part = lax.dynamic_update_slice(
            jnp.zeros((head_part.shape[0], 2048), BF16), head_part, (jnp.int32(0), (block * 256).astype(jnp.int32))
        )
        lone = (index == 0).astype(BF16)
        head_part = head_part.at[ROW_VEC - ROW_PROJ :].add(trunk_vector * lone)
        trunk = jnp.concatenate([g_in, g_mid, g_out], axis=1)
        trunk = jnp.transpose(trunk, (1, 0, 2)).reshape(-1, 2048)
        flat = jnp.concatenate([trunk, head_part], axis=0).reshape(-1)
        flat = flat[: params.shape[0] * count]
        grad = lax.psum_scatter(flat, ALL, scatter_dimension=0, tiled=True).astype(F32)
        new_params, new_first, new_second = adam(grad, params, first, second)
        new_copy = new_params.astype(BF16)

    averages = jnp.concatenate([mean_in, mean_mid, mean_out, mean_side, head_stats[:, :head_size]], axis=1)
    spreads = jnp.concatenate([var_in, var_mid, var_out, var_side, head_stats[:, head_size : 2 * head_size]], axis=1)
    stats = jnp.stack([averages, spreads], axis=1)
    new_running = running
    for micro in range(micros):
        new_running = (1.0 - MOMENTUM) * new_running + MOMENTUM * stats[micro]
    return (
        scalars[:, 0],
        scalars[:, 1].astype(jnp.int32),
        new_params,
        new_first,
        new_second,
        new_copy,
        new_running,
    )


def solution(mesh):
    img, rows = mesh.shape["img"], mesh.shape["rows"]
    fine = Mesh(mesh.devices.reshape(MB, img // MB, 2, rows // 2), ALL)
    split = P(ALL)
    placed = (
        P(None, ("g", "p"), ("x", "c"), None, None),
        P(None, ("g", "p"), ("x", "c"), None),
        P(None, ALL),
        P(None, ALL),
        split,
        split,
        split,
        P(),
    )
    return jax.shard_map(
        on_device,
        mesh=fine,
        in_specs=placed,
        out_specs=(P(), P(), split, split, split, split, P()),
        check_vma=False,
    )
```

```python
import jax
import jax.numpy as jnp
from jax import lax
from jax.experimental import pallas as pl
from jax.experimental.pallas import tpu as pltpu
from jax.sharding import Mesh, PartitionSpec as P

D_IN = 1024
MID = 512
OUT = 2048
PRED = 512
MB = 4
STEP = 5
NORM = 11776
PARAMS = 20734976

EPS_NORM = 1e-05
MOMENTUM = 0.1
RATE = 0.03
BETA_ONE = 0.5
BETA_TWO = 0.5
DECAY = 0.01
ADAM_EPS = 1e-08
COS_EPS = 1e-06

ROW_CIN, ROW_CMID, ROW_COUT, ROW_SIDE = 0, 256, 1408, 1920
ROW_PROJ, ROW_PIN, ROW_POUT, ROW_VEC = 2944, 9088, 9600, 10112
LANES = 8
GROUPS, GROUP = 4, 736
GRAD_OUT, GRAD_MID = 1536, 1152
ALL = ("g", "p", "x", "c")
PLANE = ("p", "x", "c")
F32, BF16 = jnp.float32, jnp.bfloat16
COST_SHARE = 8


def params_of(mib=60, steps=1):
    return pltpu.CompilerParams(
        vmem_limit_bytes=mib << 20, dimension_semantics=("arbitrary",) * steps
    )


def cost(flops, moved):
    return pl.CostEstimate(flops=flops // COST_SHARE, bytes_accessed=moved // COST_SHARE, transcendentals=0)


def whole_block(shape):
    zeros = (0,) * len(shape)
    return pl.BlockSpec(shape, lambda *_: zeros)


def sigmoid(v):
    return 1.0 / (1.0 + jnp.exp(-v))


def dot(a, b):
    return jnp.dot(a, b, preferred_element_type=F32)


def dot_nt(a, b):
    return lax.dot_general(a, b, (((1,), (1,)), ((), ())), preferred_element_type=F32)


def dot_tn(a, b):
    return lax.dot_general(a, b, (((0,), (0,)), ((), ())), preferred_element_type=F32)


def fold(v):
    return jnp.sum(v.reshape(-1, 8, v.shape[-1]), axis=0)


def unwide(wide_ref, scratch, out_ref):
    rows = wide_ref.shape[0]
    for part in range(4):
        for col in range(4):
            lanes = pl.ds(part * 512 + col * 128, 128)
            scratch[col, pl.ds(part, rows, stride=4), :] = wide_ref[:, lanes].astype(F32)
    for col in range(4):
        out_ref[:, col * 128 : (col + 1) * 128] = scratch[col].astype(BF16)


def trunk_pieces(start, stop):
    found = []
    for group in range(GROUPS):
        low, high = max(start, group * GROUP), min(stop, (group + 1) * GROUP)
        if low < high:
            found.append((group, low - group * GROUP, low - start, high - low))
    return found


def trunk_specs(start, stop):
    def spec(group):
        return pl.BlockSpec(
            (1, LANES, GROUP, 256), lambda *_: (group, 0, 0, 0), pipeline_mode=pl.Buffered(1)
        )

    return [spec(piece[0]) for piece in trunk_pieces(start, stop)]


def join_trunk(refs, start, stop, out_ref):
    for ref, (_, low, to, rows) in zip(refs, trunk_pieces(start, stop)):
        for block in range(LANES):
            out_ref[to : to + rows, block * 256 : block * 256 + 256] = ref[0, block, low : low + rows, :]


def unwide_trunk(refs, start, stop, scratch, out_ref):
    for ref, (_, low, to, rows) in zip(refs, trunk_pieces(start, stop)):
        for part in range(4):
            for col in range(4):
                block, lanes = 2 * part + col // 2, slice((col % 2) * 128, (col % 2) * 128 + 128)
                scratch[col, pl.ds(part + 4 * to, rows, stride=4), :] = ref[0, block, low : low + rows, lanes].astype(F32)
    for col in range(4):
        out_ref[:, col * 128 : (col + 1) * 128] = scratch[col].astype(BF16)


def window_kernel(off_ref, flat_ref, out_ref):
    off = off_ref[0]
    rows = out_ref.shape[0]
    for col in range(16):
        out_ref[:, col * 128 : (col + 1) * 128] = flat_ref[pl.ds(off + col, rows, stride=16), :].astype(BF16)


def flat_to_window(params, rows, shift, index, count):
    own = params.shape[0] // 128
    head = shift * count
    nxt = lax.ppermute(
        params[: head * 128].astype(BF16), ALL, [(i + 1, i) for i in range(count - 1)]
    )
    flat = jnp.concatenate([params, nxt.astype(F32), jnp.zeros((1024,), F32)]).reshape(-1, 128)
    return pl.pallas_call(
        window_kernel,
        out_shape=jax.ShapeDtypeStruct((rows, 2048), BF16),
        in_specs=[pl.BlockSpec(memory_space=pltpu.SMEM), whole_block((own + head + 8, 128))],
        out_specs=whole_block((rows, 2048)),
        compiler_params=pltpu.CompilerParams(vmem_limit_bytes=40 << 20),
    )((index * shift).astype(jnp.int32)[None], flat)


def adam(grad, params, first, second):
    new_first = BETA_ONE * first + (1.0 - BETA_ONE) * grad
    new_second = BETA_TWO * second + (1.0 - BETA_TWO) * grad * grad
    corrected_first = new_first / (1.0 - BETA_ONE**STEP)
    corrected_second = new_second / (1.0 - BETA_TWO**STEP)
    new_params = params - RATE * (
        corrected_first / (jnp.sqrt(corrected_second) + ADAM_EPS) + DECAY * params
    )
    return new_params, new_first, new_second


def adam_kernel(off_ref, tail_ref, win_ref, p_ref, m_ref, v_ref, po_ref, mo_ref, vo_ref, co_ref, flat):
    step = pl.program_id(0)

    @pl.when(step == 0)
    def _():
        tail = tail_ref.shape[0]
        rows = win_ref.shape[0]
        for col in range(16):
            lanes = pl.ds(col * 128, 128)
            flat[pl.ds(col, tail, stride=16), :] = tail_ref[:, lanes].astype(F32)
            flat[pl.ds(tail * 16 + col, rows, stride=16), :] = win_ref[:, lanes].astype(F32)

    size = p_ref.shape[0]
    grad = flat[pl.ds(off_ref[0] + step * size, size), :]
    po_ref[...], mo_ref[...], vo_ref[...] = adam(grad, p_ref[...], m_ref[...], v_ref[...])
    co_ref[...] = po_ref[...].astype(BF16)


def tail_rows(shift, count):
    return -(-shift * (count - 1) // 256) * 16


def adam_from_window(window, prev, shift, index, params, first, second):
    own = params.shape[0] // 128
    rows, tail = window.shape[0], prev.shape[0]
    block = 512
    steps = -(-own // block)
    assert steps * block <= rows * 16
    off = (tail * 16 - index * shift).astype(jnp.int32)[None]
    spec = pl.BlockSpec((block, 128), lambda i: (i, 0))
    shaped = [v.reshape(own, 128) for v in (params, first, second)]
    outs = pl.pallas_call(
        adam_kernel,
        grid=(steps,),
        out_shape=[jax.ShapeDtypeStruct((own, 128), F32)] * 3 + [jax.ShapeDtypeStruct((own, 128), BF16)],
        in_specs=[pl.BlockSpec(memory_space=pltpu.SMEM), whole_block((tail, 2048)), whole_block((rows, 2048))] + [spec] * 3,
        out_specs=[spec] * 4,
        scratch_shapes=[pltpu.VMEM(((tail + rows) * 16, 128), F32)],
        compiler_params=params_of(40),
    )(off, prev, window, *shaped)
    return [v.reshape(-1) for v in outs]


def conv_in_kernel(x_ref, w_ref, wide_ref, h_ref, xe_ref, st_ref, wb, wf, hs, xs):
    micro, part = pl.program_id(0), pl.program_id(1)

    @pl.when((micro == 0) & (part == 0))
    def _():
        unwide(wide_ref, wf, wb)

    images = x_ref.shape[1] // 64
    h = dot(x_ref[0], wb[...])
    for col in range(4):
        hs[col] = h[:, col * 128 : (col + 1) * 128]

    def body(i, carry):
        at = pl.multiple_of(i * 64, 64)
        low = pl.multiple_of(i * 16, 16)
        w = [jnp.broadcast_to(w_ref[0, k, pl.ds(low, 16), :], (16, 128)) for k in range(4)]
        new = []
        for col in range(4):
            lanes = slice(col * 128, (col + 1) * 128)
            total, square = carry[col]
            for side in range(2):
                half = hs[col, pl.ds(at + side, 32, stride=2), :].reshape(2, 2, 8, 128)
                for row in range(2):
                    h = half[:, row].reshape(16, 128) * w[2 * row + side]
                    total, square = total + fold(h), square + fold(h * h)
                    h_ref[0, 2 * row + side, pl.ds(low, 16), lanes] = h
            new.append((total, square))
        w = w[0]
        for col in range(8):
            lanes = slice(col * 128, (col + 1) * 128)
            for row in range(2):
                xs[col, row * 16 : row * 16 + 16, :] = x_ref[0, pl.ds(at + row * 32, 16), lanes].astype(F32)
            xe_ref[0, pl.ds(low, 16), lanes] = (xs[col, pl.ds(0, 16, stride=2), :] * w).astype(BF16)
        return tuple(new)

    zero = jnp.zeros((8, 128), F32)
    found = lax.fori_loop(0, images, body, ((zero, zero),) * 4)

    @pl.when(part == 0)
    def _():
        st_ref[...] = jnp.zeros_like(st_ref)

    for col in range(4):
        lanes = slice(col * 128, (col + 1) * 128)
        for k in range(2):
            st_ref[0, k : k + 1, lanes] += jnp.sum(found[col][k], axis=0, keepdims=True)


def conv_in(x, wph, wide):
    micros, pixels, _ = x.shape
    images = pixels // 64
    parts = 2
    b = images // parts
    return pl.pallas_call(
        conv_in_kernel,
        grid=(micros, parts),
        out_shape=[
            jax.ShapeDtypeStruct((micros, 4, images * 16, MID), F32),
            jax.ShapeDtypeStruct((micros, images * 16, D_IN), BF16),
            jax.ShapeDtypeStruct((micros, 8, MID), F32),
            jax.ShapeDtypeStruct((D_IN, MID), BF16),
        ],
        in_specs=[
            pl.BlockSpec((1, b * 64, D_IN), lambda m, k: (m, k, 0)),
            pl.BlockSpec((1, 4, b * 16, 1), lambda m, k: (m, 0, k, 0)),
            whole_block((256, 2048)),
        ],
        out_specs=[
            pl.BlockSpec((1, 4, b * 16, MID), lambda m, k: (m, 0, k, 0)),
            pl.BlockSpec((1, b * 16, D_IN), lambda m, k: (m, k, 0)),
            pl.BlockSpec((1, 8, MID), lambda m, k: (m, 0, 0)),
            whole_block((D_IN, MID)),
        ],
        scratch_shapes=[
            pltpu.VMEM((4, D_IN, 128), F32),
            pltpu.VMEM((4, b * 64, 128), F32),
            pltpu.VMEM((8, 32, 128), F32),
        ],
        compiler_params=params_of(56, 2),
        cost_estimate=cost(2 * micros * images * 64 * D_IN * MID, 40 << 20),
    )(x, wph, wide)


def halo_kernel(xh_ref, wb_ref, hh_ref, hs):
    h = dot(xh_ref[0], wb_ref[...])
    rows = hh_ref.shape[2]
    for col in range(4):
        lanes = slice(col * 128, (col + 1) * 128)
        hs[col] = h[:, lanes]
        for side in range(2):
            hh_ref[0, side, :, lanes] = hs[col, pl.ds(side, rows, stride=2), :]


def conv_in_halo(xh, weight):
    micros, pixels, _ = xh.shape
    return pl.pallas_call(
        halo_kernel,
        grid=(micros,),
        out_shape=jax.ShapeDtypeStruct((micros, 2, pixels // 2, MID), F32),
        in_specs=[pl.BlockSpec((1, pixels, D_IN), lambda m: (m, 0, 0)), whole_block((D_IN, MID))],
        out_specs=pl.BlockSpec((1, 2, pixels // 2, MID), lambda m: (m, 0, 0, 0)),
        scratch_shapes=[pltpu.VMEM((4, pixels, 128), F32)],
        compiler_params=params_of(40),
        cost_estimate=cost(2 * micros * pixels * D_IN * MID, 9 << 20),
    )(xh, weight)


def side_kernel(xe_ref, *refs):
    pieces, (hs_ref, st_ref, weight) = refs[:-3], refs[-3:]

    @pl.when((pl.program_id(0) == 0) & (pl.program_id(1) == 0))
    def _():
        join_trunk(pieces, ROW_SIDE, ROW_PROJ, weight)

    n = hs_ref.shape[2]
    h = dot(xe_ref[0], weight[:, pl.ds(pl.multiple_of(pl.program_id(1) * n, n), n)])
    hs_ref[0] = h
    st_ref[...] = jnp.zeros_like(st_ref)
    st_ref[0, 0:1, :] = jnp.sum(h, axis=0, keepdims=True)
    st_ref[0, 1:2, :] = jnp.sum(h * h, axis=0, keepdims=True)


def conv_side(xe, trunk):
    micros, rows, _ = xe.shape
    cols = 4
    n = OUT // cols
    return pl.pallas_call(
        side_kernel,
        grid=(micros, cols),
        out_shape=[
            jax.ShapeDtypeStruct((micros, rows, OUT), F32),
            jax.ShapeDtypeStruct((micros, 8, OUT), F32),
        ],
        in_specs=[
            pl.BlockSpec((1, rows, D_IN), lambda m, k: (m, 0, 0)),
        ]
        + trunk_specs(ROW_SIDE, ROW_PROJ),
        out_specs=[
            pl.BlockSpec((1, rows, n), lambda m, k: (m, 0, k)),
            pl.BlockSpec((1, 8, n), lambda m, k: (m, 0, k)),
        ],
        scratch_shapes=[pltpu.VMEM((D_IN, OUT), BF16)],
        compiler_params=params_of(56, 2),
        cost_estimate=cost(2 * micros * rows * D_IN * OUT, 16 << 20),
    )(xe, *[trunk] * len(trunk_pieces(ROW_SIDE, ROW_PROJ)))


def shift_right(v):
    moved = pltpu.roll(v, 1, 1)
    return jnp.where(lax.broadcasted_iota(jnp.int32, v.shape, 1) == 0, 0.0, moved)


def shift_left(v):
    moved = pltpu.roll(v, 7, 1)
    return jnp.where(lax.broadcasted_iota(jnp.int32, v.shape, 1) == 7, 0.0, moved)


def conv_mid_kernel(h_ref, hh_ref, cf_ref, w_ref, wh_ref, *refs):
    pieces, (cols_ref, hm_ref, st_ref, wb, wf) = refs[:-5], refs[-5:]
    micro = pl.program_id(0)

    @pl.when(micro == 0)
    def _():
        unwide_trunk(pieces, ROW_CMID, ROW_COUT, wf, wb)

    images = h_ref.shape[2] // 16
    scale, shift = cf_ref[0, 0:1, :], cf_ref[0, 1:2, :]

    def act(h, w):
        v = h * scale + shift
        return v * sigmoid(v) * w

    def body(i, carry):
        at = pl.ds(pl.multiple_of(i * 16, 16), 16)
        half = pl.ds(pl.multiple_of(i * 8, 8), 8)
        a = [act(h_ref[0, k, at, :], w_ref[0, k, at, :]).reshape(2, 8, MID) for k in range(4)]
        above = [act(hh_ref[0, k, half, :], wh_ref[0, k, half, :]).reshape(1, 8, MID) for k in range(2)]
        a1s, a3s = shift_right(a[1]), shift_right(a[3])
        up2 = jnp.concatenate([above[0], a[2][:1]], axis=0)
        up3 = jnp.concatenate([above[1], a[3][:1]], axis=0)
        up3s = jnp.concatenate([shift_right(above[1]), a3s[:1]], axis=0)
        for tap, value in enumerate([up3s, up2, up3, a1s, a[0], a[1], a3s, a[2], a[3]]):
            cols_ref[0, at, tap * MID : (tap + 1) * MID] = value.reshape(16, MID).astype(BF16)
        return carry

    lax.fori_loop(0, images, body, 0)
    h = dot(cols_ref[0], wb[...])
    hm_ref[0] = h
    hw = h * w_ref[0, 0]
    st_ref[...] = jnp.zeros_like(st_ref)
    st_ref[0, 0:1, :] = jnp.sum(hw, axis=0, keepdims=True)
    st_ref[0, 1:2, :] = jnp.sum(hw * hw, axis=0, keepdims=True)


def conv_mid(h, hh, coef, wph, whalo, trunk):
    micros, _, rows, _ = h.shape
    return pl.pallas_call(
        conv_mid_kernel,
        grid=(micros,),
        out_shape=[
            jax.ShapeDtypeStruct((micros, rows, 9 * MID), BF16),
            jax.ShapeDtypeStruct((micros, rows, MID), F32),
            jax.ShapeDtypeStruct((micros, 8, MID), F32),
            jax.ShapeDtypeStruct((9 * MID, MID), BF16),
        ],
        in_specs=[
            pl.BlockSpec((1, 4, rows, MID), lambda m: (m, 0, 0, 0)),
            pl.BlockSpec((1, 2, rows // 2, MID), lambda m: (m, 0, 0, 0)),
            pl.BlockSpec((1, 8, MID), lambda m: (m, 0, 0)),
            pl.BlockSpec((1, 4, rows, 1), lambda m: (m, 0, 0, 0)),
            pl.BlockSpec((1, 2, rows // 2, 1), lambda m: (m, 0, 0, 0)),
        ]
        + trunk_specs(ROW_CMID, ROW_COUT),
        out_specs=[
            pl.BlockSpec((1, rows, 9 * MID), lambda m: (m, 0, 0)),
            pl.BlockSpec((1, rows, MID), lambda m: (m, 0, 0)),
            pl.BlockSpec((1, 8, MID), lambda m: (m, 0, 0)),
            pl.BlockSpec((9 * MID, MID), lambda m: (0, 0), pipeline_mode=pl.Buffered(1)),
        ],
        scratch_shapes=[pltpu.VMEM((4, 9 * MID, 128), F32)],
        compiler_params=params_of(60),
        cost_estimate=cost(2 * micros * rows * 9 * MID * MID, 50 << 20),
    )(h, hh, coef, wph, whalo, *[trunk] * len(trunk_pieces(ROW_CMID, ROW_COUT)))


def conv_out_kernel(hm_ref, cf_ref, w_ref, *refs):
    pieces, (am_ref, ho_ref, st_ref, weight_ref) = refs[:-4], refs[-4:]

    @pl.when(pl.program_id(0) == 0)
    def _():
        join_trunk(pieces, ROW_COUT, ROW_SIDE, weight_ref)

    v = hm_ref[0] * cf_ref[0, 0:1, :] + cf_ref[0, 1:2, :]
    am = (v * sigmoid(v) * w_ref[0, 0]).astype(BF16)
    am_ref[0] = am
    st_ref[...] = jnp.zeros_like(st_ref)
    for k in range(4):
        lanes = slice(k * 512, (k + 1) * 512)
        h = dot(am, weight_ref[:, lanes])
        ho_ref[0, :, lanes] = h
        st_ref[0, 0:1, lanes] = jnp.sum(h, axis=0, keepdims=True)
        st_ref[0, 1:2, lanes] = jnp.sum(h * h, axis=0, keepdims=True)


def conv_out(hm, coef, wph, trunk):
    micros, rows, _ = hm.shape
    return pl.pallas_call(
        conv_out_kernel,
        grid=(micros,),
        out_shape=[
            jax.ShapeDtypeStruct((micros, rows, MID), BF16),
            jax.ShapeDtypeStruct((micros, rows, OUT), F32),
            jax.ShapeDtypeStruct((micros, 8, OUT), F32),
            jax.ShapeDtypeStruct((MID, OUT), BF16),
        ],
        in_specs=[
            pl.BlockSpec((1, rows, MID), lambda m: (m, 0, 0)),
            pl.BlockSpec((1, 8, MID), lambda m: (m, 0, 0)),
            pl.BlockSpec((1, 1, rows, 1), lambda m: (m, 0, 0, 0)),
        ]
        + trunk_specs(ROW_COUT, ROW_SIDE),
        out_specs=[
            pl.BlockSpec((1, rows, MID), lambda m: (m, 0, 0)),
            pl.BlockSpec((1, rows, OUT), lambda m: (m, 0, 0)),
            pl.BlockSpec((1, 8, OUT), lambda m: (m, 0, 0)),
            pl.BlockSpec((MID, OUT), lambda m: (0, 0), pipeline_mode=pl.Buffered(1)),
        ],
        compiler_params=params_of(56),
        cost_estimate=cost(2 * micros * rows * MID * OUT, 18 << 20),
    )(hm, coef, wph, *[trunk] * len(trunk_pieces(ROW_COUT, ROW_SIDE)))


def pool_kernel(ho_ref, hs_ref, cf_ref, w_ref, out_ref):
    images = out_ref.shape[1]
    so, ss, shift = cf_ref[0, 0:1, :], cf_ref[0, 1:2, :], cf_ref[0, 2:3, :]

    def body(i, carry):
        total = []
        for k in range(8):
            at = pl.ds(pl.multiple_of(i * 128 + k * 16, 16), 16)
            j = ho_ref[0, at, :] * so + hs_ref[0, at, :] * ss + shift
            r = j * sigmoid(j) * w_ref[0, 0, at, :]
            total.append(jnp.sum(r, axis=0, keepdims=True))
        out_ref[0, pl.ds(pl.multiple_of(i * 8, 8), 8), :] = jnp.concatenate(total, axis=0)
        return carry

    lax.fori_loop(0, images // 8, body, 0)


def pool(ho, hs, coef, wph):
    micros, rows, _ = ho.shape
    n = 512
    images = rows // 16
    return pl.pallas_call(
        pool_kernel,
        grid=(micros, OUT // n),
        out_shape=jax.ShapeDtypeStruct((micros, images, OUT), F32),
        in_specs=[
            pl.BlockSpec((1, rows, n), lambda m, k: (m, 0, k)),
            pl.BlockSpec((1, rows, n), lambda m, k: (m, 0, k)),
            pl.BlockSpec((1, 8, n), lambda m, k: (m, 0, k)),
            pl.BlockSpec((1, 1, rows, 1), lambda m, k: (m, 0, 0, 0)),
        ],
        out_specs=pl.BlockSpec((1, images, n), lambda m, k: (m, 0, k)),
        compiler_params=params_of(56, 2),
        cost_estimate=cost(20 * micros * rows * OUT, 18 << 20),
    )(ho, hs, coef, wph)


def slope_kernel(ho_ref, hs_ref, cf_ref, w_ref, out_ref):
    images = out_ref.shape[2]
    so, ss, shift = cf_ref[0, 0:1, :], cf_ref[0, 1:2, :], cf_ref[0, 2:3, :]

    def body(i, carry):
        plain, out, side = [], [], []
        for k in range(8):
            at = pl.ds(pl.multiple_of(i * 128 + k * 16, 16), 16)
            ho, hs = ho_ref[0, at, :], hs_ref[0, at, :]
            j = ho * so + hs * ss + shift
            s = sigmoid(j)
            d = s * (1.0 + j * (1.0 - s)) * w_ref[0, 0, at, :]
            plain.append(jnp.sum(d, axis=0, keepdims=True))
            out.append(jnp.sum(d * ho, axis=0, keepdims=True))
            side.append(jnp.sum(d * hs, axis=0, keepdims=True))
        at = pl.ds(pl.multiple_of(i * 8, 8), 8)
        for k, value in enumerate((plain, out, side)):
            out_ref[0, k, at, :] = jnp.concatenate(value, axis=0)
        return carry

    lax.fori_loop(0, images // 8, body, 0)


def slopes(ho, hs, coef, wph):
    micros, rows, _ = ho.shape
    n = 512
    images = rows // 16
    return pl.pallas_call(
        slope_kernel,
        grid=(micros, OUT // n),
        out_shape=jax.ShapeDtypeStruct((micros, 3, images, OUT), F32),
        in_specs=[
            pl.BlockSpec((1, rows, n), lambda m, k: (m, 0, k)),
            pl.BlockSpec((1, rows, n), lambda m, k: (m, 0, k)),
            pl.BlockSpec((1, 8, n), lambda m, k: (m, 0, k)),
            pl.BlockSpec((1, 1, rows, 1), lambda m, k: (m, 0, 0, 0)),
        ],
        out_specs=pl.BlockSpec((1, 3, images, n), lambda m, k: (m, 0, 0, k)),
        compiler_params=params_of(56, 2),
        cost_estimate=cost(30 * micros * rows * OUT, 20 << 20),
    )(ho, hs, coef, wph)


def back_out_kernel(
    ho_ref, hs_ref, gs_ref, cf_ref, w_ref, am_ref, xe_ref, wo_ref, hm_ref, cm_ref,
    d_ref, st_ref, gw_ref, amt, xet, da, dho, dhs, acc_out, acc_side,
):
    micro, part = pl.program_id(0), pl.program_id(1)
    parts = pl.num_programs(1)
    images = gs_ref.shape[1]

    @pl.when(part == 0)
    def _():
        amt[...] = am_ref[0].T
        xet[...] = xe_ref[0].T

    cf = [cf_ref[0, k : k + 1, :] for k in range(7)]

    def body(i, carry):
        gs = gs_ref[0, pl.ds(pl.multiple_of(i * 8, 8), 8), :]
        for k in range(8):
            at = pl.ds(pl.multiple_of(i * 128 + k * 16, 16), 16)
            ho, hs = ho_ref[0, at, :], hs_ref[0, at, :]
            w = w_ref[0, 0, at, :]
            j = ho * cf[0] + hs * cf[1] + cf[2]
            s = sigmoid(j)
            g = s * (1.0 + j * (1.0 - s)) * gs[k : k + 1, :]
            dho[at, :] = ((g * cf[0] + cf[3] + ho * cf[4]) * w).astype(BF16)
            dhs[at, :] = ((g * cf[1] + cf[5] + hs * cf[6]) * w).astype(BF16)
        return carry

    lax.fori_loop(0, images // 8, body, 0)
    g_out = dot(amt[...], dho[...])
    g_side = dot(xet[...], dhs[...])
    back = dot_nt(dho[...], wo_ref[...])

    @pl.when(micro == 0)
    def _():
        acc_out[part] = g_out
        acc_side[part] = g_side

    @pl.when(micro > 0)
    def _():
        acc_out[part] += g_out
        acc_side[part] += g_side

    @pl.when(part == 0)
    def _():
        da[...] = back

    @pl.when(part > 0)
    def _():
        da[...] += back

    @pl.when(part == parts - 1)
    def _():
        hm = hm_ref[0]
        v = hm * cm_ref[0, 0:1, :] + cm_ref[0, 1:2, :]
        s = sigmoid(v)
        d = s * (1.0 + v * (1.0 - s)) * da[...] * w_ref[0, 0]
        d_ref[0] = d
        st_ref[...] = jnp.zeros_like(st_ref)
        st_ref[0, 0:1, :] = jnp.sum(d, axis=0, keepdims=True)
        st_ref[0, 1:2, :] = jnp.sum(d * hm, axis=0, keepdims=True)

    @pl.when((micro == pl.num_programs(0) - 1) & (part == parts - 1))
    def _():
        for k in range(4):
            for half in range(2):
                lanes = slice(half * 256, half * 256 + 256)
                gw_ref[2 * k + half, 0:MID, :] = acc_out[k, :, lanes].astype(BF16)
                gw_ref[2 * k + half, MID:, :] = acc_side[k, :, lanes].astype(BF16)


def back_out(ho, hs, gs, coef, wph, am, xe, weight, hm, coef_mid):
    micros, rows, _ = ho.shape
    n = 512
    images = rows // 16
    return pl.pallas_call(
        back_out_kernel,
        grid=(micros, OUT // n),
        out_shape=[
            jax.ShapeDtypeStruct((micros, rows, MID), F32),
            jax.ShapeDtypeStruct((micros, 8, MID), F32),
            jax.ShapeDtypeStruct((LANES, GRAD_OUT, 256), BF16),
        ],
        in_specs=[
            pl.BlockSpec((1, rows, n), lambda m, k: (m, 0, k)),
            pl.BlockSpec((1, rows, n), lambda m, k: (m, 0, k)),
            pl.BlockSpec((1, images, n), lambda m, k: (m, 0, k)),
            pl.BlockSpec((1, 8, n), lambda m, k: (m, 0, k)),
            pl.BlockSpec((1, 1, rows, 1), lambda m, k: (m, 0, 0, 0)),
            pl.BlockSpec((1, rows, MID), lambda m, k: (m, 0, 0)),
            pl.BlockSpec((1, rows, D_IN), lambda m, k: (m, 0, 0)),
            pl.BlockSpec((MID, n), lambda m, k: (0, k)),
            pl.BlockSpec((1, rows, MID), lambda m, k: (m, 0, 0)),
            pl.BlockSpec((1, 8, MID), lambda m, k: (m, 0, 0)),
        ],
        out_specs=[
            pl.BlockSpec((1, rows, MID), lambda m, k: (m, 0, 0)),
            pl.BlockSpec((1, 8, MID), lambda m, k: (m, 0, 0)),
            whole_block((LANES, GRAD_OUT, 256)),
        ],
        scratch_shapes=[
            pltpu.VMEM((MID, rows), BF16),
            pltpu.VMEM((D_IN, rows), BF16),
            pltpu.VMEM((rows, MID), F32),
            pltpu.VMEM((rows, n), BF16),
            pltpu.VMEM((rows, n), BF16),
            pltpu.VMEM((OUT // n, MID, n), F32),
            pltpu.VMEM((OUT // n, D_IN, n), F32),
        ],
        compiler_params=params_of(60, 2),
        cost_estimate=cost(2 * micros * rows * OUT * (2 * MID + D_IN), 40 << 20),
    )(ho, hs, gs, coef, wph, am, xe, weight, hm, coef_mid)


def back_mid_kernel(
    hm_ref, d_ref, cm_ref, cols_ref, wb, h_ref, hh_ref, cf_ref, w_ref, wh_ref,
    din_ref, dh_ref, st_ref, gw_ref, dt, acc,
):
    micro = pl.program_id(0)
    images = h_ref.shape[2] // 16

    low = ((d_ref[0] * cm_ref[0, 0:1, :] + cm_ref[0, 1:2, :] + hm_ref[0] * cm_ref[0, 2:3, :]) * w_ref[0, 0]).astype(BF16)
    for tap in range(9):
        lanes = slice(tap * MID, (tap + 1) * MID)
        g = dot_tn(cols_ref[0, :, lanes], low)

        @pl.when(micro == 0)
        def _():
            for col in range(4):
                acc[col, lanes, :] = g[:, col * 128 : (col + 1) * 128]

        @pl.when(micro > 0)
        def _():
            for col in range(4):
                acc[col, lanes, :] += g[:, col * 128 : (col + 1) * 128]

    scale, shift = cf_ref[0, 0:1, :], cf_ref[0, 1:2, :]
    zero = jnp.zeros((8, MID), F32)

    def back(h, grad, w):
        v = h * scale + shift
        s = sigmoid(v)
        return s * (1.0 + v * (1.0 - s)) * grad * w

    def body(i, carry):
        total, product = carry
        at = pl.ds(pl.multiple_of(i * 16, 16), 16)
        half = pl.ds(pl.multiple_of(i * 8, 8), 8)
        near = pl.ds(pl.multiple_of((i % (images // 2)) * 16, 16), 16)
        t = [dt[k, near, :].reshape(2, 8, MID) for k in range(9)]
        below1 = t[1]
        below3 = t[2] + shift_left(t[0])
        last = jnp.zeros((1, 8, MID), F32)
        grads = [
            t[4],
            t[5] + shift_left(t[3]),
            t[7] + jnp.concatenate([below1[1:], last], axis=0),
            t[8] + shift_left(t[6]) + jnp.concatenate([below3[1:], last], axis=0),
        ]
        for k in range(4):
            h = h_ref[0, k, at, :]
            d = back(h, grads[k].reshape(16, MID), w_ref[0, k, at, :])
            din_ref[0, k, at, :] = d.astype(BF16)
            total = total + fold(d)
            product = product + fold(d * h)
        for k, grad in enumerate((below1, below3)):
            h = hh_ref[0, k, half, :]
            d = back(h, grad[0], wh_ref[0, k, half, :])
            dh_ref[0, k, half, :] = d
            total = total + d
            product = product + d * h
        return total, product

    found = (zero, zero)
    for part in range(2):
        start, stop = part * images // 2, (part + 1) * images // 2
        for tap in range(9):
            dt[tap] = dot_nt(low[start * 16 : stop * 16], wb[tap * MID : (tap + 1) * MID, :])
        found = lax.fori_loop(start, stop, body, found)
    total, product = found
    st_ref[...] = jnp.zeros_like(st_ref)
    st_ref[0, 0:1, :] = jnp.sum(total, axis=0, keepdims=True)
    st_ref[0, 1:2, :] = jnp.sum(product, axis=0, keepdims=True)

    @pl.when(micro == pl.num_programs(0) - 1)
    def _():
        for k in range(LANES):
            for half in range(2):
                found = acc[(k % 2) * 2 + half, pl.ds(k // 2, GRAD_MID, stride=4), :]
                gw_ref[k, :, half * 128 : half * 128 + 128] = found.astype(BF16)


def back_mid(hm, d, coef_mid, cols, weight, h, hh, coef, wph, whalo):
    micros, _, rows, _ = h.shape
    return pl.pallas_call(
        back_mid_kernel,
        grid=(micros,),
        out_shape=[
            jax.ShapeDtypeStruct((micros, 4, rows, MID), BF16),
            jax.ShapeDtypeStruct((micros, 2, rows // 2, MID), F32),
            jax.ShapeDtypeStruct((micros, 8, MID), F32),
            jax.ShapeDtypeStruct((LANES, GRAD_MID, 256), BF16),
        ],
        in_specs=[
            pl.BlockSpec((1, rows, MID), lambda m: (m, 0, 0)),
            pl.BlockSpec((1, rows, MID), lambda m: (m, 0, 0)),
            pl.BlockSpec((1, 8, MID), lambda m: (m, 0, 0)),
            pl.BlockSpec((1, rows, 9 * MID), lambda m: (m, 0, 0)),
            pl.BlockSpec((9 * MID, MID), lambda m: (0, 0), pipeline_mode=pl.Buffered(1)),
            pl.BlockSpec((1, 4, rows, MID), lambda m: (m, 0, 0, 0)),
            pl.BlockSpec((1, 2, rows // 2, MID), lambda m: (m, 0, 0, 0)),
            pl.BlockSpec((1, 8, MID), lambda m: (m, 0, 0)),
            pl.BlockSpec((1, 4, rows, 1), lambda m: (m, 0, 0, 0)),
            pl.BlockSpec((1, 2, rows // 2, 1), lambda m: (m, 0, 0, 0)),
        ],
        out_specs=[
            pl.BlockSpec((1, 4, rows, MID), lambda m: (m, 0, 0, 0)),
            pl.BlockSpec((1, 2, rows // 2, MID), lambda m: (m, 0, 0, 0)),
            pl.BlockSpec((1, 8, MID), lambda m: (m, 0, 0)),
            pl.BlockSpec((LANES, GRAD_MID, 256), lambda m: (0, 0, 0), pipeline_mode=pl.Buffered(1)),
        ],
        scratch_shapes=[
            pltpu.VMEM((9, rows // 2, MID), F32),
            pltpu.VMEM((4, 9 * MID, 128), F32),
        ],
        compiler_params=params_of(62),
        cost_estimate=cost(4 * micros * rows * 9 * MID * MID, 60 << 20),
    )(hm, d, coef_mid, cols, weight, h, hh, coef, wph, whalo)


def back_in_kernel(h_ref, din_ref, dh_ref, cf_ref, w_ref, wh_ref, x_ref, xh_ref, gw_ref, ds, acc, turned):
    micro, part = pl.program_id(0), pl.program_id(1)
    images = h_ref.shape[2] // 16
    ca, cb, cc = cf_ref[0, 0:1, :], cf_ref[0, 1:2, :], cf_ref[0, 2:3, :]

    def body(i, carry):
        at = pl.ds(pl.multiple_of(i * 16, 16), 16)
        half = pl.ds(pl.multiple_of(i * 8, 8), 8)
        for k in range(4):
            h = h_ref[0, k, at, :]
            d = (din_ref[0, k, at, :].astype(F32) * ca + cb + h * cc) * w_ref[0, k, at, :]
            row, side = k // 2, k % 2
            for o in range(2):
                for col in range(4):
                    to = pl.ds(i * 64 + (2 * o + row) * 16 + side, 8, stride=2)
                    ds[col, to, :] = d[o * 8 : o * 8 + 8, col * 128 : (col + 1) * 128]
        for side in range(2):
            d = dh_ref[0, side, half, :] * ca
            for col in range(4):
                ds[col, pl.ds(images * 64 + i * 16 + side, 8, stride=2), :] = d[:, col * 128 : (col + 1) * 128]
        return carry

    lax.fori_loop(0, images, body, 0)
    low = jnp.concatenate([ds[col].astype(BF16) for col in range(4)], axis=1)
    g = dot_tn(low[: images * 64], x_ref[0]) + dot_tn(low[images * 64 :], xh_ref[0])

    @pl.when((micro == 0) & (part == 0))
    def _():
        acc[...] = g

    @pl.when((micro > 0) | (part > 0))
    def _():
        acc[...] += g

    @pl.when((micro == pl.num_programs(0) - 1) & (part == pl.num_programs(1) - 1))
    def _():
        for col in range(4):
            turned[col] = acc[col * 128 : (col + 1) * 128, :].T
        for k in range(LANES):
            for half in range(2):
                found = turned[(k % 2) * 2 + half, pl.ds(k // 2, D_IN // 4, stride=4), :]
                gw_ref[k, :, half * 128 : half * 128 + 128] = found.astype(BF16)


def back_in(h, din, dhalo, coef, wph, whalo, x, xh, first, micros):
    rows = h.shape[2]
    parts = 2
    r = rows // parts
    return pl.pallas_call(
        back_in_kernel,
        grid=(micros, parts),
        out_shape=jax.ShapeDtypeStruct((LANES, 256, 256), BF16),
        in_specs=[
            pl.BlockSpec((1, 4, r, MID), lambda m, k: (m + first, 0, k, 0)),
            pl.BlockSpec((1, 4, r, MID), lambda m, k: (m + first, 0, k, 0)),
            pl.BlockSpec((1, 2, r // 2, MID), lambda m, k: (m + first, 0, k, 0)),
            pl.BlockSpec((1, 8, MID), lambda m, k: (m + first, 0, 0)),
            pl.BlockSpec((1, 4, r, 1), lambda m, k: (m + first, 0, k, 0)),
            pl.BlockSpec((1, 2, r // 2, 1), lambda m, k: (m + first, 0, k, 0)),
            pl.BlockSpec((1, r * 4, D_IN), lambda m, k: (m + first, k, 0)),
            pl.BlockSpec((1, r, D_IN), lambda m, k: (m + first, k, 0)),
        ],
        out_specs=whole_block((LANES, 256, 256)),
        scratch_shapes=[
            pltpu.VMEM((4, r * 5, 128), F32),
            pltpu.VMEM((MID, D_IN), F32),
            pltpu.VMEM((4, D_IN, 128), F32),
        ],
        compiler_params=params_of(60, 2),
        cost_estimate=cost(2 * micros * rows * 5 * D_IN * MID, 50 << 20),
    )(h, din, dhalo, coef, wph, whalo, x, xh)


def swap(value, axis, bit):
    size = lax.axis_size(axis)
    return lax.ppermute(value, axis, [(i, i ^ bit) for i in range(size)])


def bits_of(axis):
    size, bit, found = lax.axis_size(axis), 1, []
    while bit < size:
        found.append(bit)
        bit *= 2
    return found


def add_all(value, axes=("c", "x", "p", "g")):
    for axis in axes:
        for bit in bits_of(axis):
            value = value + swap(value, axis, bit)
    return value


def exchange_planes(value):
    planes = lax.axis_size("g")
    here = lax.axis_index("g")
    own = lax.dynamic_index_in_dim(value, here, 0, keepdims=True)
    result = lax.dynamic_update_slice_in_dim(jnp.zeros_like(value), own, here, 0)
    for step in range(1, planes):
        block = lax.dynamic_index_in_dim(value, (here + step) % planes, 0, keepdims=True)
        got = lax.ppermute(block, "g", [(i, (i + step) % planes) for i in range(planes)])
        result = lax.dynamic_update_slice_in_dim(result, got, (here + planes - step) % planes, 0)
    return result


def gather_axis(value, axis):
    value = value[None]
    for bit in bits_of(axis):
        other = swap(value, axis, bit)
        mine = (lax.axis_index(axis) // bit) % 2
        value = jnp.where(mine == 0, jnp.concatenate([value, other]), jnp.concatenate([other, value]))
    return value


def to_heads(value):
    routed = exchange_planes(value)
    for axis in ("p", "x", "c"):
        routed = gather_axis(routed, axis)
    order = (3, 2, 1, 0, 4) + tuple(range(5, routed.ndim))
    routed = jnp.transpose(routed, order)
    return routed.reshape((-1,) + value.shape[2:])


def halve(value, axis, dim):
    own = lax.axis_index(axis)
    keep = lax.dynamic_index_in_dim(value, own, dim, keepdims=False)
    send = lax.dynamic_index_in_dim(value, 1 - own, dim, keepdims=False)
    return keep + swap(send, axis, 1)


def plane_reduce(value):
    half = value.shape[1] // 2
    value = halve(value.reshape((2, 2, 2) + value.shape[1:]), "c", 2)
    a = halve(halve(value[:, :, :half], "x", 1), "p", 0)
    b = halve(halve(value[:, :, half:], "p", 0), "x", 0)
    return jnp.concatenate([a, b], axis=0)


def to_plane(value, first, steps=(1, 2)):
    for step in steps:
        pairs = [(i ^ step, i) for i in range(GROUPS) if step == 1 and i % 2 == first or i == first]
        value = value + lax.ppermute(value, "g", pairs)
    return value


def spread_trunk(block, plane, plane_rows):
    planes = lax.axis_size("g")
    result = None
    for target in range(planes):
        parts = []
        for source in range(planes):
            low = max(target * GROUP, source * plane_rows)
            high = min((target + 1) * GROUP, (source + 1) * plane_rows)
            if low < high:
                piece = block[low - source * plane_rows : high - source * plane_rows]
                parts.append(piece if source == target else lax.ppermute(piece, "g", [(source, target)]))
        whole = parts[0] if len(parts) == 1 else jnp.concatenate(parts, axis=0)
        result = whole if result is None else jnp.where(plane == target, whole, result)
    return result


def first_rows_everywhere(block, plane, plane_rows):
    last = lax.axis_size("g") - 1
    at = ROW_VEC - last * plane_rows
    send = jnp.concatenate([block[:ROW_CMID], block[at : at + 16]], axis=0)
    first, vec = send[:ROW_CMID], send[ROW_CMID:]
    for target in range(1, last + 1):
        pairs = [(0, target), (last, last - target)]
        got = lax.ppermute(send, "g", pairs)
        first = jnp.where(plane == target, got[:ROW_CMID], first)
        vec = jnp.where(plane == last - target, got[ROW_CMID:], vec)
    rows = jnp.concatenate([first, vec], axis=0)
    for axis in PLANE:
        rows = gather_axis(rows, axis)
    rows = jnp.transpose(rows, (3, 2, 1, 0, 4)).reshape(-1, 2048)
    return rows[:ROW_CMID], rows[ROW_CMID:]


def norm_ranges():
    widths = [MID, MID, OUT, OUT, OUT, OUT, OUT, PRED]
    return [(sum(widths[:layer]), widths[layer]) for layer in range(8)]


def silu_back(value, grad):
    gate = jax.nn.sigmoid(value)
    return grad * gate * (1.0 + value * (1.0 - gate))


def head_norm(hidden, gamma, beta):
    count = hidden.shape[0]
    average = jnp.sum(hidden, axis=0) / count
    variance = jnp.sum(hidden * hidden, axis=0) / count - average * average
    scale = lax.rsqrt(variance + EPS_NORM)
    normed = (hidden - average) * scale
    return gamma * normed + beta, (normed, scale), average, variance


def head_norm_back(grad, kept, gamma):
    normed, scale = kept
    count = grad.shape[0]
    beta_sum = jnp.sum(grad, axis=0)
    gamma_sum = jnp.sum(grad * normed, axis=0)
    back = gamma * scale * (grad - beta_sum / count - normed * gamma_sum / count)
    return back, gamma_sum, beta_sum


def heads(pooled_low, wall, gammas, betas, bias, partner, live):
    project = [wall[ROW_PROJ + 2048 * k : ROW_PROJ + 2048 * (k + 1)] for k in range(3)]
    predict_in = wall[ROW_PIN:ROW_POUT].reshape(OUT, PRED)
    predict_out = wall[ROW_POUT:ROW_VEC]
    means, variances, kept_all, normed_all, lows = [], [], [], [], []
    low = pooled_low
    for k in range(3):
        normed, kept, mean, variance = head_norm(dot(low, project[k]), gammas[4 + k], betas[4 + k])
        means.append(mean)
        variances.append(variance)
        kept_all.append(kept)
        normed_all.append(normed)
        lows.append(low)
        low = (jax.nn.silu(normed) if k < 2 else normed).astype(BF16)
    latent, latent_low = normed, low
    normed_q, kept_q, mean, variance = head_norm(dot(latent_low, predict_in), gammas[7], betas[7])
    means.append(mean)
    variances.append(variance)
    act = jax.nn.silu(normed_q).astype(BF16)
    predicted = dot(act, predict_out) + bias
    choose = (partner[:, None] == jnp.arange(latent.shape[0])[None, :]).astype(F32)
    target = jnp.dot(choose, latent, precision=lax.Precision.HIGHEST)
    inner = jnp.sum(predicted * target, axis=-1)
    inv_pred = lax.rsqrt(jnp.sum(predicted * predicted, axis=-1) + COS_EPS)
    inv_goal = lax.rsqrt(jnp.sum(target * target, axis=-1) + COS_EPS)
    flags = live.astype(F32)
    loss_sum = -jnp.sum(flags * inner * inv_pred * inv_goal)
    live_count = jnp.sum(flags)
    grad_cos = -flags / live_count
    grad_pred = grad_cos[:, None] * (
        target * (inv_pred * inv_goal)[:, None] - (inner * inv_pred**3 * inv_goal)[:, None] * predicted
    )
    grad_bias = jnp.sum(grad_pred, axis=0)
    low_p = grad_pred.astype(BF16)
    grad_act = dot_nt(low_p, predict_out)
    grad_q, gamma_q, beta_q = head_norm_back(silu_back(normed_q, grad_act), kept_q, gammas[7])
    low_q = grad_q.astype(BF16)
    grad_act = dot_nt(low_q, predict_in)
    low_f, gamma_sums, beta_sums = [None] * 3, [None] * 3, [None] * 3
    for k in (2, 1, 0):
        grad_normed = grad_act if k == 2 else silu_back(normed_all[k], grad_act)
        grad_hidden, gamma_sums[k], beta_sums[k] = head_norm_back(grad_normed, kept_all[k], gammas[4 + k])
        low_f[k] = grad_hidden.astype(BF16)
        grad_act = dot_nt(low_f[k], project[k])
    block = (lax.axis_index("p") % 2) * 4 + lax.axis_index("x") * 2 + lax.axis_index("c")

    def columns(v, start):
        return lax.dynamic_slice_in_dim(v, start, 256, 1)

    rows = [dot_tn(lows[k], columns(low_f[k], block * 256)).astype(BF16) for k in range(3)]
    g_in = dot_tn(latent_low, columns(low_q, (block % 2) * 256)).astype(BF16)
    rows.append(lax.dynamic_index_in_dim(g_in.reshape(PRED, 4, 256), block // 2, 1, keepdims=False))
    rows.append(dot_tn(act, columns(low_p, block * 256)).astype(BF16))
    vector = (gamma_sums + [gamma_q], beta_sums + [beta_q], grad_bias)
    return grad_act, jnp.concatenate(rows, axis=0), vector, block, loss_sum, live_count, means, variances


def place(values, size):
    flat, at = jnp.zeros((size,), F32), 0
    for value in values:
        flat = flat + jnp.pad(value, (at, size - at - value.shape[0]))
        at += value.shape[0]
    return flat


def norm_coefs(sums, total, gamma, beta):
    mean = sums[:, 0] / total[:, None]
    variance = sums[:, 1] / total[:, None] - mean * mean
    scale = lax.rsqrt(variance + EPS_NORM)
    a = gamma * scale
    return mean, variance, scale, a, beta - a * mean


def pack(rows):
    rows = list(rows) + [jnp.zeros_like(rows[0])] * (8 - len(rows))
    return jnp.stack(rows, axis=1)


def back_coefs(grad_sum, product_sum, mean, scale, a, total):
    gamma_sum = scale * (product_sum - mean * grad_sum)
    c = -a * scale * gamma_sum / total[:, None]
    b = -a * grad_sum / total[:, None] - c * mean
    return b, c, gamma_sum


def on_device(inputs, masks, partner, live, params, first, second, running):
    count = lax.axis_size(ALL)
    index = lax.axis_index(ALL)
    plane = lax.axis_index("g")
    own = params.shape[0] // 128
    micros, images, rows, width, _ = inputs.shape
    out_rows, out_cols = rows // 2, width // 2
    window_rows = -(-own // 256) * 16
    shift = window_rows * 16 - own
    plane_rows = window_rows * LANES
    near = (
        shift * count <= own
        and lax.axis_size("g") == GROUPS
        and lax.axis_size(PLANE) == LANES
        and ROW_COUT < plane_rows < ROW_PROJ <= 2 * plane_rows
        and window_rows - tail_rows(shift, count) < ROW_CMID <= window_rows
        and ROW_VEC % window_rows + 16 <= window_rows
        and ROW_VEC >= (lax.axis_size("g") - 1) * plane_rows
    )

    x = inputs.reshape(micros, images * rows * width, D_IN)
    x_last, mask_last = inputs[:, :, -1], masks[:, :, -1]
    mask = masks.astype(F32)
    split = mask.reshape(micros, images, out_rows, 2, out_cols, 2)
    wph = jnp.transpose(split, (0, 3, 5, 1, 2, 4)).reshape(micros, 4, -1, 1)
    around = [(i, i + 1) for i in range(lax.axis_size(("x", "c")) - 1)]
    total_in = jnp.sum(mask, axis=(1, 2, 3))
    image_pixels = jnp.sum(split[:, :, :, 0, :, 0], axis=(2, 3))
    total_out = jnp.sum(image_pixels, axis=1)
    chosen = jnp.stack([partner.astype(F32), live.astype(F32)], axis=-1)
    if near:
        window = flat_to_window(params, window_rows, shift, index, count)
        column = lax.all_to_all(window, PLANE, 1, 0, tiled=True)
        wide_in, vec = first_rows_everywhere(column, plane, plane_rows)
        trunk = spread_trunk(column, plane, plane_rows)
        trunk, x_last, wide_in = lax.optimization_barrier((trunk, x_last, wide_in))
        h, xe, st, w_first = conv_in(x, wph, wide_in)
        trunk = lax.all_gather(trunk, ALL, axis=0, tiled=False).reshape(GROUPS, LANES, GROUP, 256)
        st, image_pixels, chosen, mask_last = lax.optimization_barrier((st, image_pixels, chosen, mask_last))
    else:
        wall = lax.all_gather(params.astype(BF16), ALL, axis=0, tiled=True).reshape(-1, 2048)
        wide_in, vec = wall[:ROW_CMID], wall[ROW_VEC : ROW_VEC + 16]
        trunk = jnp.transpose(wall[:ROW_PROJ].reshape(GROUPS, GROUP, LANES, 256), (0, 2, 1, 3))
        h, xe, st, w_first = conv_in(x, wph, wide_in)

    x_halo = lax.ppermute(x_last, ("x", "c"), around).reshape(micros, images * width, D_IN)
    mask_halo = lax.ppermute(mask_last, ("x", "c"), around).astype(F32)
    image_pixels = add_all(image_pixels, ("c", "x"))
    chosen = to_heads(chosen)
    whalo = jnp.transpose(mask_halo.reshape(micros, images, out_cols, 2), (0, 3, 1, 2)).reshape(micros, 2, -1, 1)
    share_index = lax.axis_index(("x", "c"))

    pixels = jnp.broadcast_to(jnp.stack([total_in, total_out], axis=1)[..., None], (micros, 2, 128))
    sums = add_all(jnp.concatenate([st[:, :2], pixels], axis=2))
    total_in, total_out = sums[:, 0, MID], sums[:, 1, MID]
    sums = sums[..., :MID]
    hh = conv_in_halo(x_halo, w_first)
    if near:
        window, trunk, sums, hh, total_in, total_out, whalo, image_pixels, chosen = lax.optimization_barrier(
            (window, trunk, sums, hh, total_in, total_out, whalo, image_pixels, chosen)
        )
        wall = lax.all_gather(window, ALL, axis=0, tiled=True)

    vec = vec.astype(F32).reshape(-1)
    ranges = norm_ranges()
    gammas = [vec[start : start + n] for start, n in ranges]
    betas = [vec[NORM + start : NORM + start + n] for start, n in ranges]
    bias = vec[2 * NORM : 2 * NORM + OUT]

    mean_in, var_in, scale_in, a_in, b_in = norm_coefs(sums, total_in, gammas[0], betas[0])
    coef_in = pack([a_in, b_in])
    hs, st_side = conv_side(xe, trunk)
    cols, hm, st, w_mid = conv_mid(h, hh, coef_in, wph, whalo, trunk)
    sums = add_all(jnp.concatenate([st[:, :2], st_side[:, :2]], axis=2))
    mean_mid, var_mid, scale_mid, a_mid, b_mid = norm_coefs(sums[..., :MID], total_out, gammas[1], betas[1])
    mean_side, var_side, scale_side, a_side, b_side = norm_coefs(sums[..., MID:], total_out, gammas[3], betas[3])
    am, ho, st, w_out = conv_out(hm, pack([a_mid, b_mid]), wph, trunk)
    sums = add_all(st[:, :2])
    mean_out, var_out, scale_out, a_out, b_out = norm_coefs(sums, total_out, gammas[2], betas[2])
    coef_join = pack([a_out, a_side, b_out + b_side])
    pooled = pool(ho, hs, coef_join, wph)
    for axis in ("x", "c"):
        half = pooled.shape[1] // 2
        here = lax.axis_index(axis)
        keep = lax.dynamic_slice_in_dim(pooled, here * half, half, 1)
        send = lax.dynamic_slice_in_dim(pooled, (1 - here) * half, half, 1)
        pooled = keep + swap(send, axis, 1)
    share = pooled.shape[1]
    share_pixels = lax.dynamic_slice_in_dim(image_pixels, share_index * share, share, 1)
    pooled_low = to_heads((pooled / share_pixels[..., None]).astype(BF16))
    slope = slopes(ho, hs, coef_join, wph)
    pooled_low, slope = lax.optimization_barrier((pooled_low, slope))

    grad_pool, head_rows, head_vec, block, loss_sum, live_count, head_means, head_vars = heads(
        pooled_low, wall, gammas, betas, bias, chosen[:, 0].astype(jnp.int32), chosen[:, 1]
    )

    def vector_rows(gamma, beta, extra):
        return place(gamma + beta + [extra], 16 * 2048).astype(BF16).reshape(16, 2048)

    none_head = [jnp.zeros((n,), F32) for _, n in ranges[4:]]
    none_trunk = [jnp.zeros((n,), F32) for _, n in ranges[:4]]
    head_vector = vector_rows(none_trunk + head_vec[0], none_trunk + head_vec[1], head_vec[2])
    head_vector = lax.dynamic_slice_in_dim(head_vector, block * 256, 256, 1)

    head_stats = place(head_means + head_vars + [loss_sum[None], live_count[None]], 106 * 128).reshape(1, -1, 128)
    head_stats = exchange_planes(jnp.broadcast_to(head_stats, (micros,) + head_stats.shape[1:])).reshape(micros, -1)
    head_size = NORM - sum(n for _, n in ranges[:4])
    scalars = head_stats[:, 2 * head_size : 2 * head_size + 2]

    grad_pool = grad_pool.astype(BF16).reshape(lax.axis_size("g"), lax.axis_size("p"), images, OUT)
    grad_pool = lax.dynamic_index_in_dim(grad_pool, lax.axis_index("p"), 1, keepdims=False)
    gs = exchange_planes(grad_pool)
    if near:
        head_part = jnp.concatenate(
            [
                jnp.zeros((ROW_PROJ, 256), BF16),
                head_rows,
                head_vector,
                jnp.zeros((window_rows * count - ROW_VEC - 16, 256), BF16),
            ],
            axis=0,
        )
        head_part, gs, head_stats = lax.optimization_barrier((head_part, gs, head_stats))
        head_part = lax.psum_scatter(head_part, "g", scatter_dimension=0, tiled=True)
    gs = gs.astype(F32) / image_pixels[..., None]

    sums = add_all(jnp.sum(gs[:, None] * slope, axis=2))
    bo, co, gamma_out = back_coefs(sums[:, 0], sums[:, 1], mean_out, scale_out, a_out, total_out)
    bs, cs, gamma_side = back_coefs(sums[:, 0], sums[:, 2], mean_side, scale_side, a_side, total_out)
    beta_joined = sums[:, 0]
    coef_back = pack([a_out, a_side, b_out + b_side, bo, co, bs, cs])
    d_mid, st, g_out = back_out(
        ho, hs, gs, coef_back, wph, am, xe, w_out, hm, pack([a_mid, b_mid])
    )
    if near:
        head_part, g_out = lax.optimization_barrier((head_part, g_out))
        g_out = lax.psum_scatter(g_out, PLANE, scatter_dimension=0, tiled=False)
    sums = add_all(st[:, :2])
    bm, cm, gamma_mid = back_coefs(sums[:, 0], sums[:, 1], mean_mid, scale_mid, a_mid, total_out)
    beta_mid = sums[:, 0]
    d_in, d_halo, st, g_mid = back_mid(
        hm, d_mid, pack([a_mid, bm, cm]), cols, w_mid, h, hh, coef_in, wph, whalo
    )
    if near:
        g_mid = halve(g_mid.reshape(2, 2, 2, GRAD_MID, 256), "c", 2)
        out_first = to_plane(g_out[: plane_rows - ROW_COUT], 0, (1,))
        out_second = to_plane(g_out[plane_rows - ROW_COUT :], 1, (1,))
    sums = add_all(st[:, :2])
    bi, ci, gamma_in = back_coefs(sums[:, 0], sums[:, 1], mean_in, scale_in, a_in, total_in)
    beta_in = sums[:, 0]
    half = micros // 2
    if near:
        bi, ci, g_mid = lax.optimization_barrier((bi, ci, g_mid))
        coef = pack([a_in, bi, ci])
        g_in = back_in(h, d_in, d_halo, coef, wph, whalo, x, x_halo, 0, half)
        upper, lower = halve(g_mid[:, :, : GRAD_MID // 2], "x", 1), halve(g_mid[:, :, GRAD_MID // 2 :], "p", 0)
        g_in, coef, upper, lower, out_first, out_second = lax.optimization_barrier(
            (g_in, coef, upper, lower, out_first, out_second)
        )
        out_first, out_second = to_plane(out_first, 0, (2,)), to_plane(out_second, 1, (2,))
        g_in = g_in + back_in(h, d_in, d_halo, coef, wph, whalo, x, x_halo, half, micros - half)
        g_mid = jnp.concatenate([halve(upper, "p", 0), halve(lower, "x", 0)], axis=0)
        g_in = plane_reduce(g_in)
    else:
        g_in = back_in(h, d_in, d_halo, pack([a_in, bi, ci]), wph, whalo, x, x_halo, 0, micros)

    trunk_gamma = [jnp.sum(v, axis=0) for v in (gamma_in, gamma_mid, gamma_out, gamma_side)]
    trunk_beta = [jnp.sum(v, axis=0) for v in (beta_in, beta_mid, beta_joined, beta_joined)]
    trunk_vector = vector_rows(trunk_gamma + none_head, trunk_beta + none_head, jnp.zeros((OUT,), F32))

    if near:
        def blank(n):
            return jnp.zeros((n, 256), BF16)

        first_rows = jnp.concatenate([blank(ROW_CMID), to_plane(g_mid, 0), out_first], axis=0)
        second_rows = jnp.concatenate([out_second, blank(plane_rows - out_second.shape[0])], axis=0)
        part = jnp.where(plane == 0, first_rows, jnp.where(plane == 1, head_part + second_rows, head_part))
        window = lax.all_to_all(part, PLANE, 0, 1, tiled=True)
        tail = tail_rows(shift, count)
        prev = lax.ppermute(window[window_rows - tail :], ALL, [(i, i + 1) for i in range(count - 1)])
        g_in = to_plane(g_in, 0)
        for axis in PLANE:
            g_in = gather_axis(g_in, axis)
        g_in = jnp.transpose(g_in, (3, 2, 1, 0, 4)).reshape(ROW_CMID, 2048)
        window = window.at[:ROW_CMID].add(jnp.where(index == 0, g_in, 0))
        prev = prev.at[: ROW_CMID - window_rows + tail].add(jnp.where(index == 1, g_in[window_rows - tail :], 0))
        at = ROW_VEC % window_rows
        window = window.at[at : at + 16].add(jnp.where(index == ROW_VEC // window_rows, trunk_vector, 0))
        new_params, new_first, new_second, new_copy = adam_from_window(
            window, prev, shift, index, params, first, second
        )
    else:
        alone = (lax.axis_index("p") < 2).astype(BF16)
        head_part = jnp.concatenate([head_rows, head_vector], axis=0) * alone
        head_part = lax.dynamic_update_slice(
            jnp.zeros((head_part.shape[0], 2048), BF16), head_part, (jnp.int32(0), (block * 256).astype(jnp.int32))
        )
        lone = (index == 0).astype(BF16)
        head_part = head_part.at[ROW_VEC - ROW_PROJ :].add(trunk_vector * lone)
        trunk = jnp.concatenate([g_in, g_mid, g_out], axis=1)
        trunk = jnp.transpose(trunk, (1, 0, 2)).reshape(-1, 2048)
        flat = jnp.concatenate([trunk, head_part], axis=0).reshape(-1)
        flat = flat[: params.shape[0] * count]
        grad = lax.psum_scatter(flat, ALL, scatter_dimension=0, tiled=True).astype(F32)
        new_params, new_first, new_second = adam(grad, params, first, second)
        new_copy = new_params.astype(BF16)

    averages = jnp.concatenate([mean_in, mean_mid, mean_out, mean_side, head_stats[:, :head_size]], axis=1)
    spreads = jnp.concatenate([var_in, var_mid, var_out, var_side, head_stats[:, head_size : 2 * head_size]], axis=1)
    stats = jnp.stack([averages, spreads], axis=1)
    new_running = running
    for micro in range(micros):
        new_running = (1.0 - MOMENTUM) * new_running + MOMENTUM * stats[micro]
    return (
        scalars[:, 0],
        scalars[:, 1].astype(jnp.int32),
        new_params,
        new_first,
        new_second,
        new_copy,
        new_running,
    )


def solution(mesh):
    img, rows = mesh.shape["img"], mesh.shape["rows"]
    fine = Mesh(mesh.devices.reshape(MB, img // MB, 2, rows // 2), ALL)
    split = P(ALL)
    placed = (
        P(None, ("g", "p"), ("x", "c"), None, None),
        P(None, ("g", "p"), ("x", "c"), None),
        P(None, ALL),
        P(None, ALL),
        split,
        split,
        split,
        P(),
    )
    return jax.shard_map(
        on_device,
        mesh=fine,
        in_specs=placed,
        out_specs=(P(), P(), split, split, split, split, P()),
        check_vma=False,
    )
```

```python
import jax
import jax.numpy as jnp
from jax import lax
from jax.experimental import pallas as pl
from jax.experimental.pallas import tpu as pltpu
from jax.sharding import Mesh, PartitionSpec as P

D_IN = 1024
MID = 512
OUT = 2048
PRED = 512
MB = 4
STEP = 5
NORM = 11776
PARAMS = 20734976

EPS_NORM = 1e-05
MOMENTUM = 0.1
RATE = 0.03
BETA_ONE = 0.5
BETA_TWO = 0.5
DECAY = 0.01
ADAM_EPS = 1e-08
COS_EPS = 1e-06

ROW_CIN, ROW_CMID, ROW_COUT, ROW_SIDE = 0, 256, 1408, 1920
ROW_PROJ, ROW_PIN, ROW_POUT, ROW_VEC = 2944, 9088, 9600, 10112
LANES = 8
GROUPS, GROUP = 4, 736
GRAD_OUT, GRAD_MID = 1536, 1152
ALL = ("g", "p", "x", "c")
PLANE = ("p", "x", "c")
F32, BF16 = jnp.float32, jnp.bfloat16
COST_SHARE = 8


def params_of(mib=60, steps=1):
    return pltpu.CompilerParams(
        vmem_limit_bytes=mib << 20, dimension_semantics=("arbitrary",) * steps
    )


def cost(flops, moved):
    return pl.CostEstimate(flops=flops // COST_SHARE, bytes_accessed=moved // COST_SHARE, transcendentals=0)


def whole_block(shape):
    zeros = (0,) * len(shape)
    return pl.BlockSpec(shape, lambda *_: zeros)


def sigmoid(v):
    return 1.0 / (1.0 + jnp.exp(-v))


def dot(a, b):
    return jnp.dot(a, b, preferred_element_type=F32)


def dot_nt(a, b):
    return lax.dot_general(a, b, (((1,), (1,)), ((), ())), preferred_element_type=F32)


def dot_tn(a, b):
    return lax.dot_general(a, b, (((0,), (0,)), ((), ())), preferred_element_type=F32)


def fold(v):
    return jnp.sum(v.reshape(-1, 8, v.shape[-1]), axis=0)


def unwide(wide_ref, scratch, out_ref):
    rows = wide_ref.shape[0]
    for part in range(4):
        for col in range(4):
            lanes = pl.ds(part * 512 + col * 128, 128)
            scratch[col, pl.ds(part, rows, stride=4), :] = wide_ref[:, lanes].astype(F32)
    for col in range(4):
        out_ref[:, col * 128 : (col + 1) * 128] = scratch[col].astype(BF16)


def trunk_pieces(start, stop):
    found = []
    for group in range(GROUPS):
        low, high = max(start, group * GROUP), min(stop, (group + 1) * GROUP)
        if low < high:
            found.append((group, low - group * GROUP, low - start, high - low))
    return found


def trunk_specs(start, stop):
    def spec(group):
        return pl.BlockSpec(
            (1, LANES, GROUP, 256), lambda *_: (group, 0, 0, 0), pipeline_mode=pl.Buffered(1)
        )

    return [spec(piece[0]) for piece in trunk_pieces(start, stop)]


def join_trunk(refs, start, stop, out_ref):
    for ref, (_, low, to, rows) in zip(refs, trunk_pieces(start, stop)):
        for block in range(LANES):
            out_ref[to : to + rows, block * 256 : block * 256 + 256] = ref[0, block, low : low + rows, :]


def unwide_trunk(refs, start, stop, scratch, out_ref):
    for ref, (_, low, to, rows) in zip(refs, trunk_pieces(start, stop)):
        for part in range(4):
            for col in range(4):
                block, lanes = 2 * part + col // 2, slice((col % 2) * 128, (col % 2) * 128 + 128)
                scratch[col, pl.ds(part + 4 * to, rows, stride=4), :] = ref[0, block, low : low + rows, lanes].astype(F32)
    for col in range(4):
        out_ref[:, col * 128 : (col + 1) * 128] = scratch[col].astype(BF16)


def window_kernel(off_ref, flat_ref, out_ref):
    off = off_ref[0]
    rows = out_ref.shape[0]
    for col in range(16):
        out_ref[:, col * 128 : (col + 1) * 128] = flat_ref[pl.ds(off + col, rows, stride=16), :].astype(BF16)


def flat_to_window(params, rows, shift, index, count):
    own = params.shape[0] // 128
    head = shift * count
    nxt = lax.ppermute(
        params[: head * 128].astype(BF16), ALL, [(i + 1, i) for i in range(count - 1)]
    )
    flat = jnp.concatenate([params, nxt.astype(F32), jnp.zeros((1024,), F32)]).reshape(-1, 128)
    return pl.pallas_call(
        window_kernel,
        out_shape=jax.ShapeDtypeStruct((rows, 2048), BF16),
        in_specs=[pl.BlockSpec(memory_space=pltpu.SMEM), whole_block((own + head + 8, 128))],
        out_specs=whole_block((rows, 2048)),
        compiler_params=pltpu.CompilerParams(vmem_limit_bytes=40 << 20),
    )((index * shift).astype(jnp.int32)[None], flat)


def adam(grad, params, first, second):
    new_first = BETA_ONE * first + (1.0 - BETA_ONE) * grad
    new_second = BETA_TWO * second + (1.0 - BETA_TWO) * grad * grad
    corrected_first = new_first / (1.0 - BETA_ONE**STEP)
    corrected_second = new_second / (1.0 - BETA_TWO**STEP)
    new_params = params - RATE * (
        corrected_first / (jnp.sqrt(corrected_second) + ADAM_EPS) + DECAY * params
    )
    return new_params, new_first, new_second


def adam_kernel(off_ref, tail_ref, win_ref, p_ref, m_ref, v_ref, po_ref, mo_ref, vo_ref, co_ref, flat):
    step = pl.program_id(0)

    @pl.when(step == 0)
    def _():
        tail = tail_ref.shape[0]
        rows = win_ref.shape[0]
        for col in range(16):
            lanes = pl.ds(col * 128, 128)
            flat[pl.ds(col, tail, stride=16), :] = tail_ref[:, lanes].astype(F32)
            flat[pl.ds(tail * 16 + col, rows, stride=16), :] = win_ref[:, lanes].astype(F32)

    size = p_ref.shape[0]
    grad = flat[pl.ds(off_ref[0] + step * size, size), :]
    po_ref[...], mo_ref[...], vo_ref[...] = adam(grad, p_ref[...], m_ref[...], v_ref[...])
    co_ref[...] = po_ref[...].astype(BF16)


def tail_rows(shift, count):
    return -(-shift * (count - 1) // 256) * 16


def adam_from_window(window, prev, shift, index, params, first, second):
    own = params.shape[0] // 128
    rows, tail = window.shape[0], prev.shape[0]
    block = 512
    steps = -(-own // block)
    assert steps * block <= rows * 16
    off = (tail * 16 - index * shift).astype(jnp.int32)[None]
    spec = pl.BlockSpec((block, 128), lambda i: (i, 0))
    shaped = [v.reshape(own, 128) for v in (params, first, second)]
    outs = pl.pallas_call(
        adam_kernel,
        grid=(steps,),
        out_shape=[jax.ShapeDtypeStruct((own, 128), F32)] * 3 + [jax.ShapeDtypeStruct((own, 128), BF16)],
        in_specs=[pl.BlockSpec(memory_space=pltpu.SMEM), whole_block((tail, 2048)), whole_block((rows, 2048))] + [spec] * 3,
        out_specs=[spec] * 4,
        scratch_shapes=[pltpu.VMEM(((tail + rows) * 16, 128), F32)],
        compiler_params=params_of(40),
    )(off, prev, window, *shaped)
    return [v.reshape(-1) for v in outs]


def conv_in_kernel(x_ref, w_ref, wide_ref, h_ref, xe_ref, st_ref, wb, wf, hs, xs):
    micro, part = pl.program_id(0), pl.program_id(1)

    @pl.when((micro == 0) & (part == 0))
    def _():
        unwide(wide_ref, wf, wb)

    images = x_ref.shape[1] // 64
    h = dot(x_ref[0], wb[...])
    for col in range(4):
        hs[col] = h[:, col * 128 : (col + 1) * 128]

    def body(i, carry):
        at = pl.multiple_of(i * 64, 64)
        low = pl.multiple_of(i * 16, 16)
        w = [jnp.broadcast_to(w_ref[0, k, pl.ds(low, 16), :], (16, 128)) for k in range(4)]
        new = []
        for col in range(4):
            lanes = slice(col * 128, (col + 1) * 128)
            total, square = carry[col]
            for side in range(2):
                half = hs[col, pl.ds(at + side, 32, stride=2), :].reshape(2, 2, 8, 128)
                for row in range(2):
                    h = half[:, row].reshape(16, 128) * w[2 * row + side]
                    total, square = total + fold(h), square + fold(h * h)
                    h_ref[0, 2 * row + side, pl.ds(low, 16), lanes] = h
            new.append((total, square))
        w = w[0]
        for col in range(8):
            lanes = slice(col * 128, (col + 1) * 128)
            for row in range(2):
                xs[col, row * 16 : row * 16 + 16, :] = x_ref[0, pl.ds(at + row * 32, 16), lanes].astype(F32)
            xe_ref[0, pl.ds(low, 16), lanes] = (xs[col, pl.ds(0, 16, stride=2), :] * w).astype(BF16)
        return tuple(new)

    zero = jnp.zeros((8, 128), F32)
    found = lax.fori_loop(0, images, body, ((zero, zero),) * 4)

    @pl.when(part == 0)
    def _():
        st_ref[...] = jnp.zeros_like(st_ref)

    for col in range(4):
        lanes = slice(col * 128, (col + 1) * 128)
        for k in range(2):
            st_ref[0, k : k + 1, lanes] += jnp.sum(found[col][k], axis=0, keepdims=True)


def conv_in(x, wph, wide):
    micros, pixels, _ = x.shape
    images = pixels // 64
    parts = 2
    b = images // parts
    return pl.pallas_call(
        conv_in_kernel,
        grid=(micros, parts),
        out_shape=[
            jax.ShapeDtypeStruct((micros, 4, images * 16, MID), F32),
            jax.ShapeDtypeStruct((micros, images * 16, D_IN), BF16),
            jax.ShapeDtypeStruct((micros, 8, MID), F32),
            jax.ShapeDtypeStruct((D_IN, MID), BF16),
        ],
        in_specs=[
            pl.BlockSpec((1, b * 64, D_IN), lambda m, k: (m, k, 0)),
            pl.BlockSpec((1, 4, b * 16, 1), lambda m, k: (m, 0, k, 0)),
            whole_block((256, 2048)),
        ],
        out_specs=[
            pl.BlockSpec((1, 4, b * 16, MID), lambda m, k: (m, 0, k, 0)),
            pl.BlockSpec((1, b * 16, D_IN), lambda m, k: (m, k, 0)),
            pl.BlockSpec((1, 8, MID), lambda m, k: (m, 0, 0)),
            whole_block((D_IN, MID)),
        ],
        scratch_shapes=[
            pltpu.VMEM((4, D_IN, 128), F32),
            pltpu.VMEM((4, b * 64, 128), F32),
            pltpu.VMEM((8, 32, 128), F32),
        ],
        compiler_params=params_of(56, 2),
        cost_estimate=cost(2 * micros * images * 64 * D_IN * MID, 40 << 20),
    )(x, wph, wide)


def halo_kernel(xh_ref, wb_ref, hh_ref, hs):
    h = dot(xh_ref[0], wb_ref[...])
    rows = hh_ref.shape[2]
    for col in range(4):
        lanes = slice(col * 128, (col + 1) * 128)
        hs[col] = h[:, lanes]
        for side in range(2):
            hh_ref[0, side, :, lanes] = hs[col, pl.ds(side, rows, stride=2), :]


def conv_in_halo(xh, weight):
    micros, pixels, _ = xh.shape
    return pl.pallas_call(
        halo_kernel,
        grid=(micros,),
        out_shape=jax.ShapeDtypeStruct((micros, 2, pixels // 2, MID), F32),
        in_specs=[pl.BlockSpec((1, pixels, D_IN), lambda m: (m, 0, 0)), whole_block((D_IN, MID))],
        out_specs=pl.BlockSpec((1, 2, pixels // 2, MID), lambda m: (m, 0, 0, 0)),
        scratch_shapes=[pltpu.VMEM((4, pixels, 128), F32)],
        compiler_params=params_of(40),
        cost_estimate=cost(2 * micros * pixels * D_IN * MID, 9 << 20),
    )(xh, weight)


def side_kernel(xe_ref, *refs):
    pieces, (hs_ref, st_ref, weight) = refs[:-3], refs[-3:]

    @pl.when((pl.program_id(0) == 0) & (pl.program_id(1) == 0))
    def _():
        join_trunk(pieces, ROW_SIDE, ROW_PROJ, weight)

    n = hs_ref.shape[2]
    h = dot(xe_ref[0], weight[:, pl.ds(pl.multiple_of(pl.program_id(1) * n, n), n)])
    hs_ref[0] = h
    st_ref[...] = jnp.zeros_like(st_ref)
    st_ref[0, 0:1, :] = jnp.sum(h, axis=0, keepdims=True)
    st_ref[0, 1:2, :] = jnp.sum(h * h, axis=0, keepdims=True)


def conv_side(xe, trunk):
    micros, rows, _ = xe.shape
    cols = 4
    n = OUT // cols
    return pl.pallas_call(
        side_kernel,
        grid=(micros, cols),
        out_shape=[
            jax.ShapeDtypeStruct((micros, rows, OUT), F32),
            jax.ShapeDtypeStruct((micros, 8, OUT), F32),
        ],
        in_specs=[
            pl.BlockSpec((1, rows, D_IN), lambda m, k: (m, 0, 0)),
        ]
        + trunk_specs(ROW_SIDE, ROW_PROJ),
        out_specs=[
            pl.BlockSpec((1, rows, n), lambda m, k: (m, 0, k)),
            pl.BlockSpec((1, 8, n), lambda m, k: (m, 0, k)),
        ],
        scratch_shapes=[pltpu.VMEM((D_IN, OUT), BF16)],
        compiler_params=params_of(56, 2),
        cost_estimate=cost(2 * micros * rows * D_IN * OUT, 16 << 20),
    )(xe, *[trunk] * len(trunk_pieces(ROW_SIDE, ROW_PROJ)))


def shift_right(v):
    moved = pltpu.roll(v, 1, 1)
    return jnp.where(lax.broadcasted_iota(jnp.int32, v.shape, 1) == 0, 0.0, moved)


def shift_left(v):
    moved = pltpu.roll(v, 7, 1)
    return jnp.where(lax.broadcasted_iota(jnp.int32, v.shape, 1) == 7, 0.0, moved)


def conv_mid_kernel(h_ref, hh_ref, cf_ref, w_ref, wh_ref, *refs):
    pieces, (cols_ref, hm_ref, st_ref, wb, wf) = refs[:-5], refs[-5:]
    micro = pl.program_id(0)

    @pl.when(micro == 0)
    def _():
        unwide_trunk(pieces, ROW_CMID, ROW_COUT, wf, wb)

    images = h_ref.shape[2] // 16
    scale, shift = cf_ref[0, 0:1, :], cf_ref[0, 1:2, :]

    def act(h, w):
        v = h * scale + shift
        return v * sigmoid(v) * w

    def body(i, carry):
        at = pl.ds(pl.multiple_of(i * 16, 16), 16)
        half = pl.ds(pl.multiple_of(i * 8, 8), 8)
        a = [act(h_ref[0, k, at, :], w_ref[0, k, at, :]).reshape(2, 8, MID) for k in range(4)]
        above = [act(hh_ref[0, k, half, :], wh_ref[0, k, half, :]).reshape(1, 8, MID) for k in range(2)]
        a1s, a3s = shift_right(a[1]), shift_right(a[3])
        up2 = jnp.concatenate([above[0], a[2][:1]], axis=0)
        up3 = jnp.concatenate([above[1], a[3][:1]], axis=0)
        up3s = jnp.concatenate([shift_right(above[1]), a3s[:1]], axis=0)
        for tap, value in enumerate([up3s, up2, up3, a1s, a[0], a[1], a3s, a[2], a[3]]):
            cols_ref[0, at, tap * MID : (tap + 1) * MID] = value.reshape(16, MID).astype(BF16)
        return carry

    lax.fori_loop(0, images, body, 0)
    h = dot(cols_ref[0], wb[...])
    hm_ref[0] = h
    hw = h * w_ref[0, 0]
    st_ref[...] = jnp.zeros_like(st_ref)
    st_ref[0, 0:1, :] = jnp.sum(hw, axis=0, keepdims=True)
    st_ref[0, 1:2, :] = jnp.sum(hw * hw, axis=0, keepdims=True)


def conv_mid(h, hh, coef, wph, whalo, trunk):
    micros, _, rows, _ = h.shape
    return pl.pallas_call(
        conv_mid_kernel,
        grid=(micros,),
        out_shape=[
            jax.ShapeDtypeStruct((micros, rows, 9 * MID), BF16),
            jax.ShapeDtypeStruct((micros, rows, MID), F32),
            jax.ShapeDtypeStruct((micros, 8, MID), F32),
            jax.ShapeDtypeStruct((9 * MID, MID), BF16),
        ],
        in_specs=[
            pl.BlockSpec((1, 4, rows, MID), lambda m: (m, 0, 0, 0)),
            pl.BlockSpec((1, 2, rows // 2, MID), lambda m: (m, 0, 0, 0)),
            pl.BlockSpec((1, 8, MID), lambda m: (m, 0, 0)),
            pl.BlockSpec((1, 4, rows, 1), lambda m: (m, 0, 0, 0)),
            pl.BlockSpec((1, 2, rows // 2, 1), lambda m: (m, 0, 0, 0)),
        ]
        + trunk_specs(ROW_CMID, ROW_COUT),
        out_specs=[
            pl.BlockSpec((1, rows, 9 * MID), lambda m: (m, 0, 0)),
            pl.BlockSpec((1, rows, MID), lambda m: (m, 0, 0)),
            pl.BlockSpec((1, 8, MID), lambda m: (m, 0, 0)),
            pl.BlockSpec((9 * MID, MID), lambda m: (0, 0), pipeline_mode=pl.Buffered(1)),
        ],
        scratch_shapes=[pltpu.VMEM((4, 9 * MID, 128), F32)],
        compiler_params=params_of(60),
        cost_estimate=cost(2 * micros * rows * 9 * MID * MID, 50 << 20),
    )(h, hh, coef, wph, whalo, *[trunk] * len(trunk_pieces(ROW_CMID, ROW_COUT)))


def conv_out_kernel(hm_ref, cf_ref, w_ref, *refs):
    pieces, (am_ref, ho_ref, st_ref, weight_ref) = refs[:-4], refs[-4:]

    @pl.when(pl.program_id(0) == 0)
    def _():
        join_trunk(pieces, ROW_COUT, ROW_SIDE, weight_ref)

    v = hm_ref[0] * cf_ref[0, 0:1, :] + cf_ref[0, 1:2, :]
    am = (v * sigmoid(v) * w_ref[0, 0]).astype(BF16)
    am_ref[0] = am
    st_ref[...] = jnp.zeros_like(st_ref)
    for k in range(4):
        lanes = slice(k * 512, (k + 1) * 512)
        h = dot(am, weight_ref[:, lanes])
        ho_ref[0, :, lanes] = h
        st_ref[0, 0:1, lanes] = jnp.sum(h, axis=0, keepdims=True)
        st_ref[0, 1:2, lanes] = jnp.sum(h * h, axis=0, keepdims=True)


def conv_out(hm, coef, wph, trunk):
    micros, rows, _ = hm.shape
    return pl.pallas_call(
        conv_out_kernel,
        grid=(micros,),
        out_shape=[
            jax.ShapeDtypeStruct((micros, rows, MID), BF16),
            jax.ShapeDtypeStruct((micros, rows, OUT), F32),
            jax.ShapeDtypeStruct((micros, 8, OUT), F32),
            jax.ShapeDtypeStruct((MID, OUT), BF16),
        ],
        in_specs=[
            pl.BlockSpec((1, rows, MID), lambda m: (m, 0, 0)),
            pl.BlockSpec((1, 8, MID), lambda m: (m, 0, 0)),
            pl.BlockSpec((1, 1, rows, 1), lambda m: (m, 0, 0, 0)),
        ]
        + trunk_specs(ROW_COUT, ROW_SIDE),
        out_specs=[
            pl.BlockSpec((1, rows, MID), lambda m: (m, 0, 0)),
            pl.BlockSpec((1, rows, OUT), lambda m: (m, 0, 0)),
            pl.BlockSpec((1, 8, OUT), lambda m: (m, 0, 0)),
            pl.BlockSpec((MID, OUT), lambda m: (0, 0), pipeline_mode=pl.Buffered(1)),
        ],
        compiler_params=params_of(56),
        cost_estimate=cost(2 * micros * rows * MID * OUT, 18 << 20),
    )(hm, coef, wph, *[trunk] * len(trunk_pieces(ROW_COUT, ROW_SIDE)))


def pool_kernel(ho_ref, hs_ref, cf_ref, w_ref, out_ref):
    images = out_ref.shape[1]
    so, ss, shift = cf_ref[0, 0:1, :], cf_ref[0, 1:2, :], cf_ref[0, 2:3, :]

    def body(i, carry):
        total = []
        for k in range(8):
            at = pl.ds(pl.multiple_of(i * 128 + k * 16, 16), 16)
            j = ho_ref[0, at, :] * so + hs_ref[0, at, :] * ss + shift
            r = j * sigmoid(j) * w_ref[0, 0, at, :]
            total.append(jnp.sum(r, axis=0, keepdims=True))
        out_ref[0, pl.ds(pl.multiple_of(i * 8, 8), 8), :] = jnp.concatenate(total, axis=0)
        return carry

    lax.fori_loop(0, images // 8, body, 0)


def pool(ho, hs, coef, wph):
    micros, rows, _ = ho.shape
    n = 512
    images = rows // 16
    return pl.pallas_call(
        pool_kernel,
        grid=(micros, OUT // n),
        out_shape=jax.ShapeDtypeStruct((micros, images, OUT), F32),
        in_specs=[
            pl.BlockSpec((1, rows, n), lambda m, k: (m, 0, k)),
            pl.BlockSpec((1, rows, n), lambda m, k: (m, 0, k)),
            pl.BlockSpec((1, 8, n), lambda m, k: (m, 0, k)),
            pl.BlockSpec((1, 1, rows, 1), lambda m, k: (m, 0, 0, 0)),
        ],
        out_specs=pl.BlockSpec((1, images, n), lambda m, k: (m, 0, k)),
        compiler_params=params_of(56, 2),
        cost_estimate=cost(20 * micros * rows * OUT, 18 << 20),
    )(ho, hs, coef, wph)


def slope_kernel(ho_ref, hs_ref, cf_ref, w_ref, out_ref):
    images = out_ref.shape[2]
    so, ss, shift = cf_ref[0, 0:1, :], cf_ref[0, 1:2, :], cf_ref[0, 2:3, :]

    def body(i, carry):
        plain, out, side = [], [], []
        for k in range(8):
            at = pl.ds(pl.multiple_of(i * 128 + k * 16, 16), 16)
            ho, hs = ho_ref[0, at, :], hs_ref[0, at, :]
            j = ho * so + hs * ss + shift
            s = sigmoid(j)
            d = s * (1.0 + j * (1.0 - s)) * w_ref[0, 0, at, :]
            plain.append(jnp.sum(d, axis=0, keepdims=True))
            out.append(jnp.sum(d * ho, axis=0, keepdims=True))
            side.append(jnp.sum(d * hs, axis=0, keepdims=True))
        at = pl.ds(pl.multiple_of(i * 8, 8), 8)
        for k, value in enumerate((plain, out, side)):
            out_ref[0, k, at, :] = jnp.concatenate(value, axis=0)
        return carry

    lax.fori_loop(0, images // 8, body, 0)


def slopes(ho, hs, coef, wph):
    micros, rows, _ = ho.shape
    n = 512
    images = rows // 16
    return pl.pallas_call(
        slope_kernel,
        grid=(micros, OUT // n),
        out_shape=jax.ShapeDtypeStruct((micros, 3, images, OUT), F32),
        in_specs=[
            pl.BlockSpec((1, rows, n), lambda m, k: (m, 0, k)),
            pl.BlockSpec((1, rows, n), lambda m, k: (m, 0, k)),
            pl.BlockSpec((1, 8, n), lambda m, k: (m, 0, k)),
            pl.BlockSpec((1, 1, rows, 1), lambda m, k: (m, 0, 0, 0)),
        ],
        out_specs=pl.BlockSpec((1, 3, images, n), lambda m, k: (m, 0, 0, k)),
        compiler_params=params_of(56, 2),
        cost_estimate=cost(30 * micros * rows * OUT, 20 << 20),
    )(ho, hs, coef, wph)


def back_out_kernel(
    ho_ref, hs_ref, gs_ref, cf_ref, w_ref, am_ref, xe_ref, wo_ref, hm_ref, cm_ref,
    d_ref, st_ref, gw_ref, amt, xet, da, dho, dhs, acc_out, acc_side,
):
    micro, part = pl.program_id(0), pl.program_id(1)
    parts = pl.num_programs(1)
    images = gs_ref.shape[1]

    @pl.when(part == 0)
    def _():
        amt[...] = am_ref[0].T
        xet[...] = xe_ref[0].T

    cf = [cf_ref[0, k : k + 1, :] for k in range(7)]

    def body(i, carry):
        gs = gs_ref[0, pl.ds(pl.multiple_of(i * 8, 8), 8), :]
        for k in range(8):
            at = pl.ds(pl.multiple_of(i * 128 + k * 16, 16), 16)
            ho, hs = ho_ref[0, at, :], hs_ref[0, at, :]
            w = w_ref[0, 0, at, :]
            j = ho * cf[0] + hs * cf[1] + cf[2]
            s = sigmoid(j)
            g = s * (1.0 + j * (1.0 - s)) * gs[k : k + 1, :]
            dho[at, :] = ((g * cf[0] + cf[3] + ho * cf[4]) * w).astype(BF16)
            dhs[at, :] = ((g * cf[1] + cf[5] + hs * cf[6]) * w).astype(BF16)
        return carry

    lax.fori_loop(0, images // 8, body, 0)
    g_out = dot(amt[...], dho[...])
    g_side = dot(xet[...], dhs[...])
    back = dot_nt(dho[...], wo_ref[...])

    @pl.when(micro == 0)
    def _():
        acc_out[part] = g_out
        acc_side[part] = g_side

    @pl.when(micro > 0)
    def _():
        acc_out[part] += g_out
        acc_side[part] += g_side

    @pl.when(part == 0)
    def _():
        da[...] = back

    @pl.when(part > 0)
    def _():
        da[...] += back

    @pl.when(part == parts - 1)
    def _():
        hm = hm_ref[0]
        v = hm * cm_ref[0, 0:1, :] + cm_ref[0, 1:2, :]
        s = sigmoid(v)
        d = s * (1.0 + v * (1.0 - s)) * da[...] * w_ref[0, 0]
        d_ref[0] = d
        st_ref[...] = jnp.zeros_like(st_ref)
        st_ref[0, 0:1, :] = jnp.sum(d, axis=0, keepdims=True)
        st_ref[0, 1:2, :] = jnp.sum(d * hm, axis=0, keepdims=True)

    @pl.when((micro == pl.num_programs(0) - 1) & (part == parts - 1))
    def _():
        for k in range(4):
            for half in range(2):
                lanes = slice(half * 256, half * 256 + 256)
                gw_ref[2 * k + half, 0:MID, :] = acc_out[k, :, lanes].astype(BF16)
                gw_ref[2 * k + half, MID:, :] = acc_side[k, :, lanes].astype(BF16)


def back_out(ho, hs, gs, coef, wph, am, xe, weight, hm, coef_mid):
    micros, rows, _ = ho.shape
    n = 512
    images = rows // 16
    return pl.pallas_call(
        back_out_kernel,
        grid=(micros, OUT // n),
        out_shape=[
            jax.ShapeDtypeStruct((micros, rows, MID), F32),
            jax.ShapeDtypeStruct((micros, 8, MID), F32),
            jax.ShapeDtypeStruct((LANES, GRAD_OUT, 256), BF16),
        ],
        in_specs=[
            pl.BlockSpec((1, rows, n), lambda m, k: (m, 0, k)),
            pl.BlockSpec((1, rows, n), lambda m, k: (m, 0, k)),
            pl.BlockSpec((1, images, n), lambda m, k: (m, 0, k)),
            pl.BlockSpec((1, 8, n), lambda m, k: (m, 0, k)),
            pl.BlockSpec((1, 1, rows, 1), lambda m, k: (m, 0, 0, 0)),
            pl.BlockSpec((1, rows, MID), lambda m, k: (m, 0, 0)),
            pl.BlockSpec((1, rows, D_IN), lambda m, k: (m, 0, 0)),
            pl.BlockSpec((MID, n), lambda m, k: (0, k)),
            pl.BlockSpec((1, rows, MID), lambda m, k: (m, 0, 0)),
            pl.BlockSpec((1, 8, MID), lambda m, k: (m, 0, 0)),
        ],
        out_specs=[
            pl.BlockSpec((1, rows, MID), lambda m, k: (m, 0, 0)),
            pl.BlockSpec((1, 8, MID), lambda m, k: (m, 0, 0)),
            whole_block((LANES, GRAD_OUT, 256)),
        ],
        scratch_shapes=[
            pltpu.VMEM((MID, rows), BF16),
            pltpu.VMEM((D_IN, rows), BF16),
            pltpu.VMEM((rows, MID), F32),
            pltpu.VMEM((rows, n), BF16),
            pltpu.VMEM((rows, n), BF16),
            pltpu.VMEM((OUT // n, MID, n), F32),
            pltpu.VMEM((OUT // n, D_IN, n), F32),
        ],
        compiler_params=params_of(60, 2),
        cost_estimate=cost(2 * micros * rows * OUT * (2 * MID + D_IN), 40 << 20),
    )(ho, hs, gs, coef, wph, am, xe, weight, hm, coef_mid)


def back_mid_kernel(
    hm_ref, d_ref, cm_ref, cols_ref, wb, h_ref, hh_ref, cf_ref, w_ref, wh_ref,
    din_ref, dh_ref, st_ref, gw_ref, dt, acc,
):
    micro = pl.program_id(0)
    images = h_ref.shape[2] // 16

    low = ((d_ref[0] * cm_ref[0, 0:1, :] + cm_ref[0, 1:2, :] + hm_ref[0] * cm_ref[0, 2:3, :]) * w_ref[0, 0]).astype(BF16)
    for tap in range(9):
        lanes = slice(tap * MID, (tap + 1) * MID)
        g = dot_tn(cols_ref[0, :, lanes], low)

        @pl.when(micro == 0)
        def _():
            for col in range(4):
                acc[col, lanes, :] = g[:, col * 128 : (col + 1) * 128]

        @pl.when(micro > 0)
        def _():
            for col in range(4):
                acc[col, lanes, :] += g[:, col * 128 : (col + 1) * 128]

    scale, shift = cf_ref[0, 0:1, :], cf_ref[0, 1:2, :]
    zero = jnp.zeros((8, MID), F32)

    def back(h, grad, w):
        v = h * scale + shift
        s = sigmoid(v)
        return s * (1.0 + v * (1.0 - s)) * grad * w

    def body(i, carry):
        total, product = carry
        at = pl.ds(pl.multiple_of(i * 16, 16), 16)
        half = pl.ds(pl.multiple_of(i * 8, 8), 8)
        near = pl.ds(pl.multiple_of((i % (images // 2)) * 16, 16), 16)
        t = [dt[k, near, :].reshape(2, 8, MID) for k in range(9)]
        below1 = t[1]
        below3 = t[2] + shift_left(t[0])
        last = jnp.zeros((1, 8, MID), F32)
        grads = [
            t[4],
            t[5] + shift_left(t[3]),
            t[7] + jnp.concatenate([below1[1:], last], axis=0),
            t[8] + shift_left(t[6]) + jnp.concatenate([below3[1:], last], axis=0),
        ]
        for k in range(4):
            h = h_ref[0, k, at, :]
            d = back(h, grads[k].reshape(16, MID), w_ref[0, k, at, :])
            din_ref[0, k, at, :] = d.astype(BF16)
            total = total + fold(d)
            product = product + fold(d * h)
        for k, grad in enumerate((below1, below3)):
            h = hh_ref[0, k, half, :]
            d = back(h, grad[0], wh_ref[0, k, half, :])
            dh_ref[0, k, half, :] = d
            total = total + d
            product = product + d * h
        return total, product

    found = (zero, zero)
    for part in range(2):
        start, stop = part * images // 2, (part + 1) * images // 2
        for tap in range(9):
            dt[tap] = dot_nt(low[start * 16 : stop * 16], wb[tap * MID : (tap + 1) * MID, :])
        found = lax.fori_loop(start, stop, body, found)
    total, product = found
    st_ref[...] = jnp.zeros_like(st_ref)
    st_ref[0, 0:1, :] = jnp.sum(total, axis=0, keepdims=True)
    st_ref[0, 1:2, :] = jnp.sum(product, axis=0, keepdims=True)

    @pl.when(micro == pl.num_programs(0) - 1)
    def _():
        for k in range(LANES):
            for half in range(2):
                found = acc[(k % 2) * 2 + half, pl.ds(k // 2, GRAD_MID, stride=4), :]
                gw_ref[k, :, half * 128 : half * 128 + 128] = found.astype(BF16)


def back_mid(hm, d, coef_mid, cols, weight, h, hh, coef, wph, whalo):
    micros, _, rows, _ = h.shape
    return pl.pallas_call(
        back_mid_kernel,
        grid=(micros,),
        out_shape=[
            jax.ShapeDtypeStruct((micros, 4, rows, MID), BF16),
            jax.ShapeDtypeStruct((micros, 2, rows // 2, MID), F32),
            jax.ShapeDtypeStruct((micros, 8, MID), F32),
            jax.ShapeDtypeStruct((LANES, GRAD_MID, 256), BF16),
        ],
        in_specs=[
            pl.BlockSpec((1, rows, MID), lambda m: (m, 0, 0)),
            pl.BlockSpec((1, rows, MID), lambda m: (m, 0, 0)),
            pl.BlockSpec((1, 8, MID), lambda m: (m, 0, 0)),
            pl.BlockSpec((1, rows, 9 * MID), lambda m: (m, 0, 0)),
            pl.BlockSpec((9 * MID, MID), lambda m: (0, 0), pipeline_mode=pl.Buffered(1)),
            pl.BlockSpec((1, 4, rows, MID), lambda m: (m, 0, 0, 0)),
            pl.BlockSpec((1, 2, rows // 2, MID), lambda m: (m, 0, 0, 0)),
            pl.BlockSpec((1, 8, MID), lambda m: (m, 0, 0)),
            pl.BlockSpec((1, 4, rows, 1), lambda m: (m, 0, 0, 0)),
            pl.BlockSpec((1, 2, rows // 2, 1), lambda m: (m, 0, 0, 0)),
        ],
        out_specs=[
            pl.BlockSpec((1, 4, rows, MID), lambda m: (m, 0, 0, 0)),
            pl.BlockSpec((1, 2, rows // 2, MID), lambda m: (m, 0, 0, 0)),
            pl.BlockSpec((1, 8, MID), lambda m: (m, 0, 0)),
            pl.BlockSpec((LANES, GRAD_MID, 256), lambda m: (0, 0, 0), pipeline_mode=pl.Buffered(1)),
        ],
        scratch_shapes=[
            pltpu.VMEM((9, rows // 2, MID), F32),
            pltpu.VMEM((4, 9 * MID, 128), F32),
        ],
        compiler_params=params_of(62),
        cost_estimate=cost(4 * micros * rows * 9 * MID * MID, 60 << 20),
    )(hm, d, coef_mid, cols, weight, h, hh, coef, wph, whalo)


def back_in_kernel(h_ref, din_ref, dh_ref, cf_ref, w_ref, wh_ref, x_ref, xh_ref, gw_ref, ds, acc, turned):
    micro, part = pl.program_id(0), pl.program_id(1)
    images = h_ref.shape[2] // 16
    ca, cb, cc = cf_ref[0, 0:1, :], cf_ref[0, 1:2, :], cf_ref[0, 2:3, :]

    def body(i, carry):
        at = pl.ds(pl.multiple_of(i * 16, 16), 16)
        half = pl.ds(pl.multiple_of(i * 8, 8), 8)
        for k in range(4):
            h = h_ref[0, k, at, :]
            d = (din_ref[0, k, at, :].astype(F32) * ca + cb + h * cc) * w_ref[0, k, at, :]
            row, side = k // 2, k % 2
            for o in range(2):
                for col in range(4):
                    to = pl.ds(i * 64 + (2 * o + row) * 16 + side, 8, stride=2)
                    ds[col, to, :] = d[o * 8 : o * 8 + 8, col * 128 : (col + 1) * 128]
        for side in range(2):
            d = dh_ref[0, side, half, :] * ca
            for col in range(4):
                ds[col, pl.ds(images * 64 + i * 16 + side, 8, stride=2), :] = d[:, col * 128 : (col + 1) * 128]
        return carry

    lax.fori_loop(0, images, body, 0)
    low = jnp.concatenate([ds[col].astype(BF16) for col in range(4)], axis=1)
    g = dot_tn(low[: images * 64], x_ref[0]) + dot_tn(low[images * 64 :], xh_ref[0])

    @pl.when((micro == 0) & (part == 0))
    def _():
        acc[...] = g

    @pl.when((micro > 0) | (part > 0))
    def _():
        acc[...] += g

    @pl.when((micro == pl.num_programs(0) - 1) & (part == pl.num_programs(1) - 1))
    def _():
        for col in range(4):
            turned[col] = acc[col * 128 : (col + 1) * 128, :].T
        for k in range(LANES):
            for half in range(2):
                found = turned[(k % 2) * 2 + half, pl.ds(k // 2, D_IN // 4, stride=4), :]
                gw_ref[k, :, half * 128 : half * 128 + 128] = found.astype(BF16)


def back_in(h, din, dhalo, coef, wph, whalo, x, xh):
    micros, _, rows, _ = h.shape
    parts = 2
    r = rows // parts
    return pl.pallas_call(
        back_in_kernel,
        grid=(micros, parts),
        out_shape=jax.ShapeDtypeStruct((LANES, 256, 256), BF16),
        in_specs=[
            pl.BlockSpec((1, 4, r, MID), lambda m, k: (m, 0, k, 0)),
            pl.BlockSpec((1, 4, r, MID), lambda m, k: (m, 0, k, 0)),
            pl.BlockSpec((1, 2, r // 2, MID), lambda m, k: (m, 0, k, 0)),
            pl.BlockSpec((1, 8, MID), lambda m, k: (m, 0, 0)),
            pl.BlockSpec((1, 4, r, 1), lambda m, k: (m, 0, k, 0)),
            pl.BlockSpec((1, 2, r // 2, 1), lambda m, k: (m, 0, k, 0)),
            pl.BlockSpec((1, r * 4, D_IN), lambda m, k: (m, k, 0)),
            pl.BlockSpec((1, r, D_IN), lambda m, k: (m, k, 0)),
        ],
        out_specs=whole_block((LANES, 256, 256)),
        scratch_shapes=[
            pltpu.VMEM((4, r * 5, 128), F32),
            pltpu.VMEM((MID, D_IN), F32),
            pltpu.VMEM((4, D_IN, 128), F32),
        ],
        compiler_params=params_of(60, 2),
        cost_estimate=cost(2 * micros * rows * 5 * D_IN * MID, 50 << 20),
    )(h, din, dhalo, coef, wph, whalo, x, xh)


def swap(value, axis, bit):
    size = lax.axis_size(axis)
    return lax.ppermute(value, axis, [(i, i ^ bit) for i in range(size)])


def bits_of(axis):
    size, bit, found = lax.axis_size(axis), 1, []
    while bit < size:
        found.append(bit)
        bit *= 2
    return found


def add_all(value, axes=("c", "x", "p", "g")):
    for axis in axes:
        for bit in bits_of(axis):
            value = value + swap(value, axis, bit)
    return value


def exchange_planes(value):
    planes = lax.axis_size("g")
    here = lax.axis_index("g")
    own = lax.dynamic_index_in_dim(value, here, 0, keepdims=True)
    result = lax.dynamic_update_slice_in_dim(jnp.zeros_like(value), own, here, 0)
    for step in range(1, planes):
        block = lax.dynamic_index_in_dim(value, (here + step) % planes, 0, keepdims=True)
        got = lax.ppermute(block, "g", [(i, (i + step) % planes) for i in range(planes)])
        result = lax.dynamic_update_slice_in_dim(result, got, (here + planes - step) % planes, 0)
    return result


def gather_axis(value, axis):
    value = value[None]
    for bit in bits_of(axis):
        other = swap(value, axis, bit)
        mine = (lax.axis_index(axis) // bit) % 2
        value = jnp.where(mine == 0, jnp.concatenate([value, other]), jnp.concatenate([other, value]))
    return value


def to_heads(value):
    routed = exchange_planes(value)
    for axis in ("p", "x", "c"):
        routed = gather_axis(routed, axis)
    order = (3, 2, 1, 0, 4) + tuple(range(5, routed.ndim))
    routed = jnp.transpose(routed, order)
    return routed.reshape((-1,) + value.shape[2:])


def halve(value, axis, dim):
    own = lax.axis_index(axis)
    keep = lax.dynamic_index_in_dim(value, own, dim, keepdims=False)
    send = lax.dynamic_index_in_dim(value, 1 - own, dim, keepdims=False)
    return keep + swap(send, axis, 1)


def plane_reduce(value):
    half = value.shape[1] // 2
    value = halve(value.reshape((2, 2, 2) + value.shape[1:]), "c", 2)
    a = halve(halve(value[:, :, :half], "x", 1), "p", 0)
    b = halve(halve(value[:, :, half:], "p", 0), "x", 0)
    return jnp.concatenate([a, b], axis=0)


def to_plane(value, first, steps=(1, 2)):
    for step in steps:
        pairs = [(i ^ step, i) for i in range(GROUPS) if step == 1 and i % 2 == first or i == first]
        value = value + lax.ppermute(value, "g", pairs)
    return value


def spread_trunk(block, plane, plane_rows):
    planes = lax.axis_size("g")
    result = None
    for target in range(planes):
        parts = []
        for source in range(planes):
            low = max(target * GROUP, source * plane_rows)
            high = min((target + 1) * GROUP, (source + 1) * plane_rows)
            if low < high:
                piece = block[low - source * plane_rows : high - source * plane_rows]
                parts.append(piece if source == target else lax.ppermute(piece, "g", [(source, target)]))
        whole = parts[0] if len(parts) == 1 else jnp.concatenate(parts, axis=0)
        result = whole if result is None else jnp.where(plane == target, whole, result)
    return result


def first_rows_everywhere(block, plane, plane_rows):
    last = lax.axis_size("g") - 1
    at = ROW_VEC - last * plane_rows
    send = jnp.concatenate([block[:ROW_CMID], block[at : at + 16]], axis=0)
    first, vec = send[:ROW_CMID], send[ROW_CMID:]
    for target in range(1, last + 1):
        pairs = [(0, target), (last, last - target)]
        got = lax.ppermute(send, "g", pairs)
        first = jnp.where(plane == target, got[:ROW_CMID], first)
        vec = jnp.where(plane == last - target, got[ROW_CMID:], vec)
    rows = jnp.concatenate([first, vec], axis=0)
    for axis in PLANE:
        rows = gather_axis(rows, axis)
    rows = jnp.transpose(rows, (3, 2, 1, 0, 4)).reshape(-1, 2048)
    return rows[:ROW_CMID], rows[ROW_CMID:]


def norm_ranges():
    widths = [MID, MID, OUT, OUT, OUT, OUT, OUT, PRED]
    return [(sum(widths[:layer]), widths[layer]) for layer in range(8)]


def silu_back(value, grad):
    gate = jax.nn.sigmoid(value)
    return grad * gate * (1.0 + value * (1.0 - gate))


def head_norm(hidden, gamma, beta):
    count = hidden.shape[0]
    average = jnp.sum(hidden, axis=0) / count
    variance = jnp.sum(hidden * hidden, axis=0) / count - average * average
    scale = lax.rsqrt(variance + EPS_NORM)
    normed = (hidden - average) * scale
    return gamma * normed + beta, (normed, scale), average, variance


def head_norm_back(grad, kept, gamma):
    normed, scale = kept
    count = grad.shape[0]
    beta_sum = jnp.sum(grad, axis=0)
    gamma_sum = jnp.sum(grad * normed, axis=0)
    back = gamma * scale * (grad - beta_sum / count - normed * gamma_sum / count)
    return back, gamma_sum, beta_sum


def heads(pooled_low, wall, gammas, betas, bias, partner, live):
    project = [wall[ROW_PROJ + 2048 * k : ROW_PROJ + 2048 * (k + 1)] for k in range(3)]
    predict_in = wall[ROW_PIN:ROW_POUT].reshape(OUT, PRED)
    predict_out = wall[ROW_POUT:ROW_VEC]
    means, variances, kept_all, normed_all, lows = [], [], [], [], []
    low = pooled_low
    for k in range(3):
        normed, kept, mean, variance = head_norm(dot(low, project[k]), gammas[4 + k], betas[4 + k])
        means.append(mean)
        variances.append(variance)
        kept_all.append(kept)
        normed_all.append(normed)
        lows.append(low)
        low = (jax.nn.silu(normed) if k < 2 else normed).astype(BF16)
    latent, latent_low = normed, low
    normed_q, kept_q, mean, variance = head_norm(dot(latent_low, predict_in), gammas[7], betas[7])
    means.append(mean)
    variances.append(variance)
    act = jax.nn.silu(normed_q).astype(BF16)
    predicted = dot(act, predict_out) + bias
    choose = (partner[:, None] == jnp.arange(latent.shape[0])[None, :]).astype(F32)
    target = jnp.dot(choose, latent, precision=lax.Precision.HIGHEST)
    inner = jnp.sum(predicted * target, axis=-1)
    inv_pred = lax.rsqrt(jnp.sum(predicted * predicted, axis=-1) + COS_EPS)
    inv_goal = lax.rsqrt(jnp.sum(target * target, axis=-1) + COS_EPS)
    flags = live.astype(F32)
    loss_sum = -jnp.sum(flags * inner * inv_pred * inv_goal)
    live_count = jnp.sum(flags)
    grad_cos = -flags / live_count
    grad_pred = grad_cos[:, None] * (
        target * (inv_pred * inv_goal)[:, None] - (inner * inv_pred**3 * inv_goal)[:, None] * predicted
    )
    grad_bias = jnp.sum(grad_pred, axis=0)
    low_p = grad_pred.astype(BF16)
    grad_act = dot_nt(low_p, predict_out)
    grad_q, gamma_q, beta_q = head_norm_back(silu_back(normed_q, grad_act), kept_q, gammas[7])
    low_q = grad_q.astype(BF16)
    grad_act = dot_nt(low_q, predict_in)
    low_f, gamma_sums, beta_sums = [None] * 3, [None] * 3, [None] * 3
    for k in (2, 1, 0):
        grad_normed = grad_act if k == 2 else silu_back(normed_all[k], grad_act)
        grad_hidden, gamma_sums[k], beta_sums[k] = head_norm_back(grad_normed, kept_all[k], gammas[4 + k])
        low_f[k] = grad_hidden.astype(BF16)
        grad_act = dot_nt(low_f[k], project[k])
    block = (lax.axis_index("p") % 2) * 4 + lax.axis_index("x") * 2 + lax.axis_index("c")

    def columns(v, start):
        return lax.dynamic_slice_in_dim(v, start, 256, 1)

    rows = [dot_tn(lows[k], columns(low_f[k], block * 256)).astype(BF16) for k in range(3)]
    g_in = dot_tn(latent_low, columns(low_q, (block % 2) * 256)).astype(BF16)
    rows.append(lax.dynamic_index_in_dim(g_in.reshape(PRED, 4, 256), block // 2, 1, keepdims=False))
    rows.append(dot_tn(act, columns(low_p, block * 256)).astype(BF16))
    vector = (gamma_sums + [gamma_q], beta_sums + [beta_q], grad_bias)
    return grad_act, jnp.concatenate(rows, axis=0), vector, block, loss_sum, live_count, means, variances


def place(values, size):
    flat, at = jnp.zeros((size,), F32), 0
    for value in values:
        flat = flat + jnp.pad(value, (at, size - at - value.shape[0]))
        at += value.shape[0]
    return flat


def norm_coefs(sums, total, gamma, beta):
    mean = sums[:, 0] / total[:, None]
    variance = sums[:, 1] / total[:, None] - mean * mean
    scale = lax.rsqrt(variance + EPS_NORM)
    a = gamma * scale
    return mean, variance, scale, a, beta - a * mean


def pack(rows):
    rows = list(rows) + [jnp.zeros_like(rows[0])] * (8 - len(rows))
    return jnp.stack(rows, axis=1)


def back_coefs(grad_sum, product_sum, mean, scale, a, total):
    gamma_sum = scale * (product_sum - mean * grad_sum)
    c = -a * scale * gamma_sum / total[:, None]
    b = -a * grad_sum / total[:, None] - c * mean
    return b, c, gamma_sum


def on_device(inputs, masks, partner, live, params, first, second, running):
    count = lax.axis_size(ALL)
    index = lax.axis_index(ALL)
    plane = lax.axis_index("g")
    own = params.shape[0] // 128
    micros, images, rows, width, _ = inputs.shape
    out_rows, out_cols = rows // 2, width // 2
    window_rows = -(-own // 256) * 16
    shift = window_rows * 16 - own
    plane_rows = window_rows * LANES
    near = (
        shift * count <= own
        and lax.axis_size("g") == GROUPS
        and lax.axis_size(PLANE) == LANES
        and ROW_COUT < plane_rows < ROW_PROJ <= 2 * plane_rows
        and window_rows - tail_rows(shift, count) < ROW_CMID <= window_rows
        and ROW_VEC % window_rows + 16 <= window_rows
        and ROW_VEC >= (lax.axis_size("g") - 1) * plane_rows
    )

    x = inputs.reshape(micros, images * rows * width, D_IN)
    x_last, mask_last = inputs[:, :, -1], masks[:, :, -1]
    mask = masks.astype(F32)
    split = mask.reshape(micros, images, out_rows, 2, out_cols, 2)
    wph = jnp.transpose(split, (0, 3, 5, 1, 2, 4)).reshape(micros, 4, -1, 1)
    around = [(i, i + 1) for i in range(lax.axis_size(("x", "c")) - 1)]
    total_in = jnp.sum(mask, axis=(1, 2, 3))
    image_pixels = jnp.sum(split[:, :, :, 0, :, 0], axis=(2, 3))
    total_out = jnp.sum(image_pixels, axis=1)
    chosen = jnp.stack([partner.astype(F32), live.astype(F32)], axis=-1)
    if near:
        window = flat_to_window(params, window_rows, shift, index, count)
        column = lax.all_to_all(window, PLANE, 1, 0, tiled=True)
        trunk = spread_trunk(column, plane, plane_rows)
        trunk, column = lax.optimization_barrier((trunk, column))
        wide_in, vec = first_rows_everywhere(column, plane, plane_rows)
        x_last, wide_in = lax.optimization_barrier((x_last, wide_in))
        h, xe, st, w_first = conv_in(x, wph, wide_in)
        trunk = lax.all_gather(trunk, ALL, axis=0, tiled=False).reshape(GROUPS, LANES, GROUP, 256)
        st, image_pixels, chosen, mask_last = lax.optimization_barrier((st, image_pixels, chosen, mask_last))
    else:
        wall = lax.all_gather(params.astype(BF16), ALL, axis=0, tiled=True).reshape(-1, 2048)
        wide_in, vec = wall[:ROW_CMID], wall[ROW_VEC : ROW_VEC + 16]
        trunk = jnp.transpose(wall[:ROW_PROJ].reshape(GROUPS, GROUP, LANES, 256), (0, 2, 1, 3))
        h, xe, st, w_first = conv_in(x, wph, wide_in)

    x_halo = lax.ppermute(x_last, ("x", "c"), around).reshape(micros, images * width, D_IN)
    mask_halo = lax.ppermute(mask_last, ("x", "c"), around).astype(F32)
    image_pixels = add_all(image_pixels, ("c", "x"))
    chosen = to_heads(chosen)
    whalo = jnp.transpose(mask_halo.reshape(micros, images, out_cols, 2), (0, 3, 1, 2)).reshape(micros, 2, -1, 1)
    share_index = lax.axis_index(("x", "c"))

    pixels = jnp.broadcast_to(jnp.stack([total_in, total_out], axis=1)[..., None], (micros, 2, 128))
    sums = add_all(jnp.concatenate([st[:, :2], pixels], axis=2))
    total_in, total_out = sums[:, 0, MID], sums[:, 1, MID]
    sums = sums[..., :MID]
    hh = conv_in_halo(x_halo, w_first)
    if near:
        window, trunk, sums, hh, total_in, total_out, whalo, image_pixels, chosen = lax.optimization_barrier(
            (window, trunk, sums, hh, total_in, total_out, whalo, image_pixels, chosen)
        )
        wall = lax.all_gather(window, ALL, axis=0, tiled=True)

    vec = vec.astype(F32).reshape(-1)
    ranges = norm_ranges()
    gammas = [vec[start : start + n] for start, n in ranges]
    betas = [vec[NORM + start : NORM + start + n] for start, n in ranges]
    bias = vec[2 * NORM : 2 * NORM + OUT]

    mean_in, var_in, scale_in, a_in, b_in = norm_coefs(sums, total_in, gammas[0], betas[0])
    coef_in = pack([a_in, b_in])
    hs, st_side = conv_side(xe, trunk)
    cols, hm, st, w_mid = conv_mid(h, hh, coef_in, wph, whalo, trunk)
    sums = add_all(jnp.concatenate([st[:, :2], st_side[:, :2]], axis=2))
    mean_mid, var_mid, scale_mid, a_mid, b_mid = norm_coefs(sums[..., :MID], total_out, gammas[1], betas[1])
    mean_side, var_side, scale_side, a_side, b_side = norm_coefs(sums[..., MID:], total_out, gammas[3], betas[3])
    am, ho, st, w_out = conv_out(hm, pack([a_mid, b_mid]), wph, trunk)
    sums = add_all(st[:, :2])
    mean_out, var_out, scale_out, a_out, b_out = norm_coefs(sums, total_out, gammas[2], betas[2])
    coef_join = pack([a_out, a_side, b_out + b_side])
    pooled = pool(ho, hs, coef_join, wph)
    for axis in ("x", "c"):
        half = pooled.shape[1] // 2
        here = lax.axis_index(axis)
        keep = lax.dynamic_slice_in_dim(pooled, here * half, half, 1)
        send = lax.dynamic_slice_in_dim(pooled, (1 - here) * half, half, 1)
        pooled = keep + swap(send, axis, 1)
    share = pooled.shape[1]
    share_pixels = lax.dynamic_slice_in_dim(image_pixels, share_index * share, share, 1)
    pooled_low = to_heads((pooled / share_pixels[..., None]).astype(BF16))
    slope = slopes(ho, hs, coef_join, wph)
    pooled_low, slope = lax.optimization_barrier((pooled_low, slope))

    grad_pool, head_rows, head_vec, block, loss_sum, live_count, head_means, head_vars = heads(
        pooled_low, wall, gammas, betas, bias, chosen[:, 0].astype(jnp.int32), chosen[:, 1]
    )

    def vector_rows(gamma, beta, extra):
        return place(gamma + beta + [extra], 16 * 2048).astype(BF16).reshape(16, 2048)

    none_head = [jnp.zeros((n,), F32) for _, n in ranges[4:]]
    none_trunk = [jnp.zeros((n,), F32) for _, n in ranges[:4]]
    head_vector = vector_rows(none_trunk + head_vec[0], none_trunk + head_vec[1], head_vec[2])
    head_vector = lax.dynamic_slice_in_dim(head_vector, block * 256, 256, 1)

    head_stats = place(head_means + head_vars + [loss_sum[None], live_count[None]], 106 * 128).reshape(1, -1, 128)
    head_stats = exchange_planes(jnp.broadcast_to(head_stats, (micros,) + head_stats.shape[1:])).reshape(micros, -1)
    head_size = NORM - sum(n for _, n in ranges[:4])
    scalars = head_stats[:, 2 * head_size : 2 * head_size + 2]

    grad_pool = grad_pool.astype(BF16).reshape(lax.axis_size("g"), lax.axis_size("p"), images, OUT)
    grad_pool = lax.dynamic_index_in_dim(grad_pool, lax.axis_index("p"), 1, keepdims=False)
    gs = exchange_planes(grad_pool)
    if near:
        head_part = jnp.concatenate(
            [
                jnp.zeros((ROW_PROJ, 256), BF16),
                head_rows,
                head_vector,
                jnp.zeros((window_rows * count - ROW_VEC - 16, 256), BF16),
            ],
            axis=0,
        )
        head_part, gs, head_stats = lax.optimization_barrier((head_part, gs, head_stats))
        head_part = lax.psum_scatter(head_part, "g", scatter_dimension=0, tiled=True)
    gs = gs.astype(F32) / image_pixels[..., None]

    sums = add_all(jnp.sum(gs[:, None] * slope, axis=2))
    bo, co, gamma_out = back_coefs(sums[:, 0], sums[:, 1], mean_out, scale_out, a_out, total_out)
    bs, cs, gamma_side = back_coefs(sums[:, 0], sums[:, 2], mean_side, scale_side, a_side, total_out)
    beta_joined = sums[:, 0]
    coef_back = pack([a_out, a_side, b_out + b_side, bo, co, bs, cs])
    d_mid, st, g_out = back_out(
        ho, hs, gs, coef_back, wph, am, xe, w_out, hm, pack([a_mid, b_mid])
    )
    if near:
        head_part, g_out = lax.optimization_barrier((head_part, g_out))
        g_out = lax.psum_scatter(g_out, PLANE, scatter_dimension=0, tiled=False)
    sums = add_all(st[:, :2])
    bm, cm, gamma_mid = back_coefs(sums[:, 0], sums[:, 1], mean_mid, scale_mid, a_mid, total_out)
    beta_mid = sums[:, 0]
    d_in, d_halo, st, g_mid = back_mid(
        hm, d_mid, pack([a_mid, bm, cm]), cols, w_mid, h, hh, coef_in, wph, whalo
    )
    if near:
        g_mid, g_out = lax.optimization_barrier((g_mid, g_out))
        g_mid = lax.psum_scatter(g_mid, PLANE, scatter_dimension=0, tiled=False)
        out_first = to_plane(g_out[: plane_rows - ROW_COUT], 0, (1,))
        out_second = to_plane(g_out[plane_rows - ROW_COUT :], 1, (1,))
    sums = add_all(st[:, :2])
    bi, ci, gamma_in = back_coefs(sums[:, 0], sums[:, 1], mean_in, scale_in, a_in, total_in)
    beta_in = sums[:, 0]
    if near:
        bi, ci, out_first, out_second = lax.optimization_barrier((bi, ci, out_first, out_second))
        out_first, out_second = to_plane(out_first, 0, (2,)), to_plane(out_second, 1, (2,))
    g_in = back_in(h, d_in, d_halo, pack([a_in, bi, ci]), wph, whalo, x, x_halo)

    if near:
        g_in, g_mid, out_first, out_second = lax.optimization_barrier(
            (plane_reduce(g_in), g_mid, out_first, out_second)
        )
    trunk_gamma = [jnp.sum(v, axis=0) for v in (gamma_in, gamma_mid, gamma_out, gamma_side)]
    trunk_beta = [jnp.sum(v, axis=0) for v in (beta_in, beta_mid, beta_joined, beta_joined)]
    trunk_vector = vector_rows(trunk_gamma + none_head, trunk_beta + none_head, jnp.zeros((OUT,), F32))

    if near:
        def blank(n):
            return jnp.zeros((n, 256), BF16)

        first_rows = jnp.concatenate([blank(ROW_CMID), to_plane(g_mid, 0), out_first], axis=0)
        second_rows = jnp.concatenate([out_second, blank(plane_rows - out_second.shape[0])], axis=0)
        part = jnp.where(plane == 0, first_rows, jnp.where(plane == 1, head_part + second_rows, head_part))
        window = lax.all_to_all(part, PLANE, 0, 1, tiled=True)
        tail = tail_rows(shift, count)
        prev = lax.ppermute(window[window_rows - tail :], ALL, [(i, i + 1) for i in range(count - 1)])
        g_in = to_plane(g_in, 0)
        for axis in PLANE:
            g_in = gather_axis(g_in, axis)
        g_in = jnp.transpose(g_in, (3, 2, 1, 0, 4)).reshape(ROW_CMID, 2048)
        window = window.at[:ROW_CMID].add(jnp.where(index == 0, g_in, 0))
        prev = prev.at[: ROW_CMID - window_rows + tail].add(jnp.where(index == 1, g_in[window_rows - tail :], 0))
        at = ROW_VEC % window_rows
        window = window.at[at : at + 16].add(jnp.where(index == ROW_VEC // window_rows, trunk_vector, 0))
        new_params, new_first, new_second, new_copy = adam_from_window(
            window, prev, shift, index, params, first, second
        )
    else:
        alone = (lax.axis_index("p") < 2).astype(BF16)
        head_part = jnp.concatenate([head_rows, head_vector], axis=0) * alone
        head_part = lax.dynamic_update_slice(
            jnp.zeros((head_part.shape[0], 2048), BF16), head_part, (jnp.int32(0), (block * 256).astype(jnp.int32))
        )
        lone = (index == 0).astype(BF16)
        head_part = head_part.at[ROW_VEC - ROW_PROJ :].add(trunk_vector * lone)
        trunk = jnp.concatenate([g_in, g_mid, g_out], axis=1)
        trunk = jnp.transpose(trunk, (1, 0, 2)).reshape(-1, 2048)
        flat = jnp.concatenate([trunk, head_part], axis=0).reshape(-1)
        flat = flat[: params.shape[0] * count]
        grad = lax.psum_scatter(flat, ALL, scatter_dimension=0, tiled=True).astype(F32)
        new_params, new_first, new_second = adam(grad, params, first, second)
        new_copy = new_params.astype(BF16)

    averages = jnp.concatenate([mean_in, mean_mid, mean_out, mean_side, head_stats[:, :head_size]], axis=1)
    spreads = jnp.concatenate([var_in, var_mid, var_out, var_side, head_stats[:, head_size : 2 * head_size]], axis=1)
    stats = jnp.stack([averages, spreads], axis=1)
    new_running = running
    for micro in range(micros):
        new_running = (1.0 - MOMENTUM) * new_running + MOMENTUM * stats[micro]
    return (
        scalars[:, 0],
        scalars[:, 1].astype(jnp.int32),
        new_params,
        new_first,
        new_second,
        new_copy,
        new_running,
    )


def solution(mesh):
    img, rows = mesh.shape["img"], mesh.shape["rows"]
    fine = Mesh(mesh.devices.reshape(MB, img // MB, 2, rows // 2), ALL)
    split = P(ALL)
    placed = (
        P(None, ("g", "p"), ("x", "c"), None, None),
        P(None, ("g", "p"), ("x", "c"), None),
        P(None, ALL),
        P(None, ALL),
        split,
        split,
        split,
        P(),
    )
    return jax.shard_map(
        on_device,
        mesh=fine,
        in_specs=placed,
        out_specs=(P(), P(), split, split, split, split, P()),
        check_vma=False,
    )
```
